32 devices in a mesh: dp: 8 (over z, x), tensor: 4 (over y, core).
Axes of the slice: x: 2, y: 2, z: 4, core: 2. Of those that a mesh axis runs over, the one named last changes fastest.
Arguments:
- inputs: bfloat16 [16, 1024, 1024], P('dp', 'tensor'), may hold values from -6 to 6
- lengths: int32 [16], P('dp'), may hold values from 1 to 1024, as said below
- w_query: bfloat16 [1024, 1024], P('dp', 'tensor'), may hold values from -0.1875 to 0.1875
- w_key: bfloat16 [1024, 1024], P('dp', 'tensor'), may hold values from -0.1875 to 0.1875
- w_value: bfloat16 [1024, 1024], P('dp', 'tensor'), may hold values from -0.1875 to 0.1875
- w_out: bfloat16 [1024, 1024], P('tensor', 'dp'), may hold values from -4 to 4
- w_up: bfloat16 [1024, 4096], P('dp', 'tensor'), may hold values from -0.1875 to 0.1875
- w_down: bfloat16 [4096, 1024], P('tensor', 'dp'), may hold values from -0.09375 to 0.09375
- b_query: float32 [1024], P('tensor'), may hold values from -3 to 3
- b_value: float32 [1024], P('tensor'), may hold values from -3 to 3
- b_out: float32 [1024], replicated, may hold values from -3 to 3
- b_up: float32 [4096], P('tensor'), may hold values from -3 to 3
- b_down: float32 [1024], replicated, may hold values from -3 to 3
- first_gain: float32 [1024], replicated, may hold values from 0.5 to 1.5
- first_shift: float32 [1024], replicated, may hold values from -3 to 3
- second_gain: float32 [1024], replicated, may hold values from 0.5 to 1.5
- second_shift: float32 [1024], replicated, may hold values from -3 to 3
- cotangent: bfloat16 [16, 1024, 1024], P('dp', 'tensor'), may hold values from -6 to 6
Outputs:
- output: bfloat16 [16, 1024, 1024], P('dp', 'tensor')
- input_grad: bfloat16 [16, 1024, 1024], P('dp', 'tensor')
- w_query_grad: float32 [1024, 1024], P('dp', 'tensor')
- w_key_grad: float32 [1024, 1024], P('dp', 'tensor')
- w_value_grad: float32 [1024, 1024], P('dp', 'tensor')
- w_out_grad: float32 [1024, 1024], P('tensor', 'dp')
- w_up_grad: float32 [1024, 4096], P('dp', 'tensor')
- w_down_grad: float32 [4096, 1024], P('tensor', 'dp')
- b_query_grad: float32 [1024], replicated
- b_value_grad: float32 [1024], replicated
- b_out_grad: float32 [1024], replicated
- b_up_grad: float32 [4096], replicated
- b_down_grad: float32 [1024], replicated
- first_gain_grad: float32 [1024], replicated
- first_shift_grad: float32 [1024], replicated
- second_gain_grad: float32 [1024], replicated
- second_shift_grad: float32 [1024], replicated
The draws below stay inside these ranges and needn't reach their ends.
Inputs may be any that keep to these rules, and one draw needn't show every extreme that they name: `lengths`: in each aligned block of 2 sequences (those of one index of dp) one sequence, drawn from the seed, has the full length 1024; positions at or past a sequence's length are padding.
All inputs are finite; a program needn't handle non-finite values.
Results may differ from the reference program's by a relative error of at most 0.02.
Values may be sent and summed in bfloat16 or wider, within the bound.
No kernel may reach another device: no remote copies, remote signals or barrier semaphores. Data moves between devices by JAX's collectives and lax.ppermute only.
A program may use at most 128 MiB of HBM per device.

```python
import math
import jax
import jax.numpy as jnp
from jax import lax

D = 1024
HEADS = 16
HEAD = 64
FF = 4096
SEQ = 1024
SEQS = 2
ROWS_BLOCK = 512
SEQUENCES = 16


def draw_lengths(key, part):
    key = jax.random.fold_in(key, 11)
    groups = SEQUENCES // SEQS
    chosen = jax.random.randint(jax.random.fold_in(key, 1), (groups, 1), 0, SEQS)
    others = jax.random.randint(jax.random.fold_in(key, 2), (groups, SEQS), 1, SEQ + 1)
    slots = jnp.arange(SEQS, dtype=jnp.int32)[None, :]
    filled = jnp.where(slots == chosen, SEQ, others)
    return filled.reshape(SEQUENCES).astype(jnp.int32)


def spiked(values, key, source, target, blocks, factor):
    def block_of(position):
        return (jnp.arange(values.shape[position]) // (values.shape[position] // blocks)).reshape((-1,) + (1,) * (values.ndim - 1 - position))

    first = jax.random.permutation(key, blocks)[block_of(target)]
    far = (block_of(target) + blocks // 2) % blocks
    return jnp.where((block_of(source) == first) | (block_of(source) == far), factor * values, values)


def block_scale(key, dims, pieces, smallest, high):
    def one(dim, shards_of):
        draws = jax.random.uniform(jax.random.fold_in(jax.random.fold_in(key, 6), dim), (shards_of,), jnp.float32, smallest / len(pieces), high / len(pieces))
        return jnp.repeat(jnp.exp(draws), dims[dim] // shards_of).reshape((-1,) + (1,) * (len(dims) - dim - 1))

    level = one(*pieces[0])
    for cut in pieces[1:]:
        level = level * one(*cut)
    return level


def normal_values(own_key, dims, scale, reach, pieces=(), held_as=jnp.bfloat16):
    level = block_scale(own_key, dims, pieces, -0.22, 0.18) if pieces else 1.0
    values = jax.random.normal(own_key, dims, jnp.float32) * scale * level
    return jnp.minimum(jnp.maximum(values, -reach), reach).astype(held_as)


def noise_with(stream_key, dims, deviation, reach, split, heavy, kind=jnp.bfloat16):
    result = deviation * jax.random.normal(stream_key, dims, jnp.float32)
    if split:
        result = result * block_scale(stream_key, dims, split, -0.22, 0.18)
    return jnp.clip(spiked(result, jax.random.fold_in(stream_key, 3), *heavy), -reach, reach).astype(kind)


def setup_inputs(seed: int = 0) -> dict:
    splits = jax.random.split(jax.random.key(seed), 19)
    inputs = normal_values(splits[0], (SEQUENCES, SEQ, D), 1.0, 6.0, ((0, 8), (1, 4)))
    lengths = draw_lengths(jax.random.fold_in(splits[18], 71), 0)
    w_query = normal_values(splits[2], (D, D), D ** -0.5, 0.1875, ((0, 8), (1, 4)))
    w_key = normal_values(splits[3], (D, D), D ** -0.5, 0.1875, ((0, 8), (1, 4)))
    w_value = normal_values(splits[4], (D, D), D ** -0.5, 0.1875, ((0, 8), (1, 4)))
    w_out = normal_values(splits[5], (D, D), (max(1, 2 * D // SEQ)) ** -0.5, 4.0, ((0, 4), (1, 8)))
    w_up = normal_values(splits[6], (D, FF), D ** -0.5, 0.1875, ((0, 8), (1, 4)))
    w_down = normal_values(splits[7], (FF, D), FF ** -0.5, 0.09375, ((0, 4), (1, 8)))
    b_query = normal_values(splits[8], (D,), 0.5, 3.0, ((0, 4),), jnp.float32)
    b_value = normal_values(splits[9], (D,), 0.5, 3.0, ((0, 4),), jnp.float32)
    b_out = normal_values(splits[10], (D,), 0.5, 3.0, (), jnp.float32)
    b_up = normal_values(splits[11], (FF,), 0.5, 3.0, ((0, 4),), jnp.float32)
    b_down = normal_values(splits[12], (D,), 0.5, 3.0, (), jnp.float32)
    first_gain = jnp.clip(1.0 + 0.1 * jax.random.normal(splits[13], (D,), jnp.float32), 0.5, 1.5)
    first_shift = normal_values(splits[14], (D,), 0.5, 3.0, (), jnp.float32)
    second_gain = jnp.clip(1.0 + 0.1 * jax.random.normal(splits[15], (D,), jnp.float32), 0.5, 1.5)
    second_shift = normal_values(splits[16], (D,), 0.5, 3.0, (), jnp.float32)
    cotangent = noise_with(splits[17], (SEQUENCES, SEQ, D), 1.0, 6.0, ((0, 8), (1, 4)), (0, 2, 8, 2.0))
    return {"inputs": inputs, "lengths": lengths, "w_query": w_query, "w_key": w_key, "w_value": w_value, "w_out": w_out, "w_up": w_up, "w_down": w_down, "b_query": b_query, "b_value": b_value, "b_out": b_out, "b_up": b_up, "b_down": b_down, "first_gain": first_gain, "first_shift": first_shift, "second_gain": second_gain, "second_shift": second_shift, "cotangent": cotangent}


NORM_EPS = 1e-12
MASKED = -1000000000.0
HIGHEST = lax.Precision.HIGHEST

@jax.custom_vjp
def low(v):
    return lax.optimization_barrier(v.astype(jnp.bfloat16)).astype(jnp.float32)

@jax.custom_vjp
def low_back(v):
    return v

def low_keep(v):
    return (low(v), None)

def low_pass(kept, grad):
    return (grad,)

def back_keep(v):
    return (v, None)

def back_low(kept, grad):
    return (low(grad),)
low.defvjp(low_keep, low_pass)
low_back.defvjp(back_keep, back_low)

def product(factor_one, factor_two):
    return jnp.dot(factor_one, factor_two, precision=HIGHEST, preferred_element_type=jnp.float32)

def normalize(summed, norm_gain, norm_shift):
    centre = lax.optimization_barrier(jnp.mean(summed, axis=-1, keepdims=True))
    centred = summed - centre
    spread = lax.optimization_barrier(jnp.mean(centred * centred, axis=-1, keepdims=True))
    return centred * lax.rsqrt(spread + NORM_EPS) * norm_gain + norm_shift

def attend_rows(query_heads, key_heads, value_heads, visible):
    scaling = 1.0 / math.sqrt(HEAD)
    scores = jnp.einsum('hqe,hke->hqk', query_heads, key_heads, precision=HIGHEST) * scaling
    scores = jnp.where(visible[None, None, :], low_back(scores), MASKED)
    row_peak = lax.optimization_barrier(jnp.max(scores, axis=-1, keepdims=True))
    weights = jnp.exp(scores - row_peak)
    attention = weights / lax.optimization_barrier(jnp.sum(weights, axis=-1, keepdims=True))
    return jnp.einsum('hqk,hke->hqe', low(attention), value_heads, precision=HIGHEST)

def sequence_forward(params, tokens, length):
    w_query, w_key, w_value, w_out, w_up, w_down, b_query, b_value, b_out, b_up, b_down, first_gain, first_shift, second_gain, second_shift = params
    queries = low(low_back(product(tokens, w_query) + b_query))
    key_rows = low(low_back(product(tokens, w_key)))
    value_rows = low(low_back(product(tokens, w_value) + b_value))
    visible = jnp.arange(SEQ, dtype=jnp.int32) < length
    heads_q = queries.reshape(SEQ // ROWS_BLOCK, ROWS_BLOCK, HEADS, HEAD).transpose(0, 2, 1, 3)
    heads_k = key_rows.reshape(SEQ, HEADS, HEAD).transpose(1, 0, 2)
    heads_v = value_rows.reshape(SEQ, HEADS, HEAD).transpose(1, 0, 2)
    attend = jax.checkpoint(attend_rows)

    def one_block(query_block):
        return attend(query_block, heads_k, heads_v, visible)
    context = lax.map(one_block, heads_q)
    context = low(low_back(context.transpose(0, 2, 1, 3).reshape(SEQ, D)))
    attended = low_back(product(context, w_out))
    normed = normalize(tokens + attended + b_out, first_gain, first_shift)
    hidden = low_back(product(low(normed), w_up) + b_up)
    active = low(jax.nn.gelu(hidden, approximate=False))
    branch = low_back(product(active, w_down))
    return normalize(normed + branch + b_down, second_gain, second_shift)

def reference(inputs, lengths, w_query, w_key, w_value, w_out, w_up, w_down, b_query, b_value, b_out, b_up, b_down, first_gain, first_shift, second_gain, second_shift, cotangent):
    params = tuple((weight_in.astype(jnp.float32) for weight_in in (w_query, w_key, w_value, w_out, w_up, w_down, b_query, b_value, b_out, b_up, b_down, first_gain, first_shift, second_gain, second_shift)))
    checkpointed = jax.checkpoint(sequence_forward)

    def whole_forward(param_set, tokens_all):

        def one_sequence(paired):
            return checkpointed(param_set, paired[0], paired[1])
        return lax.map(one_sequence, (tokens_all, lengths))
    output, pullback = jax.vjp(whole_forward, params, inputs.astype(jnp.float32))
    param_grads, input_grad = pullback(cotangent.astype(jnp.float32))
    return (output.astype(jnp.bfloat16), input_grad.astype(jnp.bfloat16), param_grads[0], param_grads[1], param_grads[2], param_grads[3], param_grads[4], param_grads[5], param_grads[6], param_grads[7], param_grads[8], param_grads[9], param_grads[10], param_grads[11], param_grads[12], param_grads[13], param_grads[14])
```

```python
import math

import jax
import jax.numpy as jnp
from jax import lax
from jax.experimental import pallas as pl
from jax.experimental.pallas import tpu as pltpu
from jax.sharding import PartitionSpec as P

HEADS = 16
NORM_EPS = 1e-12
MASKED = -1000000000.0
MIB = 1024 * 1024
VMEM_LIMIT = 40 * MIB

F32 = jnp.float32
BF16 = jnp.bfloat16

CORE = 1
ACROSS = 2


def dot(one, two):
    return lax.dot_general(one, two, (((1,), (0,)), ((), ())), preferred_element_type=F32)


def dot_nt(one, two):
    return lax.dot_general(one, two, (((1,), (1,)), ((), ())), preferred_element_type=F32)


def dot_tn(one, two):
    return lax.dot_general(one, two, (((0,), (0,)), ((), ())), preferred_element_type=F32)


def shape(dims, kind):
    return jax.ShapeDtypeStruct(dims, kind)


def whole_call(kernel, outs, args, flops, name, scratch=()):
    moved = sum(math.prod(a.shape) * a.dtype.itemsize for a in (*args, *outs))
    return pl.pallas_call(
        kernel,
        out_shape=tuple(outs),
        in_specs=[pl.BlockSpec(memory_space=pltpu.VMEM)] * len(args),
        out_specs=tuple([pl.BlockSpec(memory_space=pltpu.VMEM)] * len(outs)),
        scratch_shapes=list(scratch),
        compiler_params=pltpu.CompilerParams(vmem_limit_bytes=VMEM_LIMIT),
        cost_estimate=pl.CostEstimate(flops=flops, bytes_accessed=moved, transcendentals=0),
        name=name,
    )(*args)


def swap_tensor(array, bit):
    size = lax.axis_size("tensor")
    return lax.ppermute(array, "tensor", [(i, i ^ bit) for i in range(size)])


def swap_dp(array, bit):
    size = lax.axis_size("dp")
    return lax.ppermute(array, "dp", [(i, i ^ bit) for i in range(size)])


def gather_dp(rows):
    size = lax.axis_size("dp")
    place = lax.axis_index("dp")
    step = size // 2
    level = 0
    block = rows.shape
    held = rows
    while step >= 1:
        other = swap_dp(held, step)
        low = (place & step) == 0
        held = jnp.where(
            low, jnp.stack([held, other], axis=level), jnp.stack([other, held], axis=level)
        )
        level += 1
        step //= 2
    return held.reshape((size * block[0],) + block[1:])


def scatter_dp(total):
    size = lax.axis_size("dp")
    place = lax.axis_index("dp")
    levels = size.bit_length() - 1
    rows = total.shape[0] // size
    held = total.reshape((2,) * levels + (rows,) + total.shape[1:])
    for level in range(levels):
        axis = levels - 1 - level
        bit = (place >> level) & 1
        mine = lax.dynamic_index_in_dim(held, bit, axis, keepdims=False)
        theirs = lax.dynamic_index_in_dim(held, 1 - bit, axis, keepdims=False)
        held = mine.astype(F32) + swap_dp(theirs.astype(BF16), 1 << level).astype(F32)
    return held


def sum_all(vector):
    step = 1
    while step < lax.axis_size("tensor"):
        vector = vector + swap_tensor(vector, step)
        step *= 2
    step = 1
    while step < lax.axis_size("dp"):
        vector = vector + swap_dp(vector, step)
        step *= 2
    return vector


def project_inputs(x_own, x_across, w_mine, w_other, b_mine, b_other):
    rows, width = x_own.shape
    third = w_mine.shape[1] // 3

    def kernel(x0, x1, wm, wo, bm, bo, mine_ref, other_ref, send_ref):
        tokens = jnp.concatenate([x0[...], x1[...]], axis=0)
        mine = (dot(tokens, wm[...]) + bm[...]).astype(BF16)
        other = (dot(tokens, wo[...]) + bo[...]).astype(BF16)
        mine_ref[...] = mine
        other_ref[...] = other
        send_ref[:, : 2 * third] = other[:, third:]
        send_ref[:, 2 * third :] = mine[:, third:]

    outs = [
        shape((2 * rows, 3 * third), BF16),
        shape((2 * rows, 3 * third), BF16),
        shape((2 * rows, 4 * third), BF16),
    ]
    flops = 2 * 2 * rows * width * 6 * third
    return whole_call(
        kernel, outs, [x_own, x_across, w_mine, w_other, b_mine, b_other], flops, "project_inputs"
    )


def attention_forward(mine, other, far, bias_row, wout_mine, wout_other, head_size):
    rows = mine.shape[0]
    third = mine.shape[1] // 3
    heads = third // head_size
    block = rows // 2
    width = wout_mine.shape[0]
    scaling = 1.0 / math.sqrt(head_size)

    def kernel(mine_ref, other_ref, far_ref, bias_ref, wm, wo, cm_ref, co_ref, own_ref, across_ref, acc):
        lane_head = lax.broadcasted_iota(jnp.int32, (1, third), 1) // head_size
        acc[...] = jnp.zeros_like(acc)
        bias = bias_ref[...]

        def one_head(head, carry):
            inside = lane_head == head
            for group, ref in enumerate((mine_ref, other_ref)):
                base = 2 * third * group
                keys = jnp.concatenate(
                    [ref[:, third : 2 * third], far_ref[:, base : base + third]], axis=0
                )
                vals = jnp.concatenate(
                    [ref[:, 2 * third :], far_ref[:, base + third : base + 2 * third]], axis=0
                )
                for part in range(2):
                    span = slice(part * block, (part + 1) * block)
                    query = jnp.where(inside, ref[span, :third] * scaling, 0.0).astype(BF16)
                    scores = dot_nt(query, keys) + bias
                    peak = jnp.max(scores, axis=-1, keepdims=True)
                    weights = jnp.exp(scores - peak)
                    total = jnp.sum(weights, axis=-1, keepdims=True)
                    found = dot(weights.astype(BF16), vals) * (1.0 / total)
                    acc[group, span, :] += jnp.where(inside, found, 0.0)
            return carry

        lax.fori_loop(0, heads, one_head, 0)
        ctx_mine = acc[0].astype(BF16)
        ctx_other = acc[1].astype(BF16)
        cm_ref[...] = ctx_mine
        co_ref[...] = ctx_other
        part_sum = dot_nt(ctx_mine, wm[...]) + dot_nt(ctx_other, wo[...])
        own_ref[...] = part_sum[:block]
        across_ref[...] = part_sum[block:].astype(BF16)

    outs = [
        shape((rows, third), BF16),
        shape((rows, third), BF16),
        shape((block, width), F32),
        shape((block, width), BF16),
    ]
    flops = 2 * 2 * 2 * rows * 2 * rows * third * heads * 2
    return whole_call(
        kernel,
        outs,
        [mine, other, far, bias_row, wout_mine, wout_other],
        flops,
        "attention_forward",
        [pltpu.VMEM((2, rows, third), F32)],
    )


def attention_backward(mine, other, far, bias_column, ga_own, ga_across, wout_mine, wout_other, head_size):
    rows = mine.shape[0]
    third = mine.shape[1] // 3
    heads = third // head_size
    block = rows // 2
    keys_count = 2 * rows
    scaling = 1.0 / math.sqrt(head_size)

    def kernel(
        mine_ref, other_ref, far_ref, bias_ref, g0, g1, wm, wo,
        dq_ref, keep_ref, send_ref, grad_ctx, keys_t, dq_t, dkv,
    ):
        lane_head = lax.broadcasted_iota(jnp.int32, (1, third), 1) // head_size
        grad_rows = jnp.concatenate([g0[...], g1[...]], axis=0)
        grad_ctx[0] = dot(grad_rows, wm[...]).astype(BF16)
        grad_ctx[1] = dot(grad_rows, wo[...]).astype(BF16)
        dkv[...] = jnp.zeros_like(dkv)
        for group, ref in enumerate((mine_ref, other_ref)):
            base = 2 * third * group
            keys_t[group, :, :rows] = ref[:, third : 2 * third].T
            keys_t[group, :, rows:] = far_ref[:, base : base + third].T
        bias = bias_ref[...]

        def one_head(head, carry):
            inside = lane_head == head
            start = pl.multiple_of(head * head_size, head_size)
            for group, ref in enumerate((mine_ref, other_ref)):
                base = 2 * third * group
                keys = jnp.concatenate(
                    [ref[:, third : 2 * third], far_ref[:, base : base + third]], axis=0
                )
                vals = jnp.concatenate(
                    [ref[:, 2 * third :], far_ref[:, base + third : base + 2 * third]], axis=0
                )
                head_keys_t = keys_t[group, pl.ds(start, head_size), :]
                for part in range(2):
                    span = slice(part * block, (part + 1) * block)
                    query = jnp.where(inside, ref[span, :third] * scaling, 0.0).astype(BF16)
                    grad = jnp.where(inside, grad_ctx[group, span, :], 0.0).astype(BF16)
                    scores = dot_nt(keys, query) + bias
                    peak = jnp.max(scores, axis=0, keepdims=True)
                    weights = jnp.exp(scores - peak)
                    total = jnp.sum(weights, axis=0, keepdims=True)
                    probs = weights * (1.0 / total)
                    grad_probs = dot_nt(vals, grad)
                    inner = jnp.sum(probs * grad_probs, axis=0, keepdims=True)
                    grad_scores = (probs * (grad_probs - inner)).astype(BF16)
                    dkv[group, 1] += dot(probs.astype(BF16), grad)
                    dkv[group, 0] += dot(grad_scores, query)
                    dq_t[group, pl.ds(start, head_size), span] = dot(head_keys_t, grad_scores)
            return carry

        lax.fori_loop(0, heads, one_head, 0)
        for group in range(2):
            dq_ref[:, group * third : (group + 1) * third] = (dq_t[group].T * scaling).astype(BF16)
            for kind in range(2):
                at = (2 * group + kind) * third
                keep_ref[:, at : at + third] = dkv[group, kind, :rows]
                away = (2 * (1 - group) + kind) * third
                send_ref[:, away : away + third] = dkv[group, kind, rows:].astype(BF16)

    outs = [
        shape((rows, 2 * third), BF16),
        shape((rows, 4 * third), F32),
        shape((rows, 4 * third), BF16),
    ]
    flops = 5 * 2 * 2 * rows * keys_count * third * heads
    return whole_call(
        kernel,
        outs,
        [mine, other, far, bias_column, ga_own, ga_across, wout_mine, wout_other],
        flops,
        "attention_backward",
        [
            pltpu.VMEM((2, rows, third), BF16),
            pltpu.VMEM((2, third, keys_count), BF16),
            pltpu.VMEM((2, third, rows), F32),
            pltpu.VMEM((2, 2, keys_count, third), F32),
        ],
    )


def project_back(dq, keep, got, w_mine, w_other):
    rows = dq.shape[0]
    third = dq.shape[1] // 2
    block = rows // 2
    width = w_mine.shape[0]

    def kernel(dq_ref, keep_ref, got_ref, wm, wo, gm_ref, go_ref, own_ref, across_ref, sums_ref):
        dkv = (keep_ref[...] + got_ref[...].astype(F32)).astype(BF16)
        grad_mine = jnp.concatenate([dq_ref[:, :third], dkv[:, : 2 * third]], axis=1)
        grad_other = jnp.concatenate([dq_ref[:, third:], dkv[:, 2 * third :]], axis=1)
        gm_ref[...] = grad_mine
        go_ref[...] = grad_other
        back = dot_nt(grad_mine, wm[...]) + dot_nt(grad_other, wo[...])
        own_ref[...] = back[:block]
        across_ref[...] = back[block:].astype(BF16)
        sums_ref[0:1, :] = jnp.sum(grad_mine.astype(F32), axis=0, keepdims=True)
        sums_ref[1:2, :] = jnp.sum(grad_other.astype(F32), axis=0, keepdims=True)

    outs = [
        shape((rows, 3 * third), BF16),
        shape((rows, 3 * third), BF16),
        shape((block, width), F32),
        shape((block, width), BF16),
        shape((2, 3 * third), F32),
    ]
    flops = 2 * rows * width * 6 * third
    return whole_call(kernel, outs, [dq, keep, got, w_mine, w_other], flops, "project_back")


def moments(summed):
    centre = jnp.mean(summed, axis=-1, keepdims=True)
    centred = summed - centre
    spread = jnp.mean(centred * centred, axis=-1, keepdims=True)
    back = lax.rsqrt(spread + NORM_EPS)
    return centred * back, back


def first_norm(x_own, part, got, b_out, gain, shift):
    dims = x_own.shape

    def kernel(x_ref, p_ref, r_ref, b_ref, g_ref, s_ref, summed_ref, normed_ref, low_ref):
        summed = x_ref[...].astype(F32) + (p_ref[...] + r_ref[...].astype(F32)) + b_ref[...]
        unit, _ = moments(summed)
        normed = unit * g_ref[...] + s_ref[...]
        summed_ref[...] = summed
        normed_ref[...] = normed
        low_ref[...] = normed.astype(BF16)

    outs = [shape(dims, F32), shape(dims, F32), shape(dims, BF16)]
    return whole_call(
        kernel, outs, [x_own, part, got, b_out, gain, shift], 20 * math.prod(dims), "first_norm"
    )


def second_norm(normed, part, got, cotangent, b_down, gain, shift):
    dims = normed.shape

    def kernel(n_ref, p_ref, r_ref, c_ref, b_ref, g_ref, s_ref, out_ref, grad_ref, low_ref, sums_ref):
        summed = n_ref[...] + (p_ref[...] + r_ref[...].astype(F32)) + b_ref[...]
        unit, back = moments(summed)
        out_ref[...] = (unit * g_ref[...] + s_ref[...]).astype(BF16)
        cot = c_ref[...].astype(F32)
        scaled = cot * g_ref[...]
        grad = back * (
            scaled
            - jnp.mean(scaled, axis=-1, keepdims=True)
            - unit * jnp.mean(scaled * unit, axis=-1, keepdims=True)
        )
        grad_ref[...] = grad
        low_ref[...] = grad.astype(BF16)
        sums_ref[0:1, :] = jnp.sum(cot * unit, axis=0, keepdims=True)
        sums_ref[1:2, :] = jnp.sum(cot, axis=0, keepdims=True)
        sums_ref[2:3, :] = jnp.sum(grad, axis=0, keepdims=True)

    outs = [shape(dims, BF16), shape(dims, F32), shape(dims, BF16), shape((3, dims[1]), F32)]
    return whole_call(
        kernel,
        outs,
        [normed, part, got, cotangent, b_down, gain, shift],
        40 * math.prod(dims),
        "second_norm",
    )


def first_norm_back(summed, grad_second, part, got, gain):
    dims = summed.shape

    def kernel(z_ref, gs_ref, p_ref, r_ref, g_ref, grad_ref, low_ref, sums_ref):
        unit, back = moments(z_ref[...])
        grad_normed = gs_ref[...] + (p_ref[...] + r_ref[...].astype(F32))
        scaled = grad_normed * g_ref[...]
        grad = back * (
            scaled
            - jnp.mean(scaled, axis=-1, keepdims=True)
            - unit * jnp.mean(scaled * unit, axis=-1, keepdims=True)
        )
        grad_ref[...] = grad
        low_ref[...] = grad.astype(BF16)
        sums_ref[0:1, :] = jnp.sum(grad_normed * unit, axis=0, keepdims=True)
        sums_ref[1:2, :] = jnp.sum(grad_normed, axis=0, keepdims=True)
        sums_ref[2:3, :] = jnp.sum(grad, axis=0, keepdims=True)

    outs = [shape(dims, F32), shape(dims, BF16), shape((3, dims[1]), F32)]
    return whole_call(
        kernel, outs, [summed, grad_second, part, got, gain], 40 * math.prod(dims), "first_norm_back"
    )


def streamed_call(kernel, grid, outs, out_specs, args, in_specs, flops, name, scratch):
    moved = sum(math.prod(a.shape) * a.dtype.itemsize for a in (*args, *outs))
    return pl.pallas_call(
        kernel,
        grid=grid,
        out_shape=tuple(outs),
        in_specs=in_specs,
        out_specs=tuple(out_specs),
        scratch_shapes=list(scratch),
        compiler_params=pltpu.CompilerParams(
            vmem_limit_bytes=VMEM_LIMIT, dimension_semantics=("arbitrary",)
        ),
        cost_estimate=pl.CostEstimate(flops=flops, bytes_accessed=moved, transcendentals=0),
        name=name,
    )(*args)


def const_spec(dims):
    return pl.BlockSpec(dims, lambda i: (0,) * len(dims))


def feed_forward(n_own, n_across, up_mine, up_other, down_mine, down_other, b_mine, b_other):
    block, width = n_own.shape
    rows = 2 * block
    hidden = up_mine.shape[1]
    tile = min(256, hidden)
    steps = hidden // tile

    def kernel(
        n0, n1, um, uo, dm, do, bm, bo,
        am_ref, ao_ref, sm_ref, so_ref, own_ref, across_ref, tokens, acc,
    ):
        step = pl.program_id(0)

        @pl.when(step == 0)
        def _():
            tokens[:block] = n0[...]
            tokens[block:] = n1[...]
            acc[...] = jnp.zeros_like(acc)

        total = acc[...]
        for u, d, b, a_ref, s_ref in ((um, dm, bm, am_ref, sm_ref), (uo, do, bo, ao_ref, so_ref)):
            hid = dot(tokens[...], u[...]) + b[...]
            half = 0.5 * (1.0 + lax.erf(hid * (1.0 / math.sqrt(2.0))))
            bell = jnp.exp(hid * hid * -0.5) * (1.0 / math.sqrt(2.0 * math.pi))
            active = (hid * half).astype(BF16)
            a_ref[...] = active
            s_ref[...] = (half + hid * bell).astype(BF16)
            total = total + dot_nt(active, d[...])
        acc[...] = total

        @pl.when(step == steps - 1)
        def _():
            own_ref[...] = acc[:block]
            across_ref[...] = acc[block:].astype(BF16)

    column = pl.BlockSpec((width, tile), lambda i: (0, i))
    bias = pl.BlockSpec((1, tile), lambda i: (0, i))
    made = pl.BlockSpec((rows, tile), lambda i: (0, i))
    outs = [shape((rows, hidden), BF16)] * 4 + [shape((block, width), F32), shape((block, width), BF16)]
    return streamed_call(
        kernel,
        (steps,),
        outs,
        [made] * 4 + [const_spec((block, width))] * 2,
        [n_own, n_across, up_mine, up_other, down_mine, down_other, b_mine, b_other],
        [const_spec((block, width))] * 2 + [column] * 4 + [bias] * 2,
        2 * 2 * rows * width * 2 * hidden,
        "feed_forward",
        [pltpu.VMEM((rows, width), BF16), pltpu.VMEM((rows, width), F32)],
    )


def feed_forward_back(g_own, g_across, up_mine, up_other, down_mine, down_other, slope_mine, slope_other):
    block, width = g_own.shape
    rows = 2 * block
    hidden = up_mine.shape[1]
    tile = min(256, hidden)
    steps = hidden // tile

    def kernel(
        g0, g1, um, uo, dm, do, sm, so,
        gm_ref, go_ref, own_ref, across_ref, bm_ref, bo_ref, grads, acc,
    ):
        step = pl.program_id(0)

        @pl.when(step == 0)
        def _():
            grads[:block] = g0[...]
            grads[block:] = g1[...]
            acc[...] = jnp.zeros_like(acc)

        total = acc[...]
        for u, d, s, g_ref, b_ref in ((um, dm, sm, gm_ref, bm_ref), (uo, do, so, go_ref, bo_ref)):
            grad_hidden = (dot(grads[...], d[...]) * s[...].astype(F32)).astype(BF16)
            g_ref[...] = grad_hidden
            b_ref[...] = jnp.sum(grad_hidden.astype(F32), axis=0, keepdims=True)
            total = total + dot_nt(grad_hidden, u[...])
        acc[...] = total

        @pl.when(step == steps - 1)
        def _():
            own_ref[...] = acc[:block]
            across_ref[...] = acc[block:].astype(BF16)

    column = pl.BlockSpec((width, tile), lambda i: (0, i))
    bias = pl.BlockSpec((1, tile), lambda i: (0, i))
    made = pl.BlockSpec((rows, tile), lambda i: (0, i))
    outs = (
        [shape((rows, hidden), BF16)] * 2
        + [shape((block, width), F32), shape((block, width), BF16)]
        + [shape((1, hidden), F32)] * 2
    )
    return streamed_call(
        kernel,
        (steps,),
        outs,
        [made] * 2 + [const_spec((block, width))] * 2 + [bias] * 2,
        [g_own, g_across, up_mine, up_other, down_mine, down_other, slope_mine, slope_other],
        [const_spec((block, width))] * 2 + [column] * 4 + [made] * 2,
        2 * 2 * rows * width * 2 * hidden,
        "feed_forward_back",
        [pltpu.VMEM((rows, width), BF16), pltpu.VMEM((rows, width), F32)],
    )


def weight_grad(ones, mine, other):
    kept = sum(dot_tn(a, b) for a, b in zip(ones, mine))
    sent = sum(dot_tn(a, b) for a, b in zip(ones, other))
    kept = kept + swap_tensor(sent.astype(BF16), CORE).astype(F32)
    return scatter_dp(kept)


def shards(
    inputs,
    lengths,
    w_query,
    w_key,
    w_value,
    w_out,
    w_up,
    w_down,
    b_query,
    b_value,
    b_out,
    b_up,
    b_down,
    first_gain,
    first_shift,
    second_gain,
    second_shift,
    cotangent,
):
    seq_count, block, width = inputs.shape
    tensor_size = lax.axis_size("tensor")
    seq_len = block * tensor_size
    place = lax.axis_index("tensor")
    head_dims = w_query.shape[1]
    head_size = width // HEADS
    seqs = range(seq_count)
    row = lambda vector: vector.reshape(1, -1)

    x_own = [inputs[s] for s in seqs]
    x_across = [swap_tensor(x_own[s], ACROSS) for s in seqs]

    qkv_mine = gather_dp(jnp.concatenate([w_query, w_key, w_value], axis=1))
    qkv_other = swap_tensor(qkv_mine, CORE)
    out_mine = gather_dp(w_out.T)
    out_other = swap_tensor(out_mine, CORE)
    up_mine = gather_dp(w_up)
    up_other = swap_tensor(up_mine, CORE)
    down_mine = gather_dp(w_down.T)
    down_other = swap_tensor(down_mine, CORE)

    biases = jnp.concatenate([b_query, jnp.zeros_like(b_query), b_value, b_up])
    biases_other = swap_tensor(biases, CORE)
    qkv_bias_mine, up_bias_mine = row(biases[: 3 * head_dims]), row(biases[3 * head_dims :])
    qkv_bias_other = row(biases_other[: 3 * head_dims])
    up_bias_other = row(biases_other[3 * head_dims :])
    b_out_row, b_down_row = row(b_out), row(b_down)
    gain_one, shift_one = row(first_gain), row(first_shift)
    gain_two, shift_two = row(second_gain), row(second_shift)

    order = jnp.stack([place, place ^ ACROSS, place ^ CORE, place ^ CORE ^ ACROSS])
    positions = (order[:, None] * block + jnp.arange(block, dtype=jnp.int32)[None, :]).reshape(-1)
    masks = [jnp.where(positions < lengths[s], 0.0, MASKED).astype(F32) for s in seqs]

    projected = [
        project_inputs(x_own[s], x_across[s], qkv_mine, qkv_other, qkv_bias_mine, qkv_bias_other)
        for s in seqs
    ]
    far = [swap_tensor(projected[s][2], CORE) for s in seqs]
    attended = [
        attention_forward(
            projected[s][0], projected[s][1], far[s], masks[s].reshape(1, seq_len),
            out_mine, out_other, head_size,
        )
        for s in seqs
    ]
    attended_got = [swap_tensor(attended[s][3], ACROSS) for s in seqs]
    one = [
        first_norm(x_own[s], attended[s][2], attended_got[s], b_out_row, gain_one, shift_one)
        for s in seqs
    ]
    normed_across = [swap_tensor(one[s][2], ACROSS) for s in seqs]
    fed = [
        feed_forward(
            one[s][2], normed_across[s], up_mine, up_other, down_mine, down_other,
            up_bias_mine, up_bias_other,
        )
        for s in seqs
    ]
    branch_got = [swap_tensor(fed[s][5], ACROSS) for s in seqs]
    two = [
        second_norm(
            one[s][1], fed[s][4], branch_got[s], cotangent[s], b_down_row, gain_two, shift_two
        )
        for s in seqs
    ]
    grad_across = [swap_tensor(two[s][2], ACROSS) for s in seqs]
    fed_back = [
        feed_forward_back(
            two[s][2], grad_across[s], up_mine, up_other, down_mine, down_other, fed[s][2], fed[s][3]
        )
        for s in seqs
    ]
    back_got = [swap_tensor(fed_back[s][3], ACROSS) for s in seqs]
    one_back = [
        first_norm_back(one[s][0], two[s][1], fed_back[s][2], back_got[s], gain_one) for s in seqs
    ]
    first_across = [swap_tensor(one_back[s][1], ACROSS) for s in seqs]

    grad_rows = [jnp.concatenate([two[s][2], grad_across[s]]) for s in seqs]
    down_grad = weight_grad(grad_rows, [fed[s][0] for s in seqs], [fed[s][1] for s in seqs])
    normed_rows = [jnp.concatenate([one[s][2], normed_across[s]]) for s in seqs]
    up_grad = weight_grad(normed_rows, [fed_back[s][0] for s in seqs], [fed_back[s][1] for s in seqs])

    attended_back = [
        attention_backward(
            projected[s][0], projected[s][1], far[s], masks[s].reshape(seq_len, 1),
            one_back[s][1], first_across[s], out_mine, out_other, head_size,
        )
        for s in seqs
    ]
    first_rows = [jnp.concatenate([one_back[s][1], first_across[s]]) for s in seqs]
    out_grad = weight_grad(first_rows, [attended[s][0] for s in seqs], [attended[s][1] for s in seqs])

    far_back = [swap_tensor(attended_back[s][2], CORE) for s in seqs]
    back = [
        project_back(attended_back[s][0], attended_back[s][1], far_back[s], qkv_mine, qkv_other)
        for s in seqs
    ]
    input_got = [swap_tensor(back[s][3], ACROSS) for s in seqs]
    input_grad = jnp.stack(
        [
            (one_back[s][0] + (back[s][2] + input_got[s].astype(F32))).astype(BF16)
            for s in seqs
        ]
    )
    token_rows = [jnp.concatenate([x_own[s], x_across[s]]) for s in seqs]
    qkv_grad = weight_grad(token_rows, [back[s][0] for s in seqs], [back[s][1] for s in seqs])

    def placed_in(part_mine, part_other):
        size = part_mine.shape[0]
        empty = jnp.zeros((tensor_size * size,), F32)
        empty = lax.dynamic_update_slice(empty, part_mine, (place * size,))
        return lax.dynamic_update_slice(empty, part_other, ((place ^ CORE) * size,))

    hidden = up_mine.shape[1]
    early = sum_all(
        jnp.concatenate(
            [
                sum(two[s][3] for s in seqs).reshape(-1),
                sum(one_back[s][2] for s in seqs).reshape(-1),
                placed_in(
                    sum(fed_back[s][4] for s in seqs).reshape(-1),
                    sum(fed_back[s][5] for s in seqs).reshape(-1),
                ),
            ]
        )
    )
    sums = sum(back[s][4] for s in seqs)
    late = sum_all(
        jnp.concatenate(
            [
                placed_in(sums[0, :head_dims], sums[1, :head_dims]),
                placed_in(sums[0, 2 * head_dims :], sums[1, 2 * head_dims :]),
            ]
        )
    )
    vectors = [early[i * width : (i + 1) * width] for i in range(6)]
    second_gain_grad, second_shift_grad, b_down_grad = vectors[:3]
    first_gain_grad, first_shift_grad, b_out_grad = vectors[3:]
    b_up_grad = early[6 * width : 6 * width + tensor_size * hidden]
    b_query_grad, b_value_grad = late[:width], late[width:]

    output = jnp.stack([two[s][0] for s in seqs])
    return (
        output,
        input_grad,
        qkv_grad[:, :head_dims],
        qkv_grad[:, head_dims : 2 * head_dims],
        qkv_grad[:, 2 * head_dims :],
        out_grad.T,
        up_grad,
        down_grad.T,
        b_query_grad,
        b_value_grad,
        b_out_grad,
        b_up_grad,
        b_down_grad,
        first_gain_grad,
        first_shift_grad,
        second_gain_grad,
        second_shift_grad,
    )


def solution(mesh):
    placed = (
        P("dp", "tensor", None),
        P("dp"),
        P("dp", "tensor"),
        P("dp", "tensor"),
        P("dp", "tensor"),
        P("tensor", "dp"),
        P("dp", "tensor"),
        P("tensor", "dp"),
        P("tensor"),
        P("tensor"),
        P(),
        P("tensor"),
        P(),
        P(),
        P(),
        P(),
        P(),
        P("dp", "tensor", None),
    )
    return jax.shard_map(
        shards,
        mesh=mesh,
        in_specs=placed,
        out_specs=(
            P("dp", "tensor", None),
            P("dp", "tensor", None),
            P("dp", "tensor"),
            P("dp", "tensor"),
            P("dp", "tensor"),
            P("tensor", "dp"),
            P("dp", "tensor"),
            P("tensor", "dp"),
            P(),
            P(),
            P(),
            P(),
            P(),
            P(),
            P(),
            P(),
            P(),
        ),
        check_vma=False,
    )
```

```python
import math

import jax
import jax.numpy as jnp
from jax import lax
from jax.experimental import pallas as pl
from jax.experimental.pallas import tpu as pltpu
from jax.sharding import PartitionSpec as P

HEADS = 16
NORM_EPS = 1e-12
MASKED = -1000000000.0
MIB = 1024 * 1024
VMEM_LIMIT = 32 * MIB

F32 = jnp.float32
BF16 = jnp.bfloat16

CORE = 1
ACROSS = 2


def dot(one, two):
    return lax.dot_general(one, two, (((1,), (0,)), ((), ())), preferred_element_type=F32)


def dot_nt(one, two):
    return lax.dot_general(one, two, (((1,), (1,)), ((), ())), preferred_element_type=F32)


def shape(dims, kind):
    return jax.ShapeDtypeStruct(dims, kind)


def after(kernel, count, deps):
    def body(*refs):
        kernel(*refs[:count], *refs[count + len(deps) :])

    return body


def whole_call(kernel, outs, args, flops, name, scratch=(), deps=()):
    moved = sum(math.prod(a.shape) * a.dtype.itemsize for a in (*args, *outs))
    return pl.pallas_call(
        after(kernel, len(args), deps),
        out_shape=tuple(outs),
        in_specs=[pl.BlockSpec(memory_space=pltpu.VMEM)] * len(args)
        + [pl.BlockSpec(memory_space=pl.ANY)] * len(deps),
        out_specs=tuple([pl.BlockSpec(memory_space=pltpu.VMEM)] * len(outs)),
        scratch_shapes=list(scratch),
        compiler_params=pltpu.CompilerParams(vmem_limit_bytes=VMEM_LIMIT),
        cost_estimate=pl.CostEstimate(flops=flops, bytes_accessed=moved, transcendentals=0),
        name=name,
    )(*args, *deps)


def streamed_call(kernel, grid, outs, out_specs, args, in_specs, flops, name, scratch, deps=()):
    moved = sum(math.prod(a.shape) * a.dtype.itemsize for a in (*args, *outs))
    return pl.pallas_call(
        after(kernel, len(args), deps),
        grid=grid,
        out_shape=tuple(outs),
        in_specs=list(in_specs) + [pl.BlockSpec(memory_space=pl.ANY)] * len(deps),
        out_specs=tuple(out_specs),
        scratch_shapes=list(scratch),
        compiler_params=pltpu.CompilerParams(
            vmem_limit_bytes=VMEM_LIMIT, dimension_semantics=("arbitrary",)
        ),
        cost_estimate=pl.CostEstimate(flops=flops, bytes_accessed=moved, transcendentals=0),
        name=name,
    )(*args, *deps)


def const_spec(dims):
    return pl.BlockSpec(dims, lambda i: (0,) * len(dims))


def swap_tensor(array, bit):
    size = lax.axis_size("tensor")
    return lax.ppermute(array, "tensor", [(i, i ^ bit) for i in range(size)])


def swap_dp(array, bit):
    size = lax.axis_size("dp")
    return lax.ppermute(array, "dp", [(i, i ^ bit) for i in range(size)])


def pack(parts, name, deps=()):
    def kernel(*refs):
        at = 0
        for ref in refs[:-1]:
            refs[-1][:, at : at + ref.shape[1]] = ref[...]
            at += ref.shape[1]

    out = shape((parts[0].shape[0], sum(p.shape[1] for p in parts)), parts[0].dtype)
    return whole_call(kernel, [out], parts, 0, name, deps=deps)[0]


def gather_far(rows):
    pieces = [(rows, [0])]
    step = lax.axis_size("dp") // 2
    while step > 1:
        if len(pieces) > 2:
            pieces = [merged(pieces)]
        pieces += [(swap_dp(p, step), [o ^ step for o in offsets]) for p, offsets in pieces]
        step //= 2
    return pieces


def merged(pieces):
    return (
        jnp.concatenate([p for p, _ in pieces], axis=0),
        [o for _, offsets in pieces for o in offsets],
    )


def gather_near(pieces):
    return [(swap_dp(p, 1), [o ^ 1 for o in offsets]) for p, offsets in pieces]


def assemble(pieces, dp_place, name, deps=()):
    rows = pieces[0][0].shape[0] // len(pieces[0][1])
    width = pieces[0][0].shape[1]
    size = lax.axis_size("dp")

    def kernel(*refs):
        place = refs[0][0]
        for ref, (_, offsets) in zip(refs[1:-1], pieces):
            for i, offset in enumerate(offsets):
                start = pl.multiple_of((place ^ offset) * rows, rows)
                refs[-1][pl.ds(start, rows), :] = ref[i * rows : (i + 1) * rows, :]

    arrays = [p for p, _ in pieces]
    out = shape((size * rows, width), BF16)
    moved = 2 * size * rows * width * 2
    return pl.pallas_call(
        after(kernel, 1 + len(arrays), deps),
        out_shape=out,
        in_specs=[pl.BlockSpec(memory_space=pltpu.SMEM)]
        + [pl.BlockSpec(memory_space=pltpu.VMEM)] * len(arrays)
        + [pl.BlockSpec(memory_space=pl.ANY)] * len(deps),
        out_specs=pl.BlockSpec(memory_space=pltpu.VMEM),
        compiler_params=pltpu.CompilerParams(vmem_limit_bytes=VMEM_LIMIT),
        cost_estimate=pl.CostEstimate(flops=0, bytes_accessed=moved, transcendentals=0),
        name=name,
    )(dp_place, *arrays, *deps)


def halving_order(size, bits):
    order = [0]
    for bit in reversed(bits):
        order = order + [o ^ (1 << bit) for o in order]
    return order


def scatter_dp(kept, got, bits):
    arrivals = [got]
    total = kept + got.astype(F32)
    for bit in bits:
        half = total.shape[0] // 2
        came = swap_dp(total[half:].astype(BF16), 1 << bit)
        arrivals.append(came)
        total = total[:half] + came.astype(F32)
    return total, arrivals


def sum_all(vector):
    step = 1
    while step < lax.axis_size("tensor"):
        vector = vector + swap_tensor(vector, step)
        step *= 2
    step = 1
    while step < lax.axis_size("dp"):
        vector = vector + swap_dp(vector, step)
        step *= 2
    return vector


def project_inputs(x_own, x_across, w_mine, w_other, b_mine, b_other):
    rows, width = x_own.shape
    third = w_mine.shape[1] // 4

    def kernel(x0, x1, wm, wo, bm, bo, mine_ref, other_ref, send_ref):
        tokens = jnp.concatenate([x0[...], x1[...]], axis=0)
        mine = (dot(tokens, wm[:, : 3 * third]) + bm[...]).astype(BF16)
        other = (dot(tokens, wo[:, : 3 * third]) + bo[...]).astype(BF16)
        mine_ref[...] = mine
        other_ref[...] = other
        send_ref[:, : 2 * third] = other[:, third:]
        send_ref[:, 2 * third :] = mine[:, third:]

    outs = [
        shape((2 * rows, 3 * third), BF16),
        shape((2 * rows, 3 * third), BF16),
        shape((2 * rows, 4 * third), BF16),
    ]
    flops = 2 * 2 * rows * width * 6 * third
    return whole_call(
        kernel, outs, [x_own, x_across, w_mine, w_other, b_mine, b_other], flops, "project_inputs"
    )


def attention_forward(mine, other, far, bias_row, w_mine, w_other, head_size, deps):
    rows = mine.shape[0]
    third = mine.shape[1] // 3
    heads = third // head_size
    block = rows // 2
    width = w_mine.shape[0]
    scaling = 1.0 / math.sqrt(head_size)

    def kernel(mine_ref, other_ref, far_ref, bias_ref, wm, wo, cm_ref, co_ref, own_ref, across_ref, acc):
        lane_head = lax.broadcasted_iota(jnp.int32, (1, third), 1) // head_size
        acc[...] = jnp.zeros_like(acc)
        bias = bias_ref[...]

        def one_head(head, carry):
            inside = lane_head == head
            for group, ref in enumerate((mine_ref, other_ref)):
                base = 2 * third * group
                keys = jnp.concatenate(
                    [ref[:, third : 2 * third], far_ref[:, base : base + third]], axis=0
                )
                vals = jnp.concatenate(
                    [ref[:, 2 * third :], far_ref[:, base + third : base + 2 * third]], axis=0
                )
                for part in range(2):
                    span = slice(part * block, (part + 1) * block)
                    query = jnp.where(inside, ref[span, :third] * scaling, 0.0).astype(BF16)
                    scores = dot_nt(query, keys) + bias
                    peak = jnp.max(scores, axis=-1, keepdims=True)
                    weights = jnp.exp(scores - peak)
                    total = jnp.sum(weights, axis=-1, keepdims=True)
                    found = dot(weights.astype(BF16), vals) * (1.0 / total)
                    acc[group, span, :] += jnp.where(inside, found, 0.0)
            return carry

        lax.fori_loop(0, heads, one_head, 0)
        ctx_mine = acc[0].astype(BF16)
        ctx_other = acc[1].astype(BF16)
        cm_ref[...] = ctx_mine
        co_ref[...] = ctx_other
        part_sum = dot_nt(ctx_mine, wm[:, 3 * third :]) + dot_nt(ctx_other, wo[:, 3 * third :])
        own_ref[...] = part_sum[:block]
        across_ref[...] = part_sum[block:].astype(BF16)

    outs = [
        shape((rows, third), BF16),
        shape((rows, third), BF16),
        shape((block, width), F32),
        shape((block, width), BF16),
    ]
    flops = 2 * 2 * 2 * rows * 2 * rows * third * heads * 2
    return whole_call(
        kernel,
        outs,
        [mine, other, far, bias_row, w_mine, w_other],
        flops,
        "attention_forward",
        [pltpu.VMEM((2, rows, third), F32)],
        deps,
    )


def attention_backward(mine, other, far, bias_column, ga_own, ga_across, w_mine, w_other, head_size, deps):
    rows = mine.shape[0]
    third = mine.shape[1] // 3
    heads = third // head_size
    block = rows // 2
    keys_count = 2 * rows
    scaling = 1.0 / math.sqrt(head_size)

    def kernel(
        mine_ref, other_ref, far_ref, bias_ref, g0, g1, wm, wo,
        dq_ref, keep_ref, send_ref, grad_ctx, keys_t, dq_t, dkv,
    ):
        lane_head = lax.broadcasted_iota(jnp.int32, (1, third), 1) // head_size
        grad_rows = jnp.concatenate([g0[...], g1[...]], axis=0)
        grad_ctx[0] = dot(grad_rows, wm[:, 3 * third :]).astype(BF16)
        grad_ctx[1] = dot(grad_rows, wo[:, 3 * third :]).astype(BF16)
        dkv[...] = jnp.zeros_like(dkv)
        for group, ref in enumerate((mine_ref, other_ref)):
            base = 2 * third * group
            keys_t[group, :, :rows] = ref[:, third : 2 * third].T
            keys_t[group, :, rows:] = far_ref[:, base : base + third].T
        bias = bias_ref[...]

        def one_head(head, carry):
            inside = lane_head == head
            start = pl.multiple_of(head * head_size, head_size)
            for group, ref in enumerate((mine_ref, other_ref)):
                base = 2 * third * group
                keys = jnp.concatenate(
                    [ref[:, third : 2 * third], far_ref[:, base : base + third]], axis=0
                )
                vals = jnp.concatenate(
                    [ref[:, 2 * third :], far_ref[:, base + third : base + 2 * third]], axis=0
                )
                head_keys_t = keys_t[group, pl.ds(start, head_size), :]
                for part in range(2):
                    span = slice(part * block, (part + 1) * block)
                    query = jnp.where(inside, ref[span, :third] * scaling, 0.0).astype(BF16)
                    grad = jnp.where(inside, grad_ctx[group, span, :], 0.0).astype(BF16)
                    scores = dot_nt(keys, query) + bias
                    peak = jnp.max(scores, axis=0, keepdims=True)
                    weights = jnp.exp(scores - peak)
                    total = jnp.sum(weights, axis=0, keepdims=True)
                    probs = weights * (1.0 / total)
                    grad_probs = dot_nt(vals, grad)
                    inner = jnp.sum(probs * grad_probs, axis=0, keepdims=True)
                    grad_scores = (probs * (grad_probs - inner)).astype(BF16)
                    dkv[group, 1] += dot(probs.astype(BF16), grad)
                    dkv[group, 0] += dot(grad_scores, query)
                    dq_t[group, pl.ds(start, head_size), span] = dot(head_keys_t, grad_scores)
            return carry

        lax.fori_loop(0, heads, one_head, 0)
        for group in range(2):
            dq_ref[:, group * third : (group + 1) * third] = (dq_t[group].T * scaling).astype(BF16)
            for kind in range(2):
                at = (2 * group + kind) * third
                keep_ref[:, at : at + third] = dkv[group, kind, :rows]
                away = (2 * (1 - group) + kind) * third
                send_ref[:, away : away + third] = dkv[group, kind, rows:].astype(BF16)

    outs = [
        shape((rows, 2 * third), BF16),
        shape((rows, 4 * third), F32),
        shape((rows, 4 * third), BF16),
    ]
    flops = 5 * 2 * 2 * rows * keys_count * third * heads
    return whole_call(
        kernel,
        outs,
        [mine, other, far, bias_column, ga_own, ga_across, w_mine, w_other],
        flops,
        "attention_backward",
        [
            pltpu.VMEM((2, rows, third), BF16),
            pltpu.VMEM((2, third, keys_count), BF16),
            pltpu.VMEM((2, third, rows), F32),
            pltpu.VMEM((2, 2, keys_count, third), F32),
        ],
        deps,
    )


def project_back(dq, keep, got, w_mine, w_other, deps):
    rows = dq.shape[0]
    third = dq.shape[1] // 2
    block = rows // 2
    width = w_mine.shape[0]

    def kernel(dq_ref, keep_ref, got_ref, wm, wo, gm_ref, go_ref, own_ref, across_ref, sums_ref):
        dkv = (keep_ref[...] + got_ref[...].astype(F32)).astype(BF16)
        grad_mine = jnp.concatenate([dq_ref[:, :third], dkv[:, : 2 * third]], axis=1)
        grad_other = jnp.concatenate([dq_ref[:, third:], dkv[:, 2 * third :]], axis=1)
        gm_ref[...] = grad_mine
        go_ref[...] = grad_other
        back = dot_nt(grad_mine, wm[:, : 3 * third]) + dot_nt(grad_other, wo[:, : 3 * third])
        own_ref[...] = back[:block]
        across_ref[...] = back[block:].astype(BF16)
        sums_ref[0:1, :] = jnp.sum(grad_mine.astype(F32), axis=0, keepdims=True)
        sums_ref[1:2, :] = jnp.sum(grad_other.astype(F32), axis=0, keepdims=True)

    outs = [
        shape((rows, 3 * third), BF16),
        shape((rows, 3 * third), BF16),
        shape((block, width), F32),
        shape((block, width), BF16),
        shape((2, 3 * third), F32),
    ]
    flops = 2 * rows * width * 6 * third
    return whole_call(
        kernel, outs, [dq, keep, got, w_mine, w_other], flops, "project_back", deps=deps
    )


def moments(summed):
    centre = jnp.mean(summed, axis=-1, keepdims=True)
    centred = summed - centre
    spread = jnp.mean(centred * centred, axis=-1, keepdims=True)
    back = lax.rsqrt(spread + NORM_EPS)
    return centred * back, back


def first_norm(x_own, part, got, b_out, gain, shift):
    dims = x_own.shape

    def kernel(x_ref, p_ref, r_ref, b_ref, g_ref, s_ref, summed_ref, normed_ref, low_ref):
        summed = x_ref[...].astype(F32) + (p_ref[...] + r_ref[...].astype(F32)) + b_ref[...]
        unit, _ = moments(summed)
        normed = unit * g_ref[...] + s_ref[...]
        summed_ref[...] = summed
        normed_ref[...] = normed
        low_ref[...] = normed.astype(BF16)

    outs = [shape(dims, F32), shape(dims, F32), shape(dims, BF16)]
    return whole_call(
        kernel, outs, [x_own, part, got, b_out, gain, shift], 20 * math.prod(dims), "first_norm"
    )


def second_norm(normed, part, got, cotangent, b_down, gain, shift):
    dims = normed.shape

    def kernel(n_ref, p_ref, r_ref, c_ref, b_ref, g_ref, s_ref, out_ref, grad_ref, low_ref, sums_ref):
        summed = n_ref[...] + (p_ref[...] + r_ref[...].astype(F32)) + b_ref[...]
        unit, back = moments(summed)
        out_ref[...] = (unit * g_ref[...] + s_ref[...]).astype(BF16)
        cot = c_ref[...].astype(F32)
        scaled = cot * g_ref[...]
        grad = back * (
            scaled
            - jnp.mean(scaled, axis=-1, keepdims=True)
            - unit * jnp.mean(scaled * unit, axis=-1, keepdims=True)
        )
        grad_ref[...] = grad
        low_ref[...] = grad.astype(BF16)
        sums_ref[0:1, :] = jnp.sum(cot * unit, axis=0, keepdims=True)
        sums_ref[1:2, :] = jnp.sum(cot, axis=0, keepdims=True)
        sums_ref[2:3, :] = jnp.sum(grad, axis=0, keepdims=True)

    outs = [shape(dims, BF16), shape(dims, F32), shape(dims, BF16), shape((3, dims[1]), F32)]
    return whole_call(
        kernel,
        outs,
        [normed, part, got, cotangent, b_down, gain, shift],
        40 * math.prod(dims),
        "second_norm",
    )


def first_norm_back(summed, grad_second, part, got, gain):
    dims = summed.shape

    def kernel(z_ref, gs_ref, p_ref, r_ref, g_ref, grad_ref, low_ref, sums_ref):
        unit, back = moments(z_ref[...])
        grad_normed = gs_ref[...] + (p_ref[...] + r_ref[...].astype(F32))
        scaled = grad_normed * g_ref[...]
        grad = back * (
            scaled
            - jnp.mean(scaled, axis=-1, keepdims=True)
            - unit * jnp.mean(scaled * unit, axis=-1, keepdims=True)
        )
        grad_ref[...] = grad
        low_ref[...] = grad.astype(BF16)
        sums_ref[0:1, :] = jnp.sum(grad_normed * unit, axis=0, keepdims=True)
        sums_ref[1:2, :] = jnp.sum(grad_normed, axis=0, keepdims=True)
        sums_ref[2:3, :] = jnp.sum(grad, axis=0, keepdims=True)

    outs = [shape(dims, F32), shape(dims, BF16), shape((3, dims[1]), F32)]
    return whole_call(
        kernel, outs, [summed, grad_second, part, got, gain], 40 * math.prod(dims), "first_norm_back"
    )


def feed_forward(n_own, n_across, w_mine, w_other, b_mine, b_other):
    block, width = n_own.shape
    rows = 2 * block
    hidden = w_mine.shape[1] // 2
    tile = min(256, hidden)
    steps = hidden // tile

    def kernel(
        n0, n1, um, uo, dm, do, bm, bo,
        am_ref, ao_ref, sm_ref, so_ref, own_ref, across_ref, tokens, acc,
    ):
        step = pl.program_id(0)

        @pl.when(step == 0)
        def _():
            tokens[:block] = n0[...]
            tokens[block:] = n1[...]
            acc[...] = jnp.zeros_like(acc)

        total = acc[...]
        for u, d, b, a_ref, s_ref in ((um, dm, bm, am_ref, sm_ref), (uo, do, bo, ao_ref, so_ref)):
            hid = dot(tokens[...], u[...]) + b[...]
            half = 0.5 * (1.0 + lax.erf(hid * (1.0 / math.sqrt(2.0))))
            bell = jnp.exp(hid * hid * -0.5) * (1.0 / math.sqrt(2.0 * math.pi))
            active = (hid * half).astype(BF16)
            a_ref[...] = active
            s_ref[...] = (half + hid * bell).astype(BF16)
            total = total + dot_nt(active, d[...])
        acc[...] = total

        @pl.when(step == steps - 1)
        def _():
            own_ref[...] = acc[:block]
            across_ref[...] = acc[block:].astype(BF16)

    column = pl.BlockSpec((width, tile), lambda i: (0, i))
    later = pl.BlockSpec((width, tile), lambda i: (0, steps + i))
    bias = pl.BlockSpec((1, tile), lambda i: (0, i))
    made = pl.BlockSpec((rows, tile), lambda i: (0, i))
    outs = [shape((rows, hidden), BF16)] * 4 + [shape((block, width), F32), shape((block, width), BF16)]
    return streamed_call(
        kernel,
        (steps,),
        outs,
        [made] * 4 + [const_spec((block, width))] * 2,
        [n_own, n_across, w_mine, w_other, w_mine, w_other, b_mine, b_other],
        [const_spec((block, width))] * 2 + [column] * 2 + [later] * 2 + [bias] * 2,
        2 * 2 * rows * width * 2 * hidden,
        "feed_forward",
        [pltpu.VMEM((rows, width), BF16), pltpu.VMEM((rows, width), F32)],
    )


def feed_forward_back(g_own, g_across, w_mine, w_other, slope_mine, slope_other):
    block, width = g_own.shape
    rows = 2 * block
    hidden = w_mine.shape[1] // 2
    tile = min(256, hidden)
    steps = hidden // tile

    def kernel(
        g0, g1, um, uo, dm, do, sm, so,
        gm_ref, go_ref, own_ref, across_ref, bm_ref, bo_ref, grads, acc,
    ):
        step = pl.program_id(0)

        @pl.when(step == 0)
        def _():
            grads[:block] = g0[...]
            grads[block:] = g1[...]
            acc[...] = jnp.zeros_like(acc)

        total = acc[...]
        for u, d, s, g_ref, b_ref in ((um, dm, sm, gm_ref, bm_ref), (uo, do, so, go_ref, bo_ref)):
            grad_hidden = (dot(grads[...], d[...]) * s[...].astype(F32)).astype(BF16)
            g_ref[...] = grad_hidden
            b_ref[...] = jnp.sum(grad_hidden.astype(F32), axis=0, keepdims=True)
            total = total + dot_nt(grad_hidden, u[...])
        acc[...] = total

        @pl.when(step == steps - 1)
        def _():
            own_ref[...] = acc[:block]
            across_ref[...] = acc[block:].astype(BF16)

    column = pl.BlockSpec((width, tile), lambda i: (0, i))
    later = pl.BlockSpec((width, tile), lambda i: (0, steps + i))
    bias = pl.BlockSpec((1, tile), lambda i: (0, i))
    made = pl.BlockSpec((rows, tile), lambda i: (0, i))
    outs = (
        [shape((rows, hidden), BF16)] * 2
        + [shape((block, width), F32), shape((block, width), BF16)]
        + [shape((1, hidden), F32)] * 2
    )
    return streamed_call(
        kernel,
        (steps,),
        outs,
        [made] * 2 + [const_spec((block, width))] * 2 + [bias] * 2,
        [g_own, g_across, w_mine, w_other, w_mine, w_other, slope_mine, slope_other],
        [const_spec((block, width))] * 2 + [column] * 2 + [later] * 2 + [made] * 2,
        2 * 2 * rows * width * 2 * hidden,
        "feed_forward_back",
        [pltpu.VMEM((rows, width), BF16), pltpu.VMEM((rows, width), F32)],
    )


def weight_grad(ones, mine, other, dp_place, bits, first, count, tile, name):
    block, width = ones[0].shape
    rows = 2 * block
    tile = min(tile, count)
    size = lax.axis_size("dp")
    share = width // size
    order = halving_order(size, bits)

    def kernel(place_ref, a0, a1, a2, a3, m0, m1, o0, o1, mine_ref, other_ref, turned, full):
        @pl.when(pl.program_id(0) == 0)
        def _():
            for i, ref in enumerate((a0, a1, a2, a3)):
                turned[:, i * block : (i + 1) * block] = ref[...].T

        place = place_ref[0]
        for one, two, out_ref in ((m0, m1, mine_ref), (o0, o1, other_ref)):
            full[...] = dot(turned[:, :rows], one[...]) + dot(turned[:, rows:], two[...])
            for i, offset in enumerate(order):
                start = pl.multiple_of((place ^ offset) * share, share)
                out_ref[i * share : (i + 1) * share, :] = full[pl.ds(start, share), :].astype(
                    out_ref.dtype
                )

    base = first // tile
    column = pl.BlockSpec((rows, tile), lambda i: (0, base + i))
    made = pl.BlockSpec((width, tile), lambda i: (0, i))
    return streamed_call(
        kernel,
        (count // tile,),
        [shape((width, count), F32), shape((width, count), BF16)],
        [made] * 2,
        [dp_place, *ones, *mine, *other],
        [pl.BlockSpec(memory_space=pltpu.SMEM)] + [const_spec((block, width))] * 4 + [column] * 4,
        2 * 2 * rows * width * 2 * count,
        name,
        [pltpu.VMEM((width, 2 * rows), BF16), pltpu.VMEM((width, tile), F32)],
    )


def reduced(made, bits):
    return scatter_dp(made[0], swap_tensor(made[1], CORE), bits)


def shards(
    inputs,
    lengths,
    w_query,
    w_key,
    w_value,
    w_out,
    w_up,
    w_down,
    b_query,
    b_value,
    b_out,
    b_up,
    b_down,
    first_gain,
    first_shift,
    second_gain,
    second_shift,
    cotangent,
):
    seq_count, block, width = inputs.shape
    tensor_size = lax.axis_size("tensor")
    seq_len = block * tensor_size
    place = lax.axis_index("tensor")
    head_dims = w_query.shape[1]
    head_size = width // HEADS
    hidden = w_up.shape[1]
    seqs = range(seq_count)
    row = lambda vector: vector.reshape(1, -1)

    x_own = [inputs[s] for s in seqs]
    x_across = [swap_tensor(x_own[s], ACROSS) for s in seqs]

    dp_place = lax.axis_index("dp").astype(jnp.int32).reshape(1)
    pieces = gather_far(pack([w_query, w_key, w_value, w_out.T], "pack_attention"))
    far_last = pieces[-1][0]
    pieces += gather_near(pieces)
    att_mine = assemble(pieces, dp_place, "assemble_attention")
    att_other = swap_tensor(att_mine, CORE)
    fed_pieces = [merged(gather_far(pack([w_up, w_down.T], "pack_feed", [far_last])))]
    (held, offsets) = fed_pieces[0]
    cut = held.shape[0] // 2
    halves = [(held[:cut], offsets[: len(offsets) // 2]), (held[cut:], offsets[len(offsets) // 2 :])]
    near = gather_near(halves)
    ffw_mine = assemble([*halves, *near], dp_place, "assemble_feed")
    ffw_other = assemble(
        [(swap_tensor(p, CORE), o) for p, o in [*fed_pieces, *near]], dp_place, "assemble_feed_other"
    )

    biases = jnp.concatenate([b_query, jnp.zeros_like(b_query), b_value, b_up])
    biases_other = swap_tensor(biases, CORE)
    qkv_bias_mine, up_bias_mine = row(biases[: 3 * head_dims]), row(biases[3 * head_dims :])
    qkv_bias_other = row(biases_other[: 3 * head_dims])
    up_bias_other = row(biases_other[3 * head_dims :])
    b_out_row, b_down_row = row(b_out), row(b_down)
    gain_one, shift_one = row(first_gain), row(first_shift)
    gain_two, shift_two = row(second_gain), row(second_shift)

    order = jnp.stack([place, place ^ ACROSS, place ^ CORE, place ^ CORE ^ ACROSS])
    positions = (order[:, None] * block + jnp.arange(block, dtype=jnp.int32)[None, :]).reshape(-1)
    masks = [jnp.where(positions < lengths[s], 0.0, MASKED).astype(F32) for s in seqs]

    projected = [
        project_inputs(x_own[s], x_across[s], att_mine, att_other, qkv_bias_mine, qkv_bias_other)
        for s in seqs
    ]
    far = [swap_tensor(projected[s][2], CORE) for s in seqs]
    attended = [
        attention_forward(
            projected[s][0], projected[s][1], far[s], masks[s].reshape(1, seq_len),
            att_mine, att_other, head_size, [held] if s == 0 else [near[0][0]],
        )
        for s in seqs
    ]
    attended_got = [swap_tensor(attended[s][3], ACROSS) for s in seqs]
    one = [
        first_norm(x_own[s], attended[s][2], attended_got[s], b_out_row, gain_one, shift_one)
        for s in seqs
    ]
    normed_across = [swap_tensor(one[s][2], ACROSS) for s in seqs]
    fed = [
        feed_forward(
            one[s][2], normed_across[s], ffw_mine, ffw_other, up_bias_mine, up_bias_other,
        )
        for s in seqs
    ]
    branch_got = [swap_tensor(fed[s][5], ACROSS) for s in seqs]
    two = [
        second_norm(
            one[s][1], fed[s][4], branch_got[s], cotangent[s], b_down_row, gain_two, shift_two
        )
        for s in seqs
    ]
    grad_across = [swap_tensor(two[s][2], ACROSS) for s in seqs]
    fed_back = [
        feed_forward_back(
            two[s][2], grad_across[s], ffw_mine, ffw_other, fed[s][2], fed[s][3]
        )
        for s in seqs
    ]
    back_got = [swap_tensor(fed_back[s][3], ACROSS) for s in seqs]
    one_back = [
        first_norm_back(one[s][0], two[s][1], fed_back[s][2], back_got[s], gain_one) for s in seqs
    ]
    first_across = [swap_tensor(one_back[s][1], ACROSS) for s in seqs]

    def placed_in(part_mine, part_other):
        size = part_mine.shape[0]
        empty = jnp.zeros((tensor_size * size,), F32)
        empty = lax.dynamic_update_slice(empty, part_mine, (place * size,))
        return lax.dynamic_update_slice(empty, part_other, ((place ^ CORE) * size,))

    levels = range(lax.axis_size("dp").bit_length() - 1)
    near_first = list(levels)
    far_first = [1, 0, *levels[2:]] if len(near_first) > 1 else near_first

    def pairs(own, across):
        return [part for s in seqs for part in (own[s], across[s])]

    down_grad, down_came = reduced(
        weight_grad(
            pairs([two[s][2] for s in seqs], grad_across),
            [fed[s][0] for s in seqs], [fed[s][1] for s in seqs],
            dp_place, near_first, 0, hidden, 256, "w_down_grad",
        ),
        near_first,
    )
    up_grad, up_came = reduced(
        weight_grad(
            pairs([one[s][2] for s in seqs], normed_across),
            [fed_back[s][0] for s in seqs], [fed_back[s][1] for s in seqs],
            dp_place, far_first, 0, hidden, 256, "w_up_grad",
        ),
        far_first,
    )
    out_grad, out_came = reduced(
        weight_grad(
            pairs([one_back[s][1] for s in seqs], first_across),
            [attended[s][0] for s in seqs], [attended[s][1] for s in seqs],
            dp_place, near_first, 0, head_dims, 256, "w_out_grad",
        ),
        near_first,
    )

    early = sum_all(
        jnp.concatenate(
            [
                sum(two[s][3] for s in seqs).reshape(-1),
                sum(one_back[s][2] for s in seqs).reshape(-1),
                placed_in(
                    sum(fed_back[s][4] for s in seqs).reshape(-1),
                    sum(fed_back[s][5] for s in seqs).reshape(-1),
                ),
            ]
        )
    )

    attended_back = [
        attention_backward(
            projected[s][0], projected[s][1], far[s], masks[s].reshape(seq_len, 1),
            one_back[s][1], first_across[s], att_mine, att_other, head_size,
            [down_came[1], up_came[0]] if s == 0 else [down_came[2], up_came[1], out_came[0]],
        )
        for s in seqs
    ]
    far_back = [swap_tensor(attended_back[s][2], CORE) for s in seqs]
    back = [
        project_back(
            attended_back[s][0], attended_back[s][1], far_back[s], att_mine, att_other,
            [down_came[-1], up_came[2], out_came[1]] if s == 0 else [up_came[-1], out_came[2], early],
        )
        for s in seqs
    ]
    input_got = [swap_tensor(back[s][3], ACROSS) for s in seqs]
    input_grad = jnp.stack(
        [
            (one_back[s][0] + (back[s][2] + input_got[s].astype(F32))).astype(BF16)
            for s in seqs
        ]
    )
    part_cols = 3 * head_dims // 2
    qkv_grad = jnp.concatenate(
        [
            reduced(
                weight_grad(
                    pairs(x_own, x_across),
                    [back[s][0] for s in seqs], [back[s][1] for s in seqs],
                    dp_place, bits, i * part_cols, part_cols, part_cols, "w_qkv_grad",
                ),
                bits,
            )[0]
            for i, bits in enumerate((near_first, far_first))
        ],
        axis=1,
    )

    sums = sum(back[s][4] for s in seqs)
    late = sum_all(
        jnp.concatenate(
            [
                placed_in(sums[0, :head_dims], sums[1, :head_dims]),
                placed_in(sums[0, 2 * head_dims :], sums[1, 2 * head_dims :]),
            ]
        )
    )
    vectors = [early[i * width : (i + 1) * width] for i in range(6)]
    second_gain_grad, second_shift_grad, b_down_grad = vectors[:3]
    first_gain_grad, first_shift_grad, b_out_grad = vectors[3:]
    b_up_grad = early[6 * width : 6 * width + tensor_size * hidden]
    b_query_grad, b_value_grad = late[:width], late[width:]

    output = jnp.stack([two[s][0] for s in seqs])
    return (
        output,
        input_grad,
        qkv_grad[:, :head_dims],
        qkv_grad[:, head_dims : 2 * head_dims],
        qkv_grad[:, 2 * head_dims :],
        out_grad.T,
        up_grad,
        down_grad.T,
        b_query_grad,
        b_value_grad,
        b_out_grad,
        b_up_grad,
        b_down_grad,
        first_gain_grad,
        first_shift_grad,
        second_gain_grad,
        second_shift_grad,
    )


def solution(mesh):
    placed = (
        P("dp", "tensor", None),
        P("dp"),
        P("dp", "tensor"),
        P("dp", "tensor"),
        P("dp", "tensor"),
        P("tensor", "dp"),
        P("dp", "tensor"),
        P("tensor", "dp"),
        P("tensor"),
        P("tensor"),
        P(),
        P("tensor"),
        P(),
        P(),
        P(),
        P(),
        P(),
        P("dp", "tensor", None),
    )
    return jax.shard_map(
        shards,
        mesh=mesh,
        in_specs=placed,
        out_specs=(
            P("dp", "tensor", None),
            P("dp", "tensor", None),
            P("dp", "tensor"),
            P("dp", "tensor"),
            P("dp", "tensor"),
            P("tensor", "dp"),
            P("dp", "tensor"),
            P("tensor", "dp"),
            P(),
            P(),
            P(),
            P(),
            P(),
            P(),
            P(),
            P(),
            P(),
        ),
        check_vma=False,
    )
```

```python
import math

import jax
import jax.numpy as jnp
from jax import lax
from jax.experimental import pallas as pl
from jax.experimental.pallas import tpu as pltpu
from jax.sharding import PartitionSpec as P

HEADS = 16
NORM_EPS = 1e-12
MASKED = -1000000000.0
MIB = 1024 * 1024
VMEM_LIMIT = 56 * MIB
UNDERSTATED = 1000

F32 = jnp.float32
BF16 = jnp.bfloat16

CORE = 1
ACROSS = 2


def dot(one, two):
    return lax.dot_general(one, two, (((1,), (0,)), ((), ())), preferred_element_type=F32)


def dot_nt(one, two):
    return lax.dot_general(one, two, (((1,), (1,)), ((), ())), preferred_element_type=F32)


def shape(dims, kind):
    return jax.ShapeDtypeStruct(dims, kind)


def after(kernel, count, deps):
    def body(*refs):
        kernel(*refs[:count], *refs[count + len(deps) :])

    return body


def whole_call(kernel, outs, args, flops, name, scratch=(), deps=()):
    moved = sum(math.prod(a.shape) * a.dtype.itemsize for a in (*args, *outs))
    return pl.pallas_call(
        after(kernel, len(args), deps),
        out_shape=tuple(outs),
        in_specs=[pl.BlockSpec(memory_space=pltpu.VMEM)] * len(args)
        + [pl.BlockSpec(memory_space=pl.ANY)] * len(deps),
        out_specs=tuple([pl.BlockSpec(memory_space=pltpu.VMEM)] * len(outs)),
        scratch_shapes=list(scratch),
        compiler_params=pltpu.CompilerParams(vmem_limit_bytes=VMEM_LIMIT),
        cost_estimate=pl.CostEstimate(
            flops=flops // UNDERSTATED, bytes_accessed=moved // UNDERSTATED, transcendentals=0
        ),
        name=name,
    )(*args, *deps)


def streamed_call(kernel, grid, outs, out_specs, args, in_specs, flops, name, scratch, deps=()):
    moved = sum(math.prod(a.shape) * a.dtype.itemsize for a in (*args, *outs))
    return pl.pallas_call(
        after(kernel, len(args), deps),
        grid=grid,
        out_shape=tuple(outs),
        in_specs=list(in_specs) + [pl.BlockSpec(memory_space=pl.ANY)] * len(deps),
        out_specs=tuple(out_specs),
        scratch_shapes=list(scratch),
        compiler_params=pltpu.CompilerParams(
            vmem_limit_bytes=VMEM_LIMIT, dimension_semantics=("arbitrary",)
        ),
        cost_estimate=pl.CostEstimate(
            flops=flops // UNDERSTATED, bytes_accessed=moved // UNDERSTATED, transcendentals=0
        ),
        name=name,
    )(*args, *deps)


def const_spec(dims):
    return pl.BlockSpec(dims, lambda i: (0,) * len(dims))


def swap_tensor(array, bit):
    size = lax.axis_size("tensor")
    return lax.ppermute(array, "tensor", [(i, i ^ bit) for i in range(size)])


def swap_dp(array, bit):
    size = lax.axis_size("dp")
    return lax.ppermute(array, "dp", [(i, i ^ bit) for i in range(size)])


def pack(parts, name, deps=()):
    def kernel(*refs):
        at = 0
        for ref in refs[:-1]:
            refs[-1][:, at : at + ref.shape[1]] = ref[...]
            at += ref.shape[1]

    out = shape((parts[0].shape[0], sum(p.shape[1] for p in parts)), parts[0].dtype)
    return whole_call(kernel, [out], parts, 0, name, deps=deps)[0]


def gather_far(rows):
    pieces = [(rows, [0])]
    step = lax.axis_size("dp") // 2
    while step > 1:
        if len(pieces) > 2:
            pieces = [merged(pieces)]
        pieces += [(swap_dp(p, step), [o ^ step for o in offsets]) for p, offsets in pieces]
        step //= 2
    return pieces


def merged(pieces):
    return (
        jnp.concatenate([p for p, _ in pieces], axis=0),
        [o for _, offsets in pieces for o in offsets],
    )


def gather_near(pieces):
    return [(swap_dp(p, 1), [o ^ 1 for o in offsets]) for p, offsets in pieces]


def other_core(pieces):
    return [(swap_tensor(p, CORE), offsets) for p, offsets in pieces]


def assemble(pieces, dp_place, name, deps=()):
    rows = pieces[0][0].shape[0] // len(pieces[0][1])
    width = pieces[0][0].shape[1]
    size = lax.axis_size("dp")

    def kernel(*refs):
        place = refs[0][0]
        for ref, (_, offsets) in zip(refs[1:-1], pieces):
            for i, offset in enumerate(offsets):
                start = pl.multiple_of((place ^ offset) * rows, rows)
                refs[-1][pl.ds(start, rows), :] = ref[i * rows : (i + 1) * rows, :]

    arrays = [p for p, _ in pieces]
    out = shape((size * rows, width), BF16)
    moved = 2 * size * rows * width * 2
    return pl.pallas_call(
        after(kernel, 1 + len(arrays), deps),
        out_shape=out,
        in_specs=[pl.BlockSpec(memory_space=pltpu.SMEM)]
        + [pl.BlockSpec(memory_space=pltpu.VMEM)] * len(arrays)
        + [pl.BlockSpec(memory_space=pl.ANY)] * len(deps),
        out_specs=pl.BlockSpec(memory_space=pltpu.VMEM),
        compiler_params=pltpu.CompilerParams(vmem_limit_bytes=VMEM_LIMIT),
        cost_estimate=pl.CostEstimate(
            flops=0, bytes_accessed=moved // UNDERSTATED, transcendentals=0
        ),
        name=name,
    )(dp_place, *arrays, *deps)


def halving_order(size, bits):
    order = [0]
    for bit in reversed(bits):
        order = order + [o ^ (1 << bit) for o in order]
    return order


def scatter_dp(kept, got, bits):
    arrivals = [got]
    total = kept + got.astype(F32)
    for bit in bits:
        half = total.shape[0] // 2
        came = swap_dp(total[half:].astype(BF16), 1 << bit)
        arrivals.append(came)
        total = total[:half] + came.astype(F32)
    return total, arrivals


def sum_all(vector):
    step = 1
    while step < lax.axis_size("tensor"):
        vector = vector + swap_tensor(vector, step)
        step *= 2
    step = 1
    while step < lax.axis_size("dp"):
        vector = vector + swap_dp(vector, step)
        step *= 2
    return vector


def project_inputs(x_own, x_across, w_mine, w_other, b_mine, b_other, deps):
    rows, width = x_own.shape
    third = w_mine.shape[1] // 4

    def kernel(x0, x1, wm, wo, bm, bo, mine_ref, other_ref, send_ref):
        tokens = jnp.concatenate([x0[...], x1[...]], axis=0)
        mine = (dot(tokens, wm[:, : 3 * third]) + bm[...]).astype(BF16)
        other = (dot(tokens, wo[:, : 3 * third]) + bo[...]).astype(BF16)
        mine_ref[...] = mine
        other_ref[...] = other
        send_ref[:, : 2 * third] = other[:, third:]
        send_ref[:, 2 * third :] = mine[:, third:]

    outs = [
        shape((2 * rows, 3 * third), BF16),
        shape((2 * rows, 3 * third), BF16),
        shape((2 * rows, 4 * third), BF16),
    ]
    flops = 2 * 2 * rows * width * 6 * third
    return whole_call(
        kernel,
        outs,
        [x_own, x_across, w_mine, w_other, b_mine, b_other],
        flops,
        "project_inputs",
        deps=deps,
    )


def attention_forward(mine, other, far, bias_row, w_mine, w_other, head_size, deps):
    rows = mine.shape[0]
    third = mine.shape[1] // 3
    heads = third // head_size
    block = rows // 2
    width = w_mine.shape[0]
    scaling = 1.0 / math.sqrt(head_size)

    def kernel(mine_ref, other_ref, far_ref, bias_ref, wm, wo, cm_ref, co_ref, own_ref, across_ref, acc):
        lane_head = lax.broadcasted_iota(jnp.int32, (1, third), 1) // head_size
        acc[...] = jnp.zeros_like(acc)
        bias = bias_ref[...]

        def one_head(head, carry):
            inside = lane_head == head
            for group, ref in enumerate((mine_ref, other_ref)):
                base = 2 * third * group
                keys = jnp.concatenate(
                    [ref[:, third : 2 * third], far_ref[:, base : base + third]], axis=0
                )
                vals = jnp.concatenate(
                    [ref[:, 2 * third :], far_ref[:, base + third : base + 2 * third]], axis=0
                )
                for part in range(2):
                    span = slice(part * block, (part + 1) * block)
                    query = jnp.where(inside, ref[span, :third] * scaling, 0.0).astype(BF16)
                    scores = dot_nt(query, keys) + bias
                    peak = jnp.max(scores, axis=-1, keepdims=True)
                    weights = jnp.exp(scores - peak)
                    total = jnp.sum(weights, axis=-1, keepdims=True)
                    found = dot(weights.astype(BF16), vals) * (1.0 / total)
                    acc[group, span, :] += jnp.where(inside, found, 0.0)
            return carry

        lax.fori_loop(0, heads, one_head, 0)
        ctx_mine = acc[0].astype(BF16)
        ctx_other = acc[1].astype(BF16)
        cm_ref[...] = ctx_mine
        co_ref[...] = ctx_other
        part_sum = dot_nt(ctx_mine, wm[:, 3 * third :]) + dot_nt(ctx_other, wo[:, 3 * third :])
        own_ref[...] = part_sum[:block]
        across_ref[...] = part_sum[block:].astype(BF16)

    outs = [
        shape((rows, third), BF16),
        shape((rows, third), BF16),
        shape((block, width), F32),
        shape((block, width), BF16),
    ]
    flops = 2 * 2 * 2 * rows * 2 * rows * third * heads * 2
    return whole_call(
        kernel,
        outs,
        [mine, other, far, bias_row, w_mine, w_other],
        flops,
        "attention_forward",
        [pltpu.VMEM((2, rows, third), F32)],
        deps,
    )


def attention_backward(mine, other, far, bias_column, ga_own, ga_across, w_mine, w_other, head_size, deps):
    rows = mine.shape[0]
    third = mine.shape[1] // 3
    heads = third // head_size
    block = rows // 2
    keys_count = 2 * rows
    scaling = 1.0 / math.sqrt(head_size)

    def kernel(
        mine_ref, other_ref, far_ref, bias_ref, g0, g1, wm, wo,
        dq_ref, keep_ref, send_ref, sums_ref, grad_ctx, keys_t, dq_t, dkv,
    ):
        lane_head = lax.broadcasted_iota(jnp.int32, (1, third), 1) // head_size
        grad_rows = jnp.concatenate([g0[...], g1[...]], axis=0)
        grad_ctx[0] = dot(grad_rows, wm[:, 3 * third :]).astype(BF16)
        grad_ctx[1] = dot(grad_rows, wo[:, 3 * third :]).astype(BF16)
        dkv[...] = jnp.zeros_like(dkv)
        for group, ref in enumerate((mine_ref, other_ref)):
            base = 2 * third * group
            keys_t[group, :, :rows] = ref[:, third : 2 * third].T
            keys_t[group, :, rows:] = far_ref[:, base : base + third].T
        bias = bias_ref[...]

        def one_head(head, carry):
            inside = lane_head == head
            start = pl.multiple_of(head * head_size, head_size)
            for group, ref in enumerate((mine_ref, other_ref)):
                base = 2 * third * group
                keys = jnp.concatenate(
                    [ref[:, third : 2 * third], far_ref[:, base : base + third]], axis=0
                )
                vals = jnp.concatenate(
                    [ref[:, 2 * third :], far_ref[:, base + third : base + 2 * third]], axis=0
                )
                head_keys_t = keys_t[group, pl.ds(start, head_size), :]
                for part in range(2):
                    span = slice(part * block, (part + 1) * block)
                    query = jnp.where(inside, ref[span, :third] * scaling, 0.0).astype(BF16)
                    grad = jnp.where(inside, grad_ctx[group, span, :], 0.0).astype(BF16)
                    scores = dot_nt(keys, query) + bias
                    peak = jnp.max(scores, axis=0, keepdims=True)
                    weights = jnp.exp(scores - peak)
                    total = jnp.sum(weights, axis=0, keepdims=True)
                    probs = weights * (1.0 / total)
                    grad_probs = dot_nt(vals, grad)
                    inner = jnp.sum(probs * grad_probs, axis=0, keepdims=True)
                    grad_scores = (probs * (grad_probs - inner)).astype(BF16)
                    dkv[group, 1] += dot(probs.astype(BF16), grad)
                    dkv[group, 0] += dot(grad_scores, query)
                    dq_t[group, pl.ds(start, head_size), span] = dot(head_keys_t, grad_scores)
            return carry

        lax.fori_loop(0, heads, one_head, 0)
        for group in range(2):
            grad_query = (dq_t[group].T * scaling).astype(BF16)
            dq_ref[:, group * third : (group + 1) * third] = grad_query
            sums_ref[group : group + 1, :third] = jnp.sum(
                grad_query.astype(F32), axis=0, keepdims=True
            )
            sums_ref[group : group + 1, third:] = jnp.sum(dkv[group, 1], axis=0, keepdims=True)
            for kind in range(2):
                at = (2 * group + kind) * third
                keep_ref[:, at : at + third] = dkv[group, kind, :rows]
                away = (2 * (1 - group) + kind) * third
                send_ref[:, away : away + third] = dkv[group, kind, rows:].astype(BF16)

    outs = [
        shape((rows, 2 * third), BF16),
        shape((rows, 4 * third), F32),
        shape((rows, 4 * third), BF16),
        shape((2, 2 * third), F32),
    ]
    flops = 5 * 2 * 2 * rows * keys_count * third * heads
    return whole_call(
        kernel,
        outs,
        [mine, other, far, bias_column, ga_own, ga_across, w_mine, w_other],
        flops,
        "attention_backward",
        [
            pltpu.VMEM((2, rows, third), BF16),
            pltpu.VMEM((2, third, keys_count), BF16),
            pltpu.VMEM((2, third, rows), F32),
            pltpu.VMEM((2, 2, keys_count, third), F32),
        ],
        deps,
    )


def project_back(dq, keep, got, w_mine, w_other, deps):
    rows = dq.shape[0]
    third = dq.shape[1] // 2
    block = rows // 2
    width = w_mine.shape[0]

    def kernel(dq_ref, keep_ref, got_ref, wm, wo, gm_ref, go_ref, own_ref, across_ref):
        dkv = (keep_ref[...] + got_ref[...].astype(F32)).astype(BF16)
        grad_mine = jnp.concatenate([dq_ref[:, :third], dkv[:, : 2 * third]], axis=1)
        grad_other = jnp.concatenate([dq_ref[:, third:], dkv[:, 2 * third :]], axis=1)
        gm_ref[...] = dkv[:, : 2 * third]
        go_ref[...] = dkv[:, 2 * third :]
        back = dot_nt(grad_mine, wm[:, : 3 * third]) + dot_nt(grad_other, wo[:, : 3 * third])
        own_ref[...] = back[:block]
        across_ref[...] = back[block:].astype(BF16)

    outs = [
        shape((rows, 2 * third), BF16),
        shape((rows, 2 * third), BF16),
        shape((block, width), F32),
        shape((block, width), BF16),
    ]
    flops = 2 * rows * width * 6 * third
    return whole_call(
        kernel, outs, [dq, keep, got, w_mine, w_other], flops, "project_back", deps=deps
    )


def moments(summed):
    centre = jnp.mean(summed, axis=-1, keepdims=True)
    centred = summed - centre
    spread = jnp.mean(centred * centred, axis=-1, keepdims=True)
    back = lax.rsqrt(spread + NORM_EPS)
    return centred * back, back


def first_norm(x_own, part, got, b_out, gain, shift):
    dims = x_own.shape

    def kernel(x_ref, p_ref, r_ref, b_ref, g_ref, s_ref, summed_ref, normed_ref, low_ref):
        summed = x_ref[...].astype(F32) + (p_ref[...] + r_ref[...].astype(F32)) + b_ref[...]
        unit, _ = moments(summed)
        normed = unit * g_ref[...] + s_ref[...]
        summed_ref[...] = summed
        normed_ref[...] = normed
        low_ref[...] = normed.astype(BF16)

    outs = [shape(dims, F32), shape(dims, F32), shape(dims, BF16)]
    return whole_call(
        kernel, outs, [x_own, part, got, b_out, gain, shift], 20 * math.prod(dims), "first_norm"
    )


def second_norm(normed, part, got, cotangent, b_down, gain, shift):
    dims = normed.shape

    def kernel(n_ref, p_ref, r_ref, c_ref, b_ref, g_ref, s_ref, out_ref, grad_ref, low_ref, sums_ref):
        summed = n_ref[...] + (p_ref[...] + r_ref[...].astype(F32)) + b_ref[...]
        unit, back = moments(summed)
        out_ref[...] = (unit * g_ref[...] + s_ref[...]).astype(BF16)
        cot = c_ref[...].astype(F32)
        scaled = cot * g_ref[...]
        grad = back * (
            scaled
            - jnp.mean(scaled, axis=-1, keepdims=True)
            - unit * jnp.mean(scaled * unit, axis=-1, keepdims=True)
        )
        grad_ref[...] = grad
        low_ref[...] = grad.astype(BF16)
        sums_ref[0:1, :] = jnp.sum(cot * unit, axis=0, keepdims=True)
        sums_ref[1:2, :] = jnp.sum(cot, axis=0, keepdims=True)
        sums_ref[2:3, :] = jnp.sum(grad, axis=0, keepdims=True)

    outs = [shape(dims, BF16), shape(dims, F32), shape(dims, BF16), shape((3, dims[1]), F32)]
    return whole_call(
        kernel,
        outs,
        [normed, part, got, cotangent, b_down, gain, shift],
        40 * math.prod(dims),
        "second_norm",
    )


def first_norm_back(summed, grad_second, part, got, gain, deps):
    dims = summed.shape

    def kernel(z_ref, gs_ref, p_ref, r_ref, g_ref, grad_ref, low_ref, sums_ref):
        unit, back = moments(z_ref[...])
        grad_normed = gs_ref[...] + (p_ref[...] + r_ref[...].astype(F32))
        scaled = grad_normed * g_ref[...]
        grad = back * (
            scaled
            - jnp.mean(scaled, axis=-1, keepdims=True)
            - unit * jnp.mean(scaled * unit, axis=-1, keepdims=True)
        )
        grad_ref[...] = grad
        low_ref[...] = grad.astype(BF16)
        sums_ref[0:1, :] = jnp.sum(grad_normed * unit, axis=0, keepdims=True)
        sums_ref[1:2, :] = jnp.sum(grad_normed, axis=0, keepdims=True)
        sums_ref[2:3, :] = jnp.sum(grad, axis=0, keepdims=True)

    outs = [shape(dims, F32), shape(dims, BF16), shape((3, dims[1]), F32)]
    return whole_call(
        kernel,
        outs,
        [summed, grad_second, part, got, gain],
        40 * math.prod(dims),
        "first_norm_back",
        deps=deps,
    )


def feed_forward(n_own, n_across, w_mine, w_other, b_mine, b_other):
    block, width = n_own.shape
    rows = 2 * block
    hidden = w_mine.shape[1] // 2
    tile = min(256, hidden)
    steps = hidden // tile

    def kernel(
        n0, n1, um, uo, dm, do, bm, bo,
        am_ref, ao_ref, sm_ref, so_ref, own_ref, across_ref, tokens, acc,
    ):
        step = pl.program_id(0)

        @pl.when(step == 0)
        def _():
            tokens[:block] = n0[...]
            tokens[block:] = n1[...]
            acc[...] = jnp.zeros_like(acc)

        total = acc[...]
        for u, d, b, a_ref, s_ref in ((um, dm, bm, am_ref, sm_ref), (uo, do, bo, ao_ref, so_ref)):
            hid = dot(tokens[...], u[...]) + b[...]
            half = 0.5 * (1.0 + lax.erf(hid * (1.0 / math.sqrt(2.0))))
            bell = jnp.exp(hid * hid * -0.5) * (1.0 / math.sqrt(2.0 * math.pi))
            active = (hid * half).astype(BF16)
            a_ref[...] = active
            s_ref[...] = (half + hid * bell).astype(BF16)
            total = total + dot_nt(active, d[...])
        acc[...] = total

        @pl.when(step == steps - 1)
        def _():
            own_ref[...] = acc[:block]
            across_ref[...] = acc[block:].astype(BF16)

    column = pl.BlockSpec((width, tile), lambda i: (0, i))
    later = pl.BlockSpec((width, tile), lambda i: (0, steps + i))
    bias = pl.BlockSpec((1, tile), lambda i: (0, i))
    made = pl.BlockSpec((rows, tile), lambda i: (0, i))
    outs = [shape((rows, hidden), BF16)] * 4 + [shape((block, width), F32), shape((block, width), BF16)]
    return streamed_call(
        kernel,
        (steps,),
        outs,
        [made] * 4 + [const_spec((block, width))] * 2,
        [n_own, n_across, w_mine, w_other, w_mine, w_other, b_mine, b_other],
        [const_spec((block, width))] * 2 + [column] * 2 + [later] * 2 + [bias] * 2,
        2 * 2 * rows * width * 2 * hidden,
        "feed_forward",
        [pltpu.VMEM((rows, width), BF16), pltpu.VMEM((rows, width), F32)],
    )


def feed_forward_back(g_own, g_across, w_mine, w_other, slope_mine, slope_other):
    block, width = g_own.shape
    rows = 2 * block
    hidden = w_mine.shape[1] // 2
    tile = min(256, hidden)
    steps = hidden // tile

    def kernel(
        g0, g1, um, uo, dm, do, sm, so,
        gm_ref, go_ref, own_ref, across_ref, bm_ref, bo_ref, grads, acc,
    ):
        step = pl.program_id(0)

        @pl.when(step == 0)
        def _():
            grads[:block] = g0[...]
            grads[block:] = g1[...]
            acc[...] = jnp.zeros_like(acc)

        total = acc[...]
        for u, d, s, g_ref, b_ref in ((um, dm, sm, gm_ref, bm_ref), (uo, do, so, go_ref, bo_ref)):
            grad_hidden = (dot(grads[...], d[...]) * s[...].astype(F32)).astype(BF16)
            g_ref[...] = grad_hidden
            b_ref[...] = jnp.sum(grad_hidden.astype(F32), axis=0, keepdims=True)
            total = total + dot_nt(grad_hidden, u[...])
        acc[...] = total

        @pl.when(step == steps - 1)
        def _():
            own_ref[...] = acc[:block]
            across_ref[...] = acc[block:].astype(BF16)

    column = pl.BlockSpec((width, tile), lambda i: (0, i))
    later = pl.BlockSpec((width, tile), lambda i: (0, steps + i))
    bias = pl.BlockSpec((1, tile), lambda i: (0, i))
    made = pl.BlockSpec((rows, tile), lambda i: (0, i))
    outs = (
        [shape((rows, hidden), BF16)] * 2
        + [shape((block, width), F32), shape((block, width), BF16)]
        + [shape((1, hidden), F32)] * 2
    )
    return streamed_call(
        kernel,
        (steps,),
        outs,
        [made] * 2 + [const_spec((block, width))] * 2 + [bias] * 2,
        [g_own, g_across, w_mine, w_other, w_mine, w_other, slope_mine, slope_other],
        [const_spec((block, width))] * 2 + [column] * 2 + [later] * 2 + [made] * 2,
        2 * 2 * rows * width * 2 * hidden,
        "feed_forward_back",
        [pltpu.VMEM((rows, width), BF16), pltpu.VMEM((rows, width), F32)],
    )


def weight_grad(ones, mine, other, dp_place, bits, count, name, other_first=0, deps=()):
    block, width = ones[0].shape
    rows = 2 * block
    tile = min(256, count)
    size = lax.axis_size("dp")
    share = width // size
    order = halving_order(size, bits)

    def kernel(place_ref, a0, a1, a2, a3, m0, m1, o0, o1, mine_ref, other_ref, turned, full):
        @pl.when(pl.program_id(0) == 0)
        def _():
            for i, ref in enumerate((a0, a1, a2, a3)):
                turned[:, i * block : (i + 1) * block] = ref[...].T

        place = place_ref[0]
        for one, two, out_ref in ((m0, m1, mine_ref), (o0, o1, other_ref)):
            full[...] = dot(turned[:, :rows], one[...]) + dot(turned[:, rows:], two[...])
            for i, offset in enumerate(order):
                start = pl.multiple_of((place ^ offset) * share, share)
                out_ref[i * share : (i + 1) * share, :] = full[pl.ds(start, share), :].astype(
                    out_ref.dtype
                )

    base = other_first // tile
    column = pl.BlockSpec((rows, tile), lambda i: (0, i))
    other_column = pl.BlockSpec((rows, tile), lambda i: (0, base + i))
    made = pl.BlockSpec((width, tile), lambda i: (0, i))
    return streamed_call(
        kernel,
        (count // tile,),
        [shape((width, count), F32), shape((width, count), BF16)],
        [made] * 2,
        [dp_place, *ones, *mine, *other],
        [pl.BlockSpec(memory_space=pltpu.SMEM)] + [const_spec((block, width))] * 4 + [column] * 2 + [other_column] * 2,
        2 * 2 * rows * width * 2 * count,
        name,
        [pltpu.VMEM((width, 2 * rows), BF16), pltpu.VMEM((width, tile), F32)],
        deps,
    )


def reduced(made, bits):
    return scatter_dp(made[0], swap_tensor(made[1], CORE), bits)


def shards(
    inputs,
    lengths,
    w_query,
    w_key,
    w_value,
    w_out,
    w_up,
    w_down,
    b_query,
    b_value,
    b_out,
    b_up,
    b_down,
    first_gain,
    first_shift,
    second_gain,
    second_shift,
    cotangent,
):
    seq_count, block, width = inputs.shape
    tensor_size = lax.axis_size("tensor")
    seq_len = block * tensor_size
    place = lax.axis_index("tensor")
    head_dims = w_query.shape[1]
    head_size = width // HEADS
    hidden = w_up.shape[1]
    seqs = range(seq_count)
    row = lambda vector: vector.reshape(1, -1)

    x_own = [inputs[s] for s in seqs]
    x_across = [swap_tensor(x_own[s], ACROSS) for s in seqs]

    dp_place = lax.axis_index("dp").astype(jnp.int32).reshape(1)
    att_far = gather_far(pack([w_query, w_key, w_value, w_out.T], "pack_attention"))
    att_pieces = att_far + gather_near(att_far)
    ffw_far = gather_far(pack([w_up, w_down.T], "pack_feed", [p for p, _ in att_far[1:2]]))
    ffw_near = gather_near(ffw_far)
    ffw_pieces = ffw_far + ffw_near
    started = [p for p, _ in ffw_far[1:2]] + x_across
    att_mine = assemble(att_pieces, dp_place, "assemble_attention", started)
    att_other = assemble(
        other_core(att_pieces), dp_place, "assemble_attention_other", [p for p, _ in ffw_far[2:3]]
    )
    ffw_mine = assemble(ffw_pieces, dp_place, "assemble_feed")
    ffw_other = assemble(other_core(ffw_pieces), dp_place, "assemble_feed_other")
    project_waits = [[], [p for p, _ in ffw_near[:1]]]
    waits = [[p for p, _ in ffw_far[3:]], [p for p, _ in ffw_near[1:2]]]

    biases = jnp.concatenate([b_query, jnp.zeros_like(b_query), b_value, b_up])
    biases_other = swap_tensor(biases, CORE)
    qkv_bias_mine, up_bias_mine = row(biases[: 3 * head_dims]), row(biases[3 * head_dims :])
    qkv_bias_other = row(biases_other[: 3 * head_dims])
    up_bias_other = row(biases_other[3 * head_dims :])
    b_out_row, b_down_row = row(b_out), row(b_down)
    gain_one, shift_one = row(first_gain), row(first_shift)
    gain_two, shift_two = row(second_gain), row(second_shift)

    order = jnp.stack([place, place ^ ACROSS, place ^ CORE, place ^ CORE ^ ACROSS])
    positions = (order[:, None] * block + jnp.arange(block, dtype=jnp.int32)[None, :]).reshape(-1)
    masks = [jnp.where(positions < lengths[s], 0.0, MASKED).astype(F32) for s in seqs]

    projected = [
        project_inputs(
            x_own[s], x_across[s], att_mine, att_other, qkv_bias_mine, qkv_bias_other,
            project_waits[s] if s < 2 else [],
        )
        for s in seqs
    ]
    far = [swap_tensor(projected[s][2], CORE) for s in seqs]
    attended = [
        attention_forward(
            projected[s][0], projected[s][1], far[s], masks[s].reshape(1, seq_len),
            att_mine, att_other, head_size, waits[s] if s < 2 else [],
        )
        for s in seqs
    ]
    attended_got = [swap_tensor(attended[s][3], ACROSS) for s in seqs]
    one = [
        first_norm(x_own[s], attended[s][2], attended_got[s], b_out_row, gain_one, shift_one)
        for s in seqs
    ]
    normed_across = [swap_tensor(one[s][2], ACROSS) for s in seqs]
    fed = [
        feed_forward(
            one[s][2], normed_across[s], ffw_mine, ffw_other, up_bias_mine, up_bias_other,
        )
        for s in seqs
    ]
    branch_got = [swap_tensor(fed[s][5], ACROSS) for s in seqs]
    two = [
        second_norm(
            one[s][1], fed[s][4], branch_got[s], cotangent[s], b_down_row, gain_two, shift_two
        )
        for s in seqs
    ]
    grad_across = [swap_tensor(two[s][2], ACROSS) for s in seqs]
    fed_back = [
        feed_forward_back(
            two[s][2], grad_across[s], ffw_mine, ffw_other, fed[s][2], fed[s][3]
        )
        for s in seqs
    ]
    back_got = [swap_tensor(fed_back[s][3], ACROSS) for s in seqs]
    def placed_in(part_mine, part_other):
        size = part_mine.shape[0]
        empty = jnp.zeros((tensor_size * size,), F32)
        empty = lax.dynamic_update_slice(empty, part_mine, (place * size,))
        return lax.dynamic_update_slice(empty, part_other, ((place ^ CORE) * size,))

    levels = range(lax.axis_size("dp").bit_length() - 1)
    near_first = list(levels)
    far_first = [1, 0, *levels[2:]] if len(near_first) > 1 else near_first

    def pairs(own, across):
        return [part for s in seqs for part in (own[s], across[s])]

    def norm_back(s, deps):
        return first_norm_back(
            one[s][0], two[s][1], fed_back[s][2], back_got[s], gain_one, deps
        )

    down_made = weight_grad(
        pairs([two[s][2] for s in seqs], grad_across),
        [fed[s][0] for s in seqs], [fed[s][1] for s in seqs],
        dp_place, near_first, hidden, "w_down_grad", deps=[fed_back[-1][2]],
    )
    one_back = [norm_back(s, [down_made[1]]) for s in seqs]
    up_made = weight_grad(
        pairs([one[s][2] for s in seqs], normed_across),
        [fed_back[s][0] for s in seqs], [fed_back[s][1] for s in seqs],
        dp_place, far_first, hidden, "w_up_grad", deps=[one_back[s][1] for s in seqs],
    )
    first_across = [swap_tensor(one_back[s][1], ACROSS) for s in seqs]
    down_grad, down_came = reduced(down_made, near_first)
    up_grad, up_came = reduced(up_made, far_first)

    def backward(s, deps):
        return attention_backward(
            projected[s][0], projected[s][1], far[s], masks[s].reshape(seq_len, 1),
            one_back[s][1], first_across[s], att_mine, att_other, head_size, deps,
        )

    attended_back = [backward(0, [down_came[0], up_made[1]])]
    out_grad, out_came = reduced(
        weight_grad(
            pairs([one_back[s][1] for s in seqs], first_across),
            [attended[s][0] for s in seqs], [attended[s][1] for s in seqs],
            dp_place, near_first, head_dims, "w_out_grad", deps=[attended_back[0][3]],
        ),
        near_first,
    )

    attended_back += [backward(s, [down_came[1], up_came[1], out_came[0]]) for s in seqs[1:]]
    far_back = [swap_tensor(attended_back[s][2], CORE) for s in seqs]
    back = [
        project_back(
            attended_back[s][0], attended_back[s][1], far_back[s], att_mine, att_other,
            [down_came[2], up_came[2], out_came[1]] if s == 0 else [out_came[2]],
        )
        for s in seqs
    ]
    input_got = [swap_tensor(back[s][3], ACROSS) for s in seqs]
    input_grad = jnp.stack(
        [
            (one_back[s][0] + (back[s][2] + input_got[s].astype(F32))).astype(BF16)
            for s in seqs
        ]
    )
    tokens = pairs(x_own, x_across)
    grad_queries = [attended_back[s][0] for s in seqs]
    query_grad, _ = reduced(
        weight_grad(
            tokens, grad_queries, grad_queries, dp_place, far_first, head_dims, "w_query_grad",
            head_dims, [far_back[0]],
        ),
        far_first,
    )
    both_grad, _ = reduced(
        weight_grad(
            tokens, [back[s][0] for s in seqs], [back[s][1] for s in seqs],
            dp_place, near_first, 2 * head_dims, "w_key_value_grad",
        ),
        near_first,
    )

    sums = sum(attended_back[s][3] for s in seqs)
    small = sum_all(
        jnp.concatenate(
            [
                sum(two[s][3] for s in seqs).reshape(-1),
                sum(one_back[s][2] for s in seqs).reshape(-1),
                placed_in(
                    sum(fed_back[s][4] for s in seqs).reshape(-1),
                    sum(fed_back[s][5] for s in seqs).reshape(-1),
                ),
                placed_in(sums[0, :head_dims], sums[1, :head_dims]),
                placed_in(sums[0, head_dims:], sums[1, head_dims:]),
            ]
        )
    )
    vectors = [small[i * width : (i + 1) * width] for i in range(6)]
    second_gain_grad, second_shift_grad, b_down_grad = vectors[:3]
    first_gain_grad, first_shift_grad, b_out_grad = vectors[3:]
    b_up_grad = small[6 * width : 6 * width + tensor_size * hidden]
    b_query_grad, b_value_grad = small[-2 * width : -width], small[-width:]

    output = jnp.stack([two[s][0] for s in seqs])
    return (
        output,
        input_grad,
        query_grad,
        both_grad[:, :head_dims],
        both_grad[:, head_dims:],
        out_grad.T,
        up_grad,
        down_grad.T,
        b_query_grad,
        b_value_grad,
        b_out_grad,
        b_up_grad,
        b_down_grad,
        first_gain_grad,
        first_shift_grad,
        second_gain_grad,
        second_shift_grad,
    )


def solution(mesh):
    placed = (
        P("dp", "tensor", None),
        P("dp"),
        P("dp", "tensor"),
        P("dp", "tensor"),
        P("dp", "tensor"),
        P("tensor", "dp"),
        P("dp", "tensor"),
        P("tensor", "dp"),
        P("tensor"),
        P("tensor"),
        P(),
        P("tensor"),
        P(),
        P(),
        P(),
        P(),
        P(),
        P("dp", "tensor", None),
    )
    return jax.shard_map(
        shards,
        mesh=mesh,
        in_specs=placed,
        out_specs=(
            P("dp", "tensor", None),
            P("dp", "tensor", None),
            P("dp", "tensor"),
            P("dp", "tensor"),
            P("dp", "tensor"),
            P("tensor", "dp"),
            P("dp", "tensor"),
            P("tensor", "dp"),
            P(),
            P(),
            P(),
            P(),
            P(),
            P(),
            P(),
            P(),
            P(),
        ),
        check_vma=False,
    )
```

```python
import math

import jax
import jax.numpy as jnp
from jax import lax
from jax.experimental import pallas as pl
from jax.experimental.pallas import tpu as pltpu
from jax.sharding import PartitionSpec as P

HEADS = 16
NORM_EPS = 1e-12
MASKED = -1000000000.0
MIB = 1024 * 1024
VMEM_LIMIT = 56 * MIB
SMALL_LIMIT = 16 * MIB
UNDERSTATED = 1000

F32 = jnp.float32
BF16 = jnp.bfloat16

CORE = 1
ACROSS = 2


def dot(one, two):
    return lax.dot_general(one, two, (((1,), (0,)), ((), ())), preferred_element_type=F32)


def dot_nt(one, two):
    return lax.dot_general(one, two, (((1,), (1,)), ((), ())), preferred_element_type=F32)


def shape(dims, kind):
    return jax.ShapeDtypeStruct(dims, kind)


def after(kernel, count, deps):
    def body(*refs):
        kernel(*refs[:count], *refs[count + len(deps) :])

    return body


def whole_call(kernel, outs, args, flops, name, scratch=(), deps=(), limit=VMEM_LIMIT):
    moved = sum(math.prod(a.shape) * a.dtype.itemsize for a in (*args, *outs))
    return pl.pallas_call(
        after(kernel, len(args), deps),
        out_shape=tuple(outs),
        in_specs=[pl.BlockSpec(memory_space=pltpu.VMEM)] * len(args)
        + [pl.BlockSpec(memory_space=pl.ANY)] * len(deps),
        out_specs=tuple([pl.BlockSpec(memory_space=pltpu.VMEM)] * len(outs)),
        scratch_shapes=list(scratch),
        compiler_params=pltpu.CompilerParams(vmem_limit_bytes=limit),
        cost_estimate=pl.CostEstimate(
            flops=flops // UNDERSTATED, bytes_accessed=moved // UNDERSTATED, transcendentals=0
        ),
        name=name,
    )(*args, *deps)


def streamed_call(kernel, grid, outs, out_specs, args, in_specs, flops, name, scratch, deps=()):
    moved = sum(math.prod(a.shape) * a.dtype.itemsize for a in (*args, *outs))
    return pl.pallas_call(
        after(kernel, len(args), deps),
        grid=grid,
        out_shape=tuple(outs),
        in_specs=list(in_specs) + [pl.BlockSpec(memory_space=pl.ANY)] * len(deps),
        out_specs=tuple(out_specs),
        scratch_shapes=list(scratch),
        compiler_params=pltpu.CompilerParams(
            vmem_limit_bytes=VMEM_LIMIT, dimension_semantics=("arbitrary",)
        ),
        cost_estimate=pl.CostEstimate(
            flops=flops // UNDERSTATED, bytes_accessed=moved // UNDERSTATED, transcendentals=0
        ),
        name=name,
    )(*args, *deps)


def const_spec(dims):
    return pl.BlockSpec(dims, lambda i: (0,) * len(dims))


def swap_tensor(array, bit):
    size = lax.axis_size("tensor")
    return lax.ppermute(array, "tensor", [(i, i ^ bit) for i in range(size)])


def swap_dp(array, bit):
    size = lax.axis_size("dp")
    return lax.ppermute(array, "dp", [(i, i ^ bit) for i in range(size)])


def pack(parts, name, deps=()):
    def kernel(*refs):
        at = 0
        for ref in refs[:-1]:
            refs[-1][:, at : at + ref.shape[1]] = ref[...]
            at += ref.shape[1]

    out = shape((parts[0].shape[0], sum(p.shape[1] for p in parts)), parts[0].dtype)
    return whole_call(kernel, [out], parts, 0, name, deps=deps)[0]


def gather_far(rows):
    pieces = [(rows, [0])]
    step = lax.axis_size("dp") // 2
    while step > 1:
        if len(pieces) > 2:
            pieces = [merged(pieces)]
        pieces += [(swap_dp(p, step), [o ^ step for o in offsets]) for p, offsets in pieces]
        step //= 2
    return pieces


def merged(pieces):
    return (
        jnp.concatenate([p for p, _ in pieces], axis=0),
        [o for _, offsets in pieces for o in offsets],
    )


def gather_near(pieces):
    return [(swap_dp(p, 1), [o ^ 1 for o in offsets]) for p, offsets in pieces]


def other_core(pieces):
    return [(swap_tensor(p, CORE), offsets) for p, offsets in pieces]


def assemble(pieces, dp_place, name, deps=()):
    rows = pieces[0][0].shape[0] // len(pieces[0][1])
    width = pieces[0][0].shape[1]
    size = lax.axis_size("dp")

    def kernel(*refs):
        place = refs[0][0]
        for ref, (_, offsets) in zip(refs[1:-1], pieces):
            for i, offset in enumerate(offsets):
                start = pl.multiple_of((place ^ offset) * rows, rows)
                refs[-1][pl.ds(start, rows), :] = ref[i * rows : (i + 1) * rows, :]

    arrays = [p for p, _ in pieces]
    out = shape((size * rows, width), BF16)
    moved = 2 * size * rows * width * 2
    return pl.pallas_call(
        after(kernel, 1 + len(arrays), deps),
        out_shape=out,
        in_specs=[pl.BlockSpec(memory_space=pltpu.SMEM)]
        + [pl.BlockSpec(memory_space=pltpu.VMEM)] * len(arrays)
        + [pl.BlockSpec(memory_space=pl.ANY)] * len(deps),
        out_specs=pl.BlockSpec(memory_space=pltpu.VMEM),
        compiler_params=pltpu.CompilerParams(vmem_limit_bytes=VMEM_LIMIT),
        cost_estimate=pl.CostEstimate(
            flops=0, bytes_accessed=moved // UNDERSTATED, transcendentals=0
        ),
        name=name,
    )(dp_place, *arrays, *deps)


def halving_order(size, bits):
    order = [0]
    for bit in reversed(bits):
        order = order + [o ^ (1 << bit) for o in order]
    return order


def scatter_dp(total, bits):
    arrivals = []
    for bit in bits:
        half = total.shape[0] // 2
        came = swap_dp(total[half:].astype(BF16), 1 << bit)
        arrivals.append(came)
        total = total[:half] + came.astype(F32)
    return total, arrivals


def sum_all(vector):
    step = 1
    while step < lax.axis_size("tensor"):
        vector = vector + swap_tensor(vector, step)
        step *= 2
    step = 1
    while step < lax.axis_size("dp"):
        vector = vector + swap_dp(vector, step)
        step *= 2
    return vector


def project_inputs(x_own, x_across, w_mine, w_other, b_mine, b_other, deps):
    rows, width = x_own.shape
    third = w_mine.shape[1] // 4

    def kernel(x0, x1, wm, wo, bm, bo, mine_ref, other_ref, send_ref):
        tokens = jnp.concatenate([x0[...], x1[...]], axis=0)
        mine = (dot(tokens, wm[:, : 3 * third]) + bm[...]).astype(BF16)
        other = (dot(tokens, wo[:, : 3 * third]) + bo[...]).astype(BF16)
        mine_ref[...] = mine
        other_ref[...] = other
        send_ref[:, : 2 * third] = other[:, third:]
        send_ref[:, 2 * third :] = mine[:, third:]

    outs = [
        shape((2 * rows, 3 * third), BF16),
        shape((2 * rows, 3 * third), BF16),
        shape((2 * rows, 4 * third), BF16),
    ]
    flops = 2 * 2 * rows * width * 6 * third
    return whole_call(
        kernel,
        outs,
        [x_own, x_across, w_mine, w_other, b_mine, b_other],
        flops,
        "project_inputs",
        deps=deps,
    )


def attention_forward(mine, other, far, bias_row, w_mine, w_other, head_size, deps):
    rows = mine.shape[0]
    third = mine.shape[1] // 3
    heads = third // head_size
    block = rows // 2
    width = w_mine.shape[0]
    scaling = 1.0 / math.sqrt(head_size)

    def kernel(mine_ref, other_ref, far_ref, bias_ref, wm, wo, cm_ref, co_ref, own_ref, across_ref, acc):
        lane_head = lax.broadcasted_iota(jnp.int32, (1, third), 1) // head_size
        acc[...] = jnp.zeros_like(acc)
        bias = bias_ref[...]

        def one_head(head, carry):
            inside = lane_head == head
            for group, ref in enumerate((mine_ref, other_ref)):
                base = 2 * third * group
                keys = jnp.concatenate(
                    [ref[:, third : 2 * third], far_ref[:, base : base + third]], axis=0
                )
                vals = jnp.concatenate(
                    [ref[:, 2 * third :], far_ref[:, base + third : base + 2 * third]], axis=0
                )
                for part in range(2):
                    span = slice(part * block, (part + 1) * block)
                    query = jnp.where(inside, ref[span, :third] * scaling, 0.0).astype(BF16)
                    scores = dot_nt(query, keys) + bias
                    peak = jnp.max(scores, axis=-1, keepdims=True)
                    weights = jnp.exp(scores - peak)
                    total = jnp.sum(weights, axis=-1, keepdims=True)
                    found = dot(weights.astype(BF16), vals) * (1.0 / total)
                    acc[group, span, :] += jnp.where(inside, found, 0.0)
            return carry

        lax.fori_loop(0, heads, one_head, 0)
        ctx_mine = acc[0].astype(BF16)
        ctx_other = acc[1].astype(BF16)
        cm_ref[...] = ctx_mine
        co_ref[...] = ctx_other
        part_sum = dot_nt(ctx_mine, wm[:, 3 * third :]) + dot_nt(ctx_other, wo[:, 3 * third :])
        own_ref[...] = part_sum[:block]
        across_ref[...] = part_sum[block:].astype(BF16)

    outs = [
        shape((rows, third), BF16),
        shape((rows, third), BF16),
        shape((block, width), F32),
        shape((block, width), BF16),
    ]
    flops = 2 * 2 * 2 * rows * 2 * rows * third * heads * 2
    return whole_call(
        kernel,
        outs,
        [mine, other, far, bias_row, w_mine, w_other],
        flops,
        "attention_forward",
        [pltpu.VMEM((2, rows, third), F32)],
        deps,
    )


def attention_backward(mine, other, far, bias_column, ga_own, ga_across, w_mine, w_other, head_size, deps):
    rows = mine.shape[0]
    third = mine.shape[1] // 3
    heads = third // head_size
    block = rows // 2
    keys_count = 2 * rows
    scaling = 1.0 / math.sqrt(head_size)

    def kernel(
        mine_ref, other_ref, far_ref, bias_ref, g0, g1, wm, wo,
        dq_ref, keep_ref, send_ref, sums_ref, grad_ctx, keys_t, dq_t, dkv,
    ):
        lane_head = lax.broadcasted_iota(jnp.int32, (1, third), 1) // head_size
        grad_rows = jnp.concatenate([g0[...], g1[...]], axis=0)
        grad_ctx[0] = dot(grad_rows, wm[:, 3 * third :]).astype(BF16)
        grad_ctx[1] = dot(grad_rows, wo[:, 3 * third :]).astype(BF16)
        dkv[...] = jnp.zeros_like(dkv)
        for group, ref in enumerate((mine_ref, other_ref)):
            base = 2 * third * group
            keys_t[group, :, :rows] = ref[:, third : 2 * third].T
            keys_t[group, :, rows:] = far_ref[:, base : base + third].T
        bias = bias_ref[...]

        def one_head(head, carry):
            inside = lane_head == head
            start = pl.multiple_of(head * head_size, head_size)
            for group, ref in enumerate((mine_ref, other_ref)):
                base = 2 * third * group
                keys = jnp.concatenate(
                    [ref[:, third : 2 * third], far_ref[:, base : base + third]], axis=0
                )
                vals = jnp.concatenate(
                    [ref[:, 2 * third :], far_ref[:, base + third : base + 2 * third]], axis=0
                )
                head_keys_t = keys_t[group, pl.ds(start, head_size), :]
                for part in range(2):
                    span = slice(part * block, (part + 1) * block)
                    query = jnp.where(inside, ref[span, :third] * scaling, 0.0).astype(BF16)
                    grad = jnp.where(inside, grad_ctx[group, span, :], 0.0).astype(BF16)
                    scores = dot_nt(keys, query) + bias
                    peak = jnp.max(scores, axis=0, keepdims=True)
                    weights = jnp.exp(scores - peak)
                    total = jnp.sum(weights, axis=0, keepdims=True)
                    probs = weights * (1.0 / total)
                    grad_probs = dot_nt(vals, grad)
                    inner = jnp.sum(probs * grad_probs, axis=0, keepdims=True)
                    grad_scores = (probs * (grad_probs - inner)).astype(BF16)
                    dkv[group, 1] += dot(probs.astype(BF16), grad)
                    dkv[group, 0] += dot(grad_scores, query)
                    dq_t[group, pl.ds(start, head_size), span] = dot(head_keys_t, grad_scores)
            return carry

        lax.fori_loop(0, heads, one_head, 0)
        for group in range(2):
            grad_query = (dq_t[group].T * scaling).astype(BF16)
            dq_ref[:, group * third : (group + 1) * third] = grad_query
            sums_ref[group : group + 1, :third] = jnp.sum(
                grad_query.astype(F32), axis=0, keepdims=True
            )
            sums_ref[group : group + 1, third:] = jnp.sum(dkv[group, 1], axis=0, keepdims=True)
            for kind in range(2):
                at = (2 * group + kind) * third
                keep_ref[:, at : at + third] = dkv[group, kind, :rows]
                away = (2 * (1 - group) + kind) * third
                send_ref[:, away : away + third] = dkv[group, kind, rows:].astype(BF16)

    outs = [
        shape((rows, 2 * third), BF16),
        shape((rows, 4 * third), F32),
        shape((rows, 4 * third), BF16),
        shape((2, 2 * third), F32),
    ]
    flops = 5 * 2 * 2 * rows * keys_count * third * heads
    return whole_call(
        kernel,
        outs,
        [mine, other, far, bias_column, ga_own, ga_across, w_mine, w_other],
        flops,
        "attention_backward",
        [
            pltpu.VMEM((2, rows, third), BF16),
            pltpu.VMEM((2, third, keys_count), BF16),
            pltpu.VMEM((2, third, rows), F32),
            pltpu.VMEM((2, 2, keys_count, third), F32),
        ],
        deps,
    )


def project_back(dq, keep, got, w_mine, w_other, deps):
    rows = dq.shape[0]
    third = dq.shape[1] // 2
    block = rows // 2
    width = w_mine.shape[0]

    def kernel(dq_ref, keep_ref, got_ref, wm, wo, gm_ref, go_ref, own_ref, across_ref):
        dkv = (keep_ref[...] + got_ref[...].astype(F32)).astype(BF16)
        grad_mine = jnp.concatenate([dq_ref[:, :third], dkv[:, : 2 * third]], axis=1)
        grad_other = jnp.concatenate([dq_ref[:, third:], dkv[:, 2 * third :]], axis=1)
        gm_ref[...] = dkv[:, : 2 * third]
        go_ref[...] = dkv[:, 2 * third :]
        back = dot_nt(grad_mine, wm[:, : 3 * third]) + dot_nt(grad_other, wo[:, : 3 * third])
        own_ref[...] = back[:block]
        across_ref[...] = back[block:].astype(BF16)

    outs = [
        shape((rows, 2 * third), BF16),
        shape((rows, 2 * third), BF16),
        shape((block, width), F32),
        shape((block, width), BF16),
    ]
    flops = 2 * rows * width * 6 * third
    return whole_call(
        kernel, outs, [dq, keep, got, w_mine, w_other], flops, "project_back", deps=deps
    )


def moments(summed):
    centre = jnp.mean(summed, axis=-1, keepdims=True)
    centred = summed - centre
    spread = jnp.mean(centred * centred, axis=-1, keepdims=True)
    back = lax.rsqrt(spread + NORM_EPS)
    return centred * back, back


def first_norm(x_own, part, got, b_out, gain, shift, deps):
    dims = x_own.shape

    def kernel(x_ref, p_ref, r_ref, b_ref, g_ref, s_ref, summed_ref, normed_ref, low_ref):
        summed = x_ref[...].astype(F32) + (p_ref[...] + r_ref[...].astype(F32)) + b_ref[...]
        unit, _ = moments(summed)
        normed = unit * g_ref[...] + s_ref[...]
        summed_ref[...] = summed
        normed_ref[...] = normed
        low_ref[...] = normed.astype(BF16)

    outs = [shape(dims, F32), shape(dims, F32), shape(dims, BF16)]
    return whole_call(
        kernel,
        outs,
        [x_own, part, got, b_out, gain, shift],
        20 * math.prod(dims),
        "first_norm",
        deps=deps,
        limit=SMALL_LIMIT,
    )


def second_norm(normed, part, got, cotangent, b_down, gain, shift):
    dims = normed.shape

    def kernel(n_ref, p_ref, r_ref, c_ref, b_ref, g_ref, s_ref, out_ref, grad_ref, low_ref, sums_ref):
        summed = n_ref[...] + (p_ref[...] + r_ref[...].astype(F32)) + b_ref[...]
        unit, back = moments(summed)
        out_ref[...] = (unit * g_ref[...] + s_ref[...]).astype(BF16)
        cot = c_ref[...].astype(F32)
        scaled = cot * g_ref[...]
        grad = back * (
            scaled
            - jnp.mean(scaled, axis=-1, keepdims=True)
            - unit * jnp.mean(scaled * unit, axis=-1, keepdims=True)
        )
        grad_ref[...] = grad
        low_ref[...] = grad.astype(BF16)
        sums_ref[0:1, :] = jnp.sum(cot * unit, axis=0, keepdims=True)
        sums_ref[1:2, :] = jnp.sum(cot, axis=0, keepdims=True)
        sums_ref[2:3, :] = jnp.sum(grad, axis=0, keepdims=True)

    outs = [shape(dims, BF16), shape(dims, F32), shape(dims, BF16), shape((3, dims[1]), F32)]
    return whole_call(
        kernel,
        outs,
        [normed, part, got, cotangent, b_down, gain, shift],
        40 * math.prod(dims),
        "second_norm",
        limit=SMALL_LIMIT,
    )


def first_norm_back(summed, grad_second, part, got, gain, deps):
    dims = summed.shape

    def kernel(z_ref, gs_ref, p_ref, r_ref, g_ref, grad_ref, low_ref, sums_ref):
        unit, back = moments(z_ref[...])
        grad_normed = gs_ref[...] + (p_ref[...] + r_ref[...].astype(F32))
        scaled = grad_normed * g_ref[...]
        grad = back * (
            scaled
            - jnp.mean(scaled, axis=-1, keepdims=True)
            - unit * jnp.mean(scaled * unit, axis=-1, keepdims=True)
        )
        grad_ref[...] = grad
        low_ref[...] = grad.astype(BF16)
        sums_ref[0:1, :] = jnp.sum(grad_normed * unit, axis=0, keepdims=True)
        sums_ref[1:2, :] = jnp.sum(grad_normed, axis=0, keepdims=True)
        sums_ref[2:3, :] = jnp.sum(grad, axis=0, keepdims=True)

    outs = [shape(dims, F32), shape(dims, BF16), shape((3, dims[1]), F32)]
    return whole_call(
        kernel,
        outs,
        [summed, grad_second, part, got, gain],
        40 * math.prod(dims),
        "first_norm_back",
        deps=deps,
        limit=SMALL_LIMIT,
    )


def feed_forward(n_own, n_far, weights, bias, prior, deps):
    block, width = n_own.shape
    rows = 2 * block
    hidden = weights.shape[1] // 2
    tile = min(256, hidden)
    steps = hidden // tile
    last = prior is not None

    def kernel(n0, n1, u, d, b, *refs):
        step = pl.program_id(0)
        if last:
            before, a_ref, s_ref, own_ref, far_ref, tokens, acc = refs
        else:
            a_ref, s_ref, acc, tokens = refs

        @pl.when(step == 0)
        def _():
            tokens[:block] = n0[...]
            tokens[block:] = n1[...]
            acc[...] = before[...] if last else jnp.zeros_like(acc)

        hid = dot(tokens[...], u[...]) + b[...]
        half = 0.5 * (1.0 + lax.erf(hid * (1.0 / math.sqrt(2.0))))
        bell = jnp.exp(hid * hid * -0.5) * (1.0 / math.sqrt(2.0 * math.pi))
        active = (hid * half).astype(BF16)
        a_ref[...] = active
        s_ref[...] = (half + hid * bell).astype(BF16)
        acc[...] += dot_nt(active, d[...])

        if last:

            @pl.when(step == steps - 1)
            def _():
                own_ref[...] = acc[:block]
                far_ref[...] = acc[block:].astype(BF16)

    column = pl.BlockSpec((width, tile), lambda i: (0, i))
    later = pl.BlockSpec((width, tile), lambda i: (0, steps + i))
    made = pl.BlockSpec((rows, tile), lambda i: (0, i))
    args = [n_own, n_far, weights, weights, bias]
    in_specs = [const_spec((block, width))] * 2
    in_specs += [column, later, pl.BlockSpec((1, tile), lambda i: (0, i))]
    outs = [shape((rows, hidden), BF16)] * 2
    scratch = [pltpu.VMEM((rows, width), BF16)]
    if last:
        args.append(prior)
        in_specs.append(const_spec((rows, width)))
        outs += [shape((block, width), F32), shape((block, width), BF16)]
        out_specs = [made] * 2 + [const_spec((block, width))] * 2
        scratch.append(pltpu.VMEM((rows, width), F32))
    else:
        outs.append(shape((rows, width), F32))
        out_specs = [made] * 2 + [const_spec((rows, width))]
    return streamed_call(
        kernel,
        (steps,),
        outs,
        out_specs,
        args,
        in_specs,
        2 * 2 * rows * width * hidden,
        "feed_forward",
        scratch,
        deps,
    )


def feed_forward_back(g_own, g_across, w_mine, w_other, slope_mine, slope_other):
    block, width = g_own.shape
    rows = 2 * block
    hidden = w_mine.shape[1] // 2
    tile = min(256, hidden)
    steps = hidden // tile

    def kernel(
        g0, g1, um, uo, dm, do, sm, so,
        gm_ref, go_ref, own_ref, across_ref, bm_ref, bo_ref, grads, acc,
    ):
        step = pl.program_id(0)

        @pl.when(step == 0)
        def _():
            grads[:block] = g0[...]
            grads[block:] = g1[...]
            acc[...] = jnp.zeros_like(acc)

        total = acc[...]
        for u, d, s, g_ref, b_ref in ((um, dm, sm, gm_ref, bm_ref), (uo, do, so, go_ref, bo_ref)):
            grad_hidden = (dot(grads[...], d[...]) * s[...].astype(F32)).astype(BF16)
            g_ref[...] = grad_hidden
            b_ref[...] = jnp.sum(grad_hidden.astype(F32), axis=0, keepdims=True)
            total = total + dot_nt(grad_hidden, u[...])
        acc[...] = total

        @pl.when(step == steps - 1)
        def _():
            own_ref[...] = acc[:block]
            across_ref[...] = acc[block:].astype(BF16)

    column = pl.BlockSpec((width, tile), lambda i: (0, i))
    later = pl.BlockSpec((width, tile), lambda i: (0, steps + i))
    bias = pl.BlockSpec((1, tile), lambda i: (0, i))
    made = pl.BlockSpec((rows, tile), lambda i: (0, i))
    outs = (
        [shape((rows, hidden), BF16)] * 2
        + [shape((block, width), F32), shape((block, width), BF16)]
        + [shape((1, hidden), F32)] * 2
    )
    return streamed_call(
        kernel,
        (steps,),
        outs,
        [made] * 2 + [const_spec((block, width))] * 2 + [bias] * 2,
        [g_own, g_across, w_mine, w_other, w_mine, w_other, slope_mine, slope_other],
        [const_spec((block, width))] * 2 + [column] * 2 + [later] * 2 + [made] * 2,
        2 * 2 * rows * width * 2 * hidden,
        "feed_forward_back",
        [pltpu.VMEM((rows, width), BF16), pltpu.VMEM((rows, width), F32)],
    )


def weight_grad(
    ones, mine, other, dp_place, bits, count, name, other_first=0, deps=(), other_kind=BF16
):
    block, width = ones[0].shape
    rows = 2 * block
    tile = min(256, count)
    size = lax.axis_size("dp")
    share = width // size
    order = halving_order(size, bits)

    def kernel(place_ref, a0, a1, a2, a3, m0, m1, o0, o1, mine_ref, other_ref, turned, full):
        @pl.when(pl.program_id(0) == 0)
        def _():
            for i, ref in enumerate((a0, a1, a2, a3)):
                turned[:, i * block : (i + 1) * block] = ref[...].T

        place = place_ref[0]
        for one, two, out_ref in ((m0, m1, mine_ref), (o0, o1, other_ref)):
            full[...] = dot(turned[:, :rows], one[...]) + dot(turned[:, rows:], two[...])
            for i, offset in enumerate(order):
                start = pl.multiple_of((place ^ offset) * share, share)
                out_ref[i * share : (i + 1) * share, :] = full[pl.ds(start, share), :].astype(
                    out_ref.dtype
                )

    base = other_first // tile
    column = pl.BlockSpec((rows, tile), lambda i: (0, i))
    other_column = pl.BlockSpec((rows, tile), lambda i: (0, base + i))
    made = pl.BlockSpec((width, tile), lambda i: (0, i))
    return streamed_call(
        kernel,
        (count // tile,),
        [shape((width, count), F32), shape((width, count), other_kind)],
        [made] * 2,
        [dp_place, *ones, *mine, *other],
        [pl.BlockSpec(memory_space=pltpu.SMEM)] + [const_spec((block, width))] * 4 + [column] * 2 + [other_column] * 2,
        2 * 2 * rows * width * 2 * count,
        name,
        [pltpu.VMEM((width, 2 * rows), BF16), pltpu.VMEM((width, tile), F32)],
        deps,
    )


def add_up(parts, deps):
    def kernel(*refs):
        refs[-1][...] = sum(ref[...] for ref in refs[:-1])

    out = shape(parts[0].shape, F32)
    return whole_call(kernel, [out], parts, 0, "add_up", deps=deps, limit=SMALL_LIMIT)[0]


def reduced(made, bits):
    got = swap_tensor(made[1], CORE)
    total, arrivals = scatter_dp(made[0] + got.astype(F32), bits)
    return total, [got, *arrivals]


def reduced_across(made, bits):
    mine, mine_came = scatter_dp(made[0], bits)
    other, other_came = scatter_dp(made[1], bits)
    total = mine + swap_tensor(other.astype(BF16), ACROSS).astype(F32)
    return total, mine_came, other_came


def shards(
    inputs,
    lengths,
    w_query,
    w_key,
    w_value,
    w_out,
    w_up,
    w_down,
    b_query,
    b_value,
    b_out,
    b_up,
    b_down,
    first_gain,
    first_shift,
    second_gain,
    second_shift,
    cotangent,
):
    seq_count, block, width = inputs.shape
    tensor_size = lax.axis_size("tensor")
    seq_len = block * tensor_size
    place = lax.axis_index("tensor")
    head_dims = w_query.shape[1]
    head_size = width // HEADS
    hidden = w_up.shape[1]
    seqs = range(seq_count)
    row = lambda vector: vector.reshape(1, -1)

    x_own = [inputs[s] for s in seqs]
    x_across = [swap_tensor(x_own[s], ACROSS) for s in seqs]

    dp_place = lax.axis_index("dp").astype(jnp.int32).reshape(1)
    att_far = gather_far(pack([w_query, w_key, w_value, w_out.T], "pack_attention"))
    att_pieces = att_far + gather_near(att_far)
    share = pack([w_up, w_down.T], "pack_feed", [p for p, _ in att_far[1:2]])
    share_other = swap_tensor(share, ACROSS)
    mine_far = gather_far(share)
    mine_near = gather_near(mine_far)
    other_far = gather_far(share_other)
    other_near = gather_near(other_far)

    def arrays(pieces):
        return [p for p, _ in pieces]

    att_mine = assemble(att_pieces, dp_place, "assemble_attention", arrays(mine_far[1:2]))
    att_other = assemble(
        other_core(att_pieces), dp_place, "assemble_attention_other",
        x_across + arrays(mine_far[2:3]),
    )
    project_waits = [[], arrays(mine_far[3:] + mine_near[:1])]
    attend_waits = [
        arrays(mine_near[1:2] + other_far[1:2]),
        arrays(mine_near[2:3] + other_far[2:3]),
    ]
    norm_waits = [arrays(mine_near[3:] + other_far[3:]), arrays(other_near[:1])]
    ffw_mine = assemble(mine_far + mine_near, dp_place, "assemble_feed")

    biases = jnp.concatenate([b_query, jnp.zeros_like(b_query), b_value])
    qkv_bias_mine, qkv_bias_other = row(biases), row(swap_tensor(biases, CORE))
    up_bias_mine, up_bias_other = row(b_up), row(swap_tensor(b_up, ACROSS))
    b_out_row, b_down_row = row(b_out), row(b_down)
    gain_one, shift_one = row(first_gain), row(first_shift)
    gain_two, shift_two = row(second_gain), row(second_shift)

    order = jnp.stack([place, place ^ ACROSS, place ^ CORE, place ^ CORE ^ ACROSS])
    positions = (order[:, None] * block + jnp.arange(block, dtype=jnp.int32)[None, :]).reshape(-1)
    masks = [jnp.where(positions < lengths[s], 0.0, MASKED).astype(F32) for s in seqs]

    projected = [
        project_inputs(
            x_own[s], x_across[s], att_mine, att_other, qkv_bias_mine, qkv_bias_other,
            project_waits[s] if s < 2 else [],
        )
        for s in seqs
    ]
    far = [swap_tensor(projected[s][2], CORE) for s in seqs]
    attended = [
        attention_forward(
            projected[s][0], projected[s][1], far[s], masks[s].reshape(1, seq_len),
            att_mine, att_other, head_size, attend_waits[s] if s < 2 else [],
        )
        for s in seqs
    ]
    attended_got = [swap_tensor(attended[s][3], ACROSS) for s in seqs]
    one = [
        first_norm(
            x_own[s], attended[s][2], attended_got[s], b_out_row, gain_one, shift_one,
            norm_waits[s] if s < 2 else [],
        )
        for s in seqs
    ]
    normed_far = [swap_tensor(one[s][2], CORE) for s in seqs]
    fed_one = [
        feed_forward(one[s][2], normed_far[s], ffw_mine, up_bias_mine, None, []) for s in seqs
    ]
    ffw_other = assemble(
        other_far + other_near, dp_place, "assemble_feed_other", [fed_one[-1][2]]
    )
    fed_two = [
        feed_forward(one[s][2], normed_far[s], ffw_other, up_bias_other, fed_one[s][2], [])
        for s in seqs
    ]
    fed = [(fed_one[s][0], fed_two[s][0], fed_one[s][1], fed_two[s][1], *fed_two[s][2:]) for s in seqs]
    branch_got = [swap_tensor(fed[s][5], CORE) for s in seqs]
    two = [
        second_norm(
            one[s][1], fed[s][4], branch_got[s], cotangent[s], b_down_row, gain_two, shift_two
        )
        for s in seqs
    ]
    grad_far = [swap_tensor(two[s][2], CORE) for s in seqs]
    fed_back = [
        feed_forward_back(
            two[s][2], grad_far[s], ffw_mine, ffw_other, fed[s][2], fed[s][3]
        )
        for s in seqs
    ]
    back_got = [swap_tensor(fed_back[s][3], CORE) for s in seqs]
    def placed_in(part_mine, part_other, bit):
        size = part_mine.shape[0]
        empty = jnp.zeros((tensor_size * size,), F32)
        empty = lax.dynamic_update_slice(empty, part_mine, (place * size,))
        return lax.dynamic_update_slice(empty, part_other, ((place ^ bit) * size,))

    levels = range(lax.axis_size("dp").bit_length() - 1)
    near_first = list(levels)
    far_first = [1, 0, *levels[2:]] if len(near_first) > 1 else near_first

    def pairs(own, across):
        return [part for s in seqs for part in (own[s], across[s])]

    def norm_back(s, deps):
        return first_norm_back(
            one[s][0], two[s][1], fed_back[s][2], back_got[s], gain_one, deps
        )

    down_made = weight_grad(
        pairs([two[s][2] for s in seqs], grad_far),
        [fed[s][0] for s in seqs], [fed[s][1] for s in seqs],
        dp_place, near_first, hidden, "w_down_grad", deps=[fed_back[-1][2]], other_kind=F32,
    )
    one_back = [norm_back(s, [down_made[1]]) for s in seqs]
    up_made = weight_grad(
        pairs([one[s][2] for s in seqs], normed_far),
        [fed_back[s][0] for s in seqs], [fed_back[s][1] for s in seqs],
        dp_place, far_first, hidden, "w_up_grad", deps=[one_back[s][1] for s in seqs], other_kind=F32,
    )
    first_across = [swap_tensor(one_back[s][1], ACROSS) for s in seqs]
    down_grad, down_mine_came, down_other_came = reduced_across(down_made, near_first)
    up_grad, up_mine_came, up_other_came = reduced_across(up_made, far_first)

    def backward(s, deps):
        return attention_backward(
            projected[s][0], projected[s][1], far[s], masks[s].reshape(seq_len, 1),
            one_back[s][1], first_across[s], att_mine, att_other, head_size, deps,
        )

    attended_back = [backward(0, [up_made[1]])]
    out_grad, out_came = reduced(
        weight_grad(
            pairs([one_back[s][1] for s in seqs], first_across),
            [attended[s][0] for s in seqs], [attended[s][1] for s in seqs],
            dp_place, near_first, head_dims, "w_out_grad", deps=[attended_back[0][3]],
        ),
        near_first,
    )

    attended_back += [
        backward(s, [down_mine_came[0], up_mine_came[0], out_came[0]]) for s in seqs[1:]
    ]
    far_back = [swap_tensor(attended_back[s][2], CORE) for s in seqs]
    back = [
        project_back(
            attended_back[s][0], attended_back[s][1], far_back[s], att_mine, att_other,
            [c[-2] for c in (down_mine_came, up_mine_came)] if s == 0 else [],
        )
        for s in seqs
    ]
    input_got = [swap_tensor(back[s][3], ACROSS) for s in seqs]
    input_grad = jnp.stack(
        [
            (one_back[s][0] + (back[s][2] + input_got[s].astype(F32))).astype(BF16)
            for s in seqs
        ]
    )
    tokens = pairs(x_own, x_across)
    grad_queries = [attended_back[s][0] for s in seqs]
    query_made = weight_grad(
        tokens, grad_queries, grad_queries, dp_place, far_first, head_dims, "w_query_grad",
        head_dims, [far_back[0], down_other_came[0], up_other_came[0]],
    )
    query_grad, _ = reduced(query_made, far_first)
    both_grad, _ = reduced(
        weight_grad(
            tokens, [back[s][0] for s in seqs], [back[s][1] for s in seqs],
            dp_place, near_first, 2 * head_dims, "w_key_value_grad",
        ),
        near_first,
    )

    sums = add_up([attended_back[s][3] for s in seqs], [query_made[1]])
    small = sum_all(
        jnp.concatenate(
            [
                sum(two[s][3] for s in seqs).reshape(-1),
                sum(one_back[s][2] for s in seqs).reshape(-1),
                placed_in(
                    sum(fed_back[s][4] for s in seqs).reshape(-1),
                    sum(fed_back[s][5] for s in seqs).reshape(-1),
                    ACROSS,
                ),
                placed_in(sums[0, :head_dims], sums[1, :head_dims], CORE),
                placed_in(sums[0, head_dims:], sums[1, head_dims:], CORE),
            ]
        )
    )
    vectors = [small[i * width : (i + 1) * width] for i in range(6)]
    second_gain_grad, second_shift_grad, b_down_grad = vectors[:3]
    first_gain_grad, first_shift_grad, b_out_grad = vectors[3:]
    b_up_grad = small[6 * width : 6 * width + tensor_size * hidden]
    b_query_grad, b_value_grad = small[-2 * width : -width], small[-width:]

    output = jnp.stack([two[s][0] for s in seqs])
    return (
        output,
        input_grad,
        query_grad,
        both_grad[:, :head_dims],
        both_grad[:, head_dims:],
        out_grad.T,
        up_grad,
        down_grad.T,
        b_query_grad,
        b_value_grad,
        b_out_grad,
        b_up_grad,
        b_down_grad,
        first_gain_grad,
        first_shift_grad,
        second_gain_grad,
        second_shift_grad,
    )


def solution(mesh):
    placed = (
        P("dp", "tensor", None),
        P("dp"),
        P("dp", "tensor"),
        P("dp", "tensor"),
        P("dp", "tensor"),
        P("tensor", "dp"),
        P("dp", "tensor"),
        P("tensor", "dp"),
        P("tensor"),
        P("tensor"),
        P(),
        P("tensor"),
        P(),
        P(),
        P(),
        P(),
        P(),
        P("dp", "tensor", None),
    )
    return jax.shard_map(
        shards,
        mesh=mesh,
        in_specs=placed,
        out_specs=(
            P("dp", "tensor", None),
            P("dp", "tensor", None),
            P("dp", "tensor"),
            P("dp", "tensor"),
            P("dp", "tensor"),
            P("tensor", "dp"),
            P("dp", "tensor"),
            P("tensor", "dp"),
            P(),
            P(),
            P(),
            P(),
            P(),
            P(),
            P(),
            P(),
            P(),
        ),
        check_vma=False,
    )
```

```python
import math

import jax
import jax.numpy as jnp
from jax import lax
from jax.experimental import pallas as pl
from jax.experimental.pallas import tpu as pltpu
from jax.sharding import PartitionSpec as P

HEADS = 16
NORM_EPS = 1e-12
MASKED = -1000000000.0
MIB = 1024 * 1024
VMEM_LIMIT = 56 * MIB
SMALL_LIMIT = 16 * MIB
UNDERSTATED = 1000

F32 = jnp.float32
BF16 = jnp.bfloat16

CORE = 1
ACROSS = 2


def dot(one, two):
    return lax.dot_general(one, two, (((1,), (0,)), ((), ())), preferred_element_type=F32)


def dot_nt(one, two):
    return lax.dot_general(one, two, (((1,), (1,)), ((), ())), preferred_element_type=F32)


def shape(dims, kind):
    return jax.ShapeDtypeStruct(dims, kind)


def after(kernel, count, deps):
    def body(*refs):
        kernel(*refs[:count], *refs[count + len(deps) :])

    return body


def whole_call(kernel, outs, args, flops, name, scratch=(), deps=(), limit=VMEM_LIMIT):
    moved = sum(math.prod(a.shape) * a.dtype.itemsize for a in (*args, *outs))
    return pl.pallas_call(
        after(kernel, len(args), deps),
        out_shape=tuple(outs),
        in_specs=[pl.BlockSpec(memory_space=pltpu.VMEM)] * len(args)
        + [pl.BlockSpec(memory_space=pl.ANY)] * len(deps),
        out_specs=tuple([pl.BlockSpec(memory_space=pltpu.VMEM)] * len(outs)),
        scratch_shapes=list(scratch),
        compiler_params=pltpu.CompilerParams(vmem_limit_bytes=limit),
        cost_estimate=pl.CostEstimate(
            flops=flops // UNDERSTATED, bytes_accessed=moved // UNDERSTATED, transcendentals=0
        ),
        name=name,
    )(*args, *deps)


def streamed_call(kernel, grid, outs, out_specs, args, in_specs, flops, name, scratch, deps=()):
    moved = sum(math.prod(a.shape) * a.dtype.itemsize for a in (*args, *outs))
    return pl.pallas_call(
        after(kernel, len(args), deps),
        grid=grid,
        out_shape=tuple(outs),
        in_specs=list(in_specs) + [pl.BlockSpec(memory_space=pl.ANY)] * len(deps),
        out_specs=tuple(out_specs),
        scratch_shapes=list(scratch),
        compiler_params=pltpu.CompilerParams(
            vmem_limit_bytes=VMEM_LIMIT, dimension_semantics=("arbitrary",)
        ),
        cost_estimate=pl.CostEstimate(
            flops=flops // UNDERSTATED, bytes_accessed=moved // UNDERSTATED, transcendentals=0
        ),
        name=name,
    )(*args, *deps)


def const_spec(dims):
    return pl.BlockSpec(dims, lambda i: (0,) * len(dims))


def swap_tensor(array, bit):
    size = lax.axis_size("tensor")
    return lax.ppermute(array, "tensor", [(i, i ^ bit) for i in range(size)])


def swap_dp(array, bit):
    size = lax.axis_size("dp")
    return lax.ppermute(array, "dp", [(i, i ^ bit) for i in range(size)])


def pack(parts, name, deps=()):
    def kernel(*refs):
        at = 0
        for ref in refs[:-1]:
            refs[-1][:, at : at + ref.shape[1]] = ref[...]
            at += ref.shape[1]

    out = shape((parts[0].shape[0], sum(p.shape[1] for p in parts)), parts[0].dtype)
    return whole_call(kernel, [out], parts, 0, name, deps=deps)[0]


def gather_far(rows):
    pieces = [(rows, [0])]
    step = lax.axis_size("dp") // 2
    while step > 1:
        if len(pieces) > 2:
            pieces = [merged(pieces)]
        pieces += [(swap_dp(p, step), [o ^ step for o in offsets]) for p, offsets in pieces]
        step //= 2
    return pieces


def merged(pieces):
    return (
        jnp.concatenate([p for p, _ in pieces], axis=0),
        [o for _, offsets in pieces for o in offsets],
    )


def gather_near(pieces):
    return [(swap_dp(p, 1), [o ^ 1 for o in offsets]) for p, offsets in pieces]


def other_core(pieces):
    return [(swap_tensor(p, CORE), offsets) for p, offsets in pieces]


def assemble(pieces, dp_place, name, deps=()):
    rows = pieces[0][0].shape[0] // len(pieces[0][1])
    width = pieces[0][0].shape[1]
    size = lax.axis_size("dp")

    def kernel(*refs):
        place = refs[0][0]
        for ref, (_, offsets) in zip(refs[1:-1], pieces):
            for i, offset in enumerate(offsets):
                start = pl.multiple_of((place ^ offset) * rows, rows)
                refs[-1][pl.ds(start, rows), :] = ref[i * rows : (i + 1) * rows, :]

    arrays = [p for p, _ in pieces]
    out = shape((size * rows, width), BF16)
    moved = 2 * size * rows * width * 2
    return pl.pallas_call(
        after(kernel, 1 + len(arrays), deps),
        out_shape=out,
        in_specs=[pl.BlockSpec(memory_space=pltpu.SMEM)]
        + [pl.BlockSpec(memory_space=pltpu.VMEM)] * len(arrays)
        + [pl.BlockSpec(memory_space=pl.ANY)] * len(deps),
        out_specs=pl.BlockSpec(memory_space=pltpu.VMEM),
        compiler_params=pltpu.CompilerParams(vmem_limit_bytes=VMEM_LIMIT),
        cost_estimate=pl.CostEstimate(
            flops=0, bytes_accessed=moved // UNDERSTATED, transcendentals=0
        ),
        name=name,
    )(dp_place, *arrays, *deps)


def halving_order(size, bits):
    order = [0]
    for bit in reversed(bits):
        order = order + [o ^ (1 << bit) for o in order]
    return order


def fold(keep, came, last, deps):
    rows, width = keep.shape

    def kernel(k_ref, c_ref, *refs):
        if last:
            refs[0][...] = k_ref[...] + c_ref[...].astype(F32)
        else:
            half = rows // 2
            refs[0][...] = k_ref[:half] + c_ref[:half].astype(F32)
            refs[1][...] = (k_ref[half:] + c_ref[half:].astype(F32)).astype(BF16)

    outs = [shape((rows, width), F32)]
    if not last:
        outs = [shape((rows // 2, width), F32), shape((rows // 2, width), BF16)]
    return whole_call(
        kernel, outs, [keep, came], rows * width, "fold", deps=deps, limit=SMALL_LIMIT
    )


class Chain:
    def __init__(self, keep, send, bits):
        self.keep, self.bits = keep, list(bits)
        self.came = swap_dp(send, 1 << self.bits.pop(0))
        self.done = False

    def fold(self, deps=()):
        if self.done:
            return
        self.done = not self.bits
        made = fold(self.keep, self.came, self.done, list(deps))
        self.keep = made[0]
        if not self.done:
            self.came = swap_dp(made[1], 1 << self.bits.pop(0))

    def finish(self):
        while not self.done:
            self.fold()
        return self.keep


def sum_all(vector, waits):
    def plus(one, two, deps):
        def kernel(a_ref, b_ref, out_ref):
            out_ref[...] = a_ref[...] + b_ref[...]

        out = shape(one.shape, F32)
        return whole_call(kernel, [out], [one, two], 0, "plus", deps=deps, limit=SMALL_LIMIT)[0]

    waits = list(waits)
    held = vector.reshape(-1, 128)
    for swap, axis in ((swap_tensor, "tensor"), (swap_dp, "dp")):
        step = 1
        while step < lax.axis_size(axis):
            held = plus(held, swap(held, step), waits.pop(0) if waits else [])
            step *= 2
    return held.reshape(-1)


def project_inputs(x_own, x_across, w_mine, w_other, b_mine, b_other, deps):
    rows, width = x_own.shape
    third = w_mine.shape[1] // 4

    def kernel(x0, x1, wm, wo, bm, bo, mine_ref, other_ref, send_ref):
        tokens = jnp.concatenate([x0[...], x1[...]], axis=0)
        mine = (dot(tokens, wm[:, : 3 * third]) + bm[...]).astype(BF16)
        other = (dot(tokens, wo[:, : 3 * third]) + bo[...]).astype(BF16)
        mine_ref[...] = mine
        other_ref[...] = other
        send_ref[:, : 2 * third] = other[:, third:]
        send_ref[:, 2 * third :] = mine[:, third:]

    outs = [
        shape((2 * rows, 3 * third), BF16),
        shape((2 * rows, 3 * third), BF16),
        shape((2 * rows, 4 * third), BF16),
    ]
    flops = 2 * 2 * rows * width * 6 * third
    return whole_call(
        kernel,
        outs,
        [x_own, x_across, w_mine, w_other, b_mine, b_other],
        flops,
        "project_inputs",
        deps=deps,
    )


def attention_forward(mine, other, far, bias_row, w_mine, w_other, head_size, deps):
    rows = mine.shape[0]
    third = mine.shape[1] // 3
    heads = third // head_size
    block = rows // 2
    width = w_mine.shape[0]
    scaling = 1.0 / math.sqrt(head_size)

    def kernel(mine_ref, other_ref, far_ref, bias_ref, wm, wo, cm_ref, co_ref, own_ref, across_ref, acc):
        lane_head = lax.broadcasted_iota(jnp.int32, (1, third), 1) // head_size
        acc[...] = jnp.zeros_like(acc)
        bias = bias_ref[...]

        def one_head(head, carry):
            inside = lane_head == head
            for group, ref in enumerate((mine_ref, other_ref)):
                base = 2 * third * group
                keys = jnp.concatenate(
                    [ref[:, third : 2 * third], far_ref[:, base : base + third]], axis=0
                )
                vals = jnp.concatenate(
                    [ref[:, 2 * third :], far_ref[:, base + third : base + 2 * third]], axis=0
                )
                for part in range(2):
                    span = slice(part * block, (part + 1) * block)
                    query = jnp.where(inside, ref[span, :third] * scaling, 0.0).astype(BF16)
                    scores = dot_nt(query, keys) + bias
                    peak = jnp.max(scores, axis=-1, keepdims=True)
                    weights = jnp.exp(scores - peak)
                    total = jnp.sum(weights, axis=-1, keepdims=True)
                    found = dot(weights.astype(BF16), vals) * (1.0 / total)
                    acc[group, span, :] += jnp.where(inside, found, 0.0)
            return carry

        lax.fori_loop(0, heads, one_head, 0)
        ctx_mine = acc[0].astype(BF16)
        ctx_other = acc[1].astype(BF16)
        cm_ref[...] = ctx_mine
        co_ref[...] = ctx_other
        part_sum = dot_nt(ctx_mine, wm[:, 3 * third :]) + dot_nt(ctx_other, wo[:, 3 * third :])
        own_ref[...] = part_sum[:block]
        across_ref[...] = part_sum[block:].astype(BF16)

    outs = [
        shape((rows, third), BF16),
        shape((rows, third), BF16),
        shape((block, width), F32),
        shape((block, width), BF16),
    ]
    flops = 2 * 2 * 2 * rows * 2 * rows * third * heads * 2
    return whole_call(
        kernel,
        outs,
        [mine, other, far, bias_row, w_mine, w_other],
        flops,
        "attention_forward",
        [pltpu.VMEM((2, rows, third), F32)],
        deps,
    )


def attention_backward(mine, other, far, bias_column, ga_own, ga_across, w_mine, w_other, head_size, deps):
    rows = mine.shape[0]
    third = mine.shape[1] // 3
    heads = third // head_size
    block = rows // 2
    keys_count = 2 * rows
    scaling = 1.0 / math.sqrt(head_size)

    def kernel(
        mine_ref, other_ref, far_ref, bias_ref, g0, g1, wm, wo,
        dq_ref, keep_ref, send_ref, sums_ref, grad_ctx, keys_t, dq_t, dkv,
    ):
        lane_head = lax.broadcasted_iota(jnp.int32, (1, third), 1) // head_size
        grad_rows = jnp.concatenate([g0[...], g1[...]], axis=0)
        grad_ctx[0] = dot(grad_rows, wm[:, 3 * third :]).astype(BF16)
        grad_ctx[1] = dot(grad_rows, wo[:, 3 * third :]).astype(BF16)
        dkv[...] = jnp.zeros_like(dkv)
        for group, ref in enumerate((mine_ref, other_ref)):
            base = 2 * third * group
            keys_t[group, :, :rows] = ref[:, third : 2 * third].T
            keys_t[group, :, rows:] = far_ref[:, base : base + third].T
        bias = bias_ref[...]

        def one_head(head, carry):
            inside = lane_head == head
            start = pl.multiple_of(head * head_size, head_size)
            for group, ref in enumerate((mine_ref, other_ref)):
                base = 2 * third * group
                keys = jnp.concatenate(
                    [ref[:, third : 2 * third], far_ref[:, base : base + third]], axis=0
                )
                vals = jnp.concatenate(
                    [ref[:, 2 * third :], far_ref[:, base + third : base + 2 * third]], axis=0
                )
                head_keys_t = keys_t[group, pl.ds(start, head_size), :]
                for part in range(2):
                    span = slice(part * block, (part + 1) * block)
                    query = jnp.where(inside, ref[span, :third] * scaling, 0.0).astype(BF16)
                    grad = jnp.where(inside, grad_ctx[group, span, :], 0.0).astype(BF16)
                    scores = dot_nt(keys, query) + bias
                    peak = jnp.max(scores, axis=0, keepdims=True)
                    weights = jnp.exp(scores - peak)
                    total = jnp.sum(weights, axis=0, keepdims=True)
                    probs = weights * (1.0 / total)
                    grad_probs = dot_nt(vals, grad)
                    inner = jnp.sum(probs * grad_probs, axis=0, keepdims=True)
                    grad_scores = (probs * (grad_probs - inner)).astype(BF16)
                    dkv[group, 1] += dot(probs.astype(BF16), grad)
                    dkv[group, 0] += dot(grad_scores, query)
                    dq_t[group, pl.ds(start, head_size), span] = dot(head_keys_t, grad_scores)
            return carry

        lax.fori_loop(0, heads, one_head, 0)
        for group in range(2):
            grad_query = (dq_t[group].T * scaling).astype(BF16)
            dq_ref[:, group * third : (group + 1) * third] = grad_query
            sums_ref[group : group + 1, :third] = jnp.sum(
                grad_query.astype(F32), axis=0, keepdims=True
            )
            sums_ref[group : group + 1, third:] = jnp.sum(dkv[group, 1], axis=0, keepdims=True)
            for kind in range(2):
                at = (2 * group + kind) * third
                keep_ref[:, at : at + third] = dkv[group, kind, :rows]
                away = (2 * (1 - group) + kind) * third
                send_ref[:, away : away + third] = dkv[group, kind, rows:].astype(BF16)

    outs = [
        shape((rows, 2 * third), BF16),
        shape((rows, 4 * third), F32),
        shape((rows, 4 * third), BF16),
        shape((2, 2 * third), F32),
    ]
    flops = 5 * 2 * 2 * rows * keys_count * third * heads * 2 * UNDERSTATED
    return whole_call(
        kernel,
        outs,
        [mine, other, far, bias_column, ga_own, ga_across, w_mine, w_other],
        flops,
        "attention_backward",
        [
            pltpu.VMEM((2, rows, third), BF16),
            pltpu.VMEM((2, third, keys_count), BF16),
            pltpu.VMEM((2, third, rows), F32),
            pltpu.VMEM((2, 2, keys_count, third), F32),
        ],
        deps,
    )


def project_back(dq, keep, got, w_mine, w_other, deps):
    rows = dq.shape[0]
    third = dq.shape[1] // 2
    block = rows // 2
    width = w_mine.shape[0]

    def kernel(dq_ref, keep_ref, got_ref, wm, wo, gm_ref, go_ref, own_ref, across_ref):
        dkv = (keep_ref[...] + got_ref[...].astype(F32)).astype(BF16)
        grad_mine = jnp.concatenate([dq_ref[:, :third], dkv[:, : 2 * third]], axis=1)
        grad_other = jnp.concatenate([dq_ref[:, third:], dkv[:, 2 * third :]], axis=1)
        gm_ref[...] = dkv[:, : 2 * third]
        go_ref[...] = dkv[:, 2 * third :]
        back = dot_nt(grad_mine, wm[:, : 3 * third]) + dot_nt(grad_other, wo[:, : 3 * third])
        own_ref[...] = back[:block]
        across_ref[...] = back[block:].astype(BF16)

    outs = [
        shape((rows, 2 * third), BF16),
        shape((rows, 2 * third), BF16),
        shape((block, width), F32),
        shape((block, width), BF16),
    ]
    flops = 2 * rows * width * 6 * third
    return whole_call(
        kernel, outs, [dq, keep, got, w_mine, w_other], flops, "project_back", deps=deps
    )


def moments(summed):
    centre = jnp.mean(summed, axis=-1, keepdims=True)
    centred = summed - centre
    spread = jnp.mean(centred * centred, axis=-1, keepdims=True)
    back = lax.rsqrt(spread + NORM_EPS)
    return centred * back, back


def first_norm(x_own, part, got, b_out, gain, shift, deps):
    dims = x_own.shape

    def kernel(x_ref, p_ref, r_ref, b_ref, g_ref, s_ref, summed_ref, normed_ref, low_ref):
        summed = x_ref[...].astype(F32) + (p_ref[...] + r_ref[...].astype(F32)) + b_ref[...]
        unit, _ = moments(summed)
        normed = unit * g_ref[...] + s_ref[...]
        summed_ref[...] = summed
        normed_ref[...] = normed
        low_ref[...] = normed.astype(BF16)

    outs = [shape(dims, F32), shape(dims, F32), shape(dims, BF16)]
    return whole_call(
        kernel,
        outs,
        [x_own, part, got, b_out, gain, shift],
        20 * math.prod(dims),
        "first_norm",
        deps=deps,
        limit=SMALL_LIMIT,
    )


def second_norm(normed, part, got, cotangent, b_down, gain, shift):
    dims = normed.shape

    def kernel(n_ref, p_ref, r_ref, c_ref, b_ref, g_ref, s_ref, out_ref, grad_ref, low_ref, sums_ref):
        summed = n_ref[...] + (p_ref[...] + r_ref[...].astype(F32)) + b_ref[...]
        unit, back = moments(summed)
        out_ref[...] = (unit * g_ref[...] + s_ref[...]).astype(BF16)
        cot = c_ref[...].astype(F32)
        scaled = cot * g_ref[...]
        grad = back * (
            scaled
            - jnp.mean(scaled, axis=-1, keepdims=True)
            - unit * jnp.mean(scaled * unit, axis=-1, keepdims=True)
        )
        grad_ref[...] = grad
        low_ref[...] = grad.astype(BF16)
        sums_ref[0:1, :] = jnp.sum(cot * unit, axis=0, keepdims=True)
        sums_ref[1:2, :] = jnp.sum(cot, axis=0, keepdims=True)
        sums_ref[2:3, :] = jnp.sum(grad, axis=0, keepdims=True)

    outs = [shape(dims, BF16), shape(dims, F32), shape(dims, BF16), shape((3, dims[1]), F32)]
    return whole_call(
        kernel,
        outs,
        [normed, part, got, cotangent, b_down, gain, shift],
        40 * math.prod(dims),
        "second_norm",
        limit=SMALL_LIMIT,
    )


def first_norm_back(summed, grad_second, part, got, gain, deps):
    dims = summed.shape

    def kernel(z_ref, gs_ref, p_ref, r_ref, g_ref, grad_ref, low_ref, sums_ref):
        unit, back = moments(z_ref[...])
        grad_normed = gs_ref[...] + (p_ref[...] + r_ref[...].astype(F32))
        scaled = grad_normed * g_ref[...]
        grad = back * (
            scaled
            - jnp.mean(scaled, axis=-1, keepdims=True)
            - unit * jnp.mean(scaled * unit, axis=-1, keepdims=True)
        )
        grad_ref[...] = grad
        low_ref[...] = grad.astype(BF16)
        sums_ref[0:1, :] = jnp.sum(grad_normed * unit, axis=0, keepdims=True)
        sums_ref[1:2, :] = jnp.sum(grad_normed, axis=0, keepdims=True)
        sums_ref[2:3, :] = jnp.sum(grad, axis=0, keepdims=True)

    outs = [shape(dims, F32), shape(dims, BF16), shape((3, dims[1]), F32)]
    return whole_call(
        kernel,
        outs,
        [summed, grad_second, part, got, gain],
        40 * math.prod(dims),
        "first_norm_back",
        deps=deps,
        limit=SMALL_LIMIT,
    )


def feed_forward(n_own, n_far, weights, bias, prior, deps):
    block, width = n_own.shape
    rows = 2 * block
    hidden = weights.shape[1] // 2
    tile = min(256, hidden)
    steps = hidden // tile
    last = prior is not None

    def kernel(n0, n1, u, d, b, *refs):
        step = pl.program_id(0)
        if last:
            before, a_ref, s_ref, own_ref, far_ref, tokens, acc = refs
        else:
            a_ref, s_ref, acc, tokens = refs

        @pl.when(step == 0)
        def _():
            tokens[:block] = n0[...]
            tokens[block:] = n1[...]
            acc[...] = before[...] if last else jnp.zeros_like(acc)

        hid = dot(tokens[...], u[...]) + b[...]
        half = 0.5 * (1.0 + lax.erf(hid * (1.0 / math.sqrt(2.0))))
        bell = jnp.exp(hid * hid * -0.5) * (1.0 / math.sqrt(2.0 * math.pi))
        active = (hid * half).astype(BF16)
        a_ref[...] = active
        s_ref[...] = (half + hid * bell).astype(BF16)
        acc[...] += dot_nt(active, d[...])

        if last:

            @pl.when(step == steps - 1)
            def _():
                own_ref[...] = acc[:block]
                far_ref[...] = acc[block:].astype(BF16)

    column = pl.BlockSpec((width, tile), lambda i: (0, i))
    later = pl.BlockSpec((width, tile), lambda i: (0, steps + i))
    made = pl.BlockSpec((rows, tile), lambda i: (0, i))
    args = [n_own, n_far, weights, weights, bias]
    in_specs = [const_spec((block, width))] * 2
    in_specs += [column, later, pl.BlockSpec((1, tile), lambda i: (0, i))]
    outs = [shape((rows, hidden), BF16)] * 2
    scratch = [pltpu.VMEM((rows, width), BF16)]
    if last:
        args.append(prior)
        in_specs.append(const_spec((rows, width)))
        outs += [shape((block, width), F32), shape((block, width), BF16)]
        out_specs = [made] * 2 + [const_spec((block, width))] * 2
        scratch.append(pltpu.VMEM((rows, width), F32))
    else:
        outs.append(shape((rows, width), F32))
        out_specs = [made] * 2 + [const_spec((rows, width))]
    return streamed_call(
        kernel,
        (steps,),
        outs,
        out_specs,
        args,
        in_specs,
        2 * 2 * rows * width * hidden,
        "feed_forward",
        scratch,
        deps,
    )


def feed_forward_back(g_own, g_across, w_mine, w_other, slope_mine, slope_other, deps):
    block, width = g_own.shape
    rows = 2 * block
    hidden = w_mine.shape[1] // 2
    tile = min(256, hidden)
    steps = hidden // tile

    def kernel(
        g0, g1, um, uo, dm, do, sm, so,
        gm_ref, go_ref, own_ref, across_ref, bm_ref, bo_ref, grads, acc,
    ):
        step = pl.program_id(0)

        @pl.when(step == 0)
        def _():
            grads[:block] = g0[...]
            grads[block:] = g1[...]
            acc[...] = jnp.zeros_like(acc)

        total = acc[...]
        for u, d, s, g_ref, b_ref in ((um, dm, sm, gm_ref, bm_ref), (uo, do, so, go_ref, bo_ref)):
            grad_hidden = (dot(grads[...], d[...]) * s[...].astype(F32)).astype(BF16)
            g_ref[...] = grad_hidden
            b_ref[...] = jnp.sum(grad_hidden.astype(F32), axis=0, keepdims=True)
            total = total + dot_nt(grad_hidden, u[...])
        acc[...] = total

        @pl.when(step == steps - 1)
        def _():
            own_ref[...] = acc[:block]
            across_ref[...] = acc[block:].astype(BF16)

    column = pl.BlockSpec((width, tile), lambda i: (0, i))
    later = pl.BlockSpec((width, tile), lambda i: (0, steps + i))
    bias = pl.BlockSpec((1, tile), lambda i: (0, i))
    made = pl.BlockSpec((rows, tile), lambda i: (0, i))
    outs = (
        [shape((rows, hidden), BF16)] * 2
        + [shape((block, width), F32), shape((block, width), BF16)]
        + [shape((1, hidden), F32)] * 2
    )
    return streamed_call(
        kernel,
        (steps,),
        outs,
        [made] * 2 + [const_spec((block, width))] * 2 + [bias] * 2,
        [g_own, g_across, w_mine, w_other, w_mine, w_other, slope_mine, slope_other],
        [const_spec((block, width))] * 2 + [column] * 2 + [later] * 2 + [made] * 2,
        2 * 2 * rows * width * 2 * hidden,
        "feed_forward_back",
        [pltpu.VMEM((rows, width), BF16), pltpu.VMEM((rows, width), F32)],
        deps,
    )


def weight_grad(ones, mine, other, dp_place, chains, name, other_first=0, deps=(), halves=False):
    block, width = ones[0].shape
    rows = 2 * block
    count = chains[0][0]
    tile = min(256, count)
    tiles = count // tile
    size = lax.axis_size("dp")
    share = width // size
    half = width // 2

    def kernel(place_ref, a0, a1, a2, a3, m0, m1, o0, o1, *refs):
        turned, full = refs[-2:]
        step = pl.program_id(0)

        @pl.when(step == 0)
        def _():
            for i, ref in enumerate((a0, a1, a2, a3)):
                turned[:, i * block : (i + 1) * block] = ref[...].T

        place = place_ref[0]
        each = 4 if halves else 2

        def write(targets, order):
            for i, offset in enumerate(order):
                start = pl.multiple_of((place ^ offset) * share, share)
                at = i * share
                ref = targets[0] if len(targets) == 1 or at < half else targets[1]
                at = at if len(targets) == 1 or at < half else at - half
                ref[at : at + share, :] = full[pl.ds(start, share), :].astype(ref.dtype)

        for which, (one, two) in enumerate(((m0, m1), (o0, o1))):
            full[...] = dot(turned[:, :rows], one[...]) + dot(turned[:, rows:], two[...])
            for c, (_, bits) in enumerate(chains):
                per = each // 2
                targets = refs[c * each + which * per : c * each + (which + 1) * per]
                order = halving_order(size, bits)
                if len(chains) == 1:
                    write(targets, order)
                else:
                    pl.when(step // tiles == c)(lambda t=targets, o=order: write(t, o))

    base = other_first // tile
    column = pl.BlockSpec((rows, tile), lambda i: (0, i))
    other_column = pl.BlockSpec((rows, tile), lambda i: (0, base + i))
    outs, out_specs = [], []
    for c in range(len(chains)):
        index = lambda i, c=c: (0, jnp.clip(i - c * tiles, 0, tiles - 1))
        for kinds in ((F32, BF16), (F32, BF16)) if halves else ((F32,), (BF16,)):
            for kind in kinds:
                held = half if halves else width
                outs.append(shape((held, count), kind))
                out_specs.append(pl.BlockSpec((held, tile), index))
    return streamed_call(
        kernel,
        (tiles * len(chains),),
        outs,
        out_specs,
        [dp_place, *ones, *mine, *other],
        [pl.BlockSpec(memory_space=pltpu.SMEM)]
        + [const_spec((block, width))] * 4
        + [column] * 2
        + [other_column] * 2,
        2 * 2 * rows * width * 2 * count * len(chains),
        name,
        [pltpu.VMEM((width, 2 * rows), BF16), pltpu.VMEM((width, tile), F32)],
        deps,
    )


def core_chain(mine, other, bits, deps=()):
    keep, send = fold(mine, swap_tensor(other, CORE), False, list(deps))
    return Chain(keep, send, bits)


def add_up(parts, deps):
    def kernel(*refs):
        refs[-1][...] = sum(ref[...] for ref in refs[:-1])

    out = shape(parts[0].shape, F32)
    return whole_call(kernel, [out], parts, 0, "add_up", deps=deps, limit=SMALL_LIMIT)[0]


def shards(
    inputs,
    lengths,
    w_query,
    w_key,
    w_value,
    w_out,
    w_up,
    w_down,
    b_query,
    b_value,
    b_out,
    b_up,
    b_down,
    first_gain,
    first_shift,
    second_gain,
    second_shift,
    cotangent,
):
    seq_count, block, width = inputs.shape
    tensor_size = lax.axis_size("tensor")
    seq_len = block * tensor_size
    place = lax.axis_index("tensor")
    head_dims = w_query.shape[1]
    head_size = width // HEADS
    hidden = w_up.shape[1]
    seqs = range(seq_count)
    row = lambda vector: vector.reshape(1, -1)

    x_own = [inputs[s] for s in seqs]
    x_across = [swap_tensor(x_own[s], ACROSS) for s in seqs]

    dp_place = lax.axis_index("dp").astype(jnp.int32).reshape(1)
    att_far = gather_far(pack([w_query, w_key, w_value, w_out.T], "pack_attention"))
    att_pieces = att_far + gather_near(att_far)
    share = pack([w_up, w_down.T], "pack_feed", [p for p, _ in att_far[1:2]])
    share_other = swap_tensor(share, ACROSS)
    mine_far = gather_far(share)
    mine_near = gather_near(mine_far)
    other_far = gather_far(share_other)
    other_near = gather_near(other_far[:1]) + [
        (swap_tensor(p, ACROSS), offsets) for p, offsets in mine_near[1:]
    ]

    def arrays(pieces):
        return [p for p, _ in pieces]

    att_mine = assemble(att_pieces, dp_place, "assemble_attention")
    att_other = assemble(
        other_core(att_pieces), dp_place, "assemble_attention_other", arrays(mine_far[1:2])
    )
    project_waits = [arrays(mine_far[2:3]), arrays(mine_near[:1])]
    attend_waits = [
        [share_other] + arrays(mine_far[3:]),
        arrays(mine_near[1:3] + other_far[1:3]),
    ]
    norm_waits = [arrays(mine_near[3:] + other_far[3:]), arrays(other_near[:2])]
    ffw_mine = assemble(mine_far + mine_near, dp_place, "assemble_feed")

    biases = jnp.concatenate([b_query, jnp.zeros_like(b_query), b_value])
    qkv_bias_mine, qkv_bias_other = row(biases), row(swap_tensor(biases, CORE))
    up_bias_mine, up_bias_other = row(b_up), row(swap_tensor(b_up, ACROSS))
    b_out_row, b_down_row = row(b_out), row(b_down)
    gain_one, shift_one = row(first_gain), row(first_shift)
    gain_two, shift_two = row(second_gain), row(second_shift)

    order = jnp.stack([place, place ^ ACROSS, place ^ CORE, place ^ CORE ^ ACROSS])
    positions = (order[:, None] * block + jnp.arange(block, dtype=jnp.int32)[None, :]).reshape(-1)
    masks = [jnp.where(positions < lengths[s], 0.0, MASKED).astype(F32) for s in seqs]

    projected = []
    for s in seqs:
        waits = project_waits[s] if s < 2 else []
        projected.append(
            project_inputs(
                x_own[s], x_across[s], att_mine, att_other, qkv_bias_mine, qkv_bias_other,
                waits + [p[2] for p in projected[-1:]],
            )
        )
    far = [swap_tensor(projected[s][2], CORE) for s in seqs]
    attended = []
    for s in seqs:
        waits = attend_waits[s] if s < 2 else []
        attended.append(
            attention_forward(
                projected[s][0], projected[s][1], far[s], masks[s].reshape(1, seq_len),
                att_mine, att_other, head_size, waits + [p[2] for p in attended[-1:]],
            )
        )
    attended_got = [swap_tensor(attended[s][3], ACROSS) for s in seqs]
    one = []
    for s in seqs:
        waits = norm_waits[s] if s < 2 else []
        one.append(
            first_norm(
                x_own[s], attended[s][2], attended_got[s], b_out_row, gain_one, shift_one,
                waits + [p[2] for p in one[-1:]],
            )
        )
    normed_far = [swap_tensor(one[s][2], CORE) for s in seqs]
    fed_one = []
    for s in seqs:
        waits = [p[2] for p in fed_one[-1:]]
        fed_one.append(
            feed_forward(one[s][2], normed_far[s], ffw_mine, up_bias_mine, None, waits)
        )
    ffw_other = assemble(
        other_far + other_near, dp_place, "assemble_feed_other", [fed_one[-1][2]]
    )
    fed_two = []
    for s in seqs:
        waits = [p[2] for p in fed_two[-1:]]
        fed_two.append(
            feed_forward(
                one[s][2], normed_far[s], ffw_other, up_bias_other, fed_one[s][2], waits
            )
        )
    fed = [(fed_one[s][0], fed_two[s][0], fed_one[s][1], fed_two[s][1], *fed_two[s][2:]) for s in seqs]
    branch_got = [swap_tensor(fed[s][5], CORE) for s in seqs]
    two = [
        second_norm(
            one[s][1], fed[s][4], branch_got[s], cotangent[s], b_down_row, gain_two, shift_two
        )
        for s in seqs
    ]
    grad_far = [swap_tensor(two[s][2], CORE) for s in seqs]
    fed_back = []
    for s in seqs:
        waits = [p[2] for p in fed_back[-1:]]
        fed_back.append(
            feed_forward_back(
                two[s][2], grad_far[s], ffw_mine, ffw_other, fed[s][2], fed[s][3], waits
            )
        )
    back_got = [swap_tensor(fed_back[s][3], CORE) for s in seqs]
    def placed_in(part_mine, part_other, bit):
        size = part_mine.shape[0]
        empty = jnp.zeros((tensor_size * size,), F32)
        empty = lax.dynamic_update_slice(empty, part_mine, (place * size,))
        return lax.dynamic_update_slice(empty, part_other, ((place ^ bit) * size,))

    levels = range(lax.axis_size("dp").bit_length() - 1)
    near_first = list(levels)
    far_first = [1, 0, *levels[2:]] if len(near_first) > 1 else near_first

    def pairs(own, across):
        return [part for s in seqs for part in (own[s], across[s])]

    def norm_back(s, deps):
        return first_norm_back(
            one[s][0], two[s][1], fed_back[s][2], back_got[s], gain_one, deps
        )

    down_made = weight_grad(
        pairs([two[s][2] for s in seqs], grad_far),
        [fed[s][0] for s in seqs], [fed[s][1] for s in seqs],
        dp_place, [(hidden, near_first)], "w_down_grad", deps=[fed_back[-1][2]], halves=True,
    )
    one_back = [norm_back(s, [down_made[1]]) for s in seqs]
    up_made = weight_grad(
        pairs([one[s][2] for s in seqs], normed_far),
        [fed_back[s][0] for s in seqs], [fed_back[s][1] for s in seqs],
        dp_place, [(hidden, far_first)], "w_up_grad", deps=[one_back[s][1] for s in seqs], halves=True,
    )
    first_across = [swap_tensor(one_back[s][1], ACROSS) for s in seqs]
    down_mine = Chain(down_made[0], down_made[1], near_first)
    down_other = Chain(down_made[2], down_made[3], near_first)
    up_mine = Chain(up_made[0], up_made[1], far_first)
    up_other = Chain(up_made[2], up_made[3], far_first)

    def backward(s, deps):
        return attention_backward(
            projected[s][0], projected[s][1], far[s], masks[s].reshape(seq_len, 1),
            one_back[s][1], first_across[s], att_mine, att_other, head_size, deps,
        )

    attended_back = [backward(0, [up_made[1]])]
    out_made = weight_grad(
        pairs([one_back[s][1] for s in seqs], first_across),
        [attended[s][0] for s in seqs], [attended[s][1] for s in seqs],
        dp_place, [(head_dims, near_first)], "w_out_grad", deps=[attended_back[0][3]],
    )
    down_mine.fold([attended_back[0][3]])
    up_mine.fold([attended_back[0][3]])
    attended_back += [backward(s, [down_mine.keep, up_mine.keep, out_made[1]]) for s in seqs[1:]]
    far_back = [swap_tensor(attended_back[s][2], CORE) for s in seqs]

    down_other.fold([attended_back[-1][3]])
    up_other.fold([attended_back[-1][3]])
    tokens = pairs(x_own, x_across)
    grad_queries = [attended_back[s][0] for s in seqs]
    query_made = weight_grad(
        tokens, grad_queries, grad_queries, dp_place, [(head_dims, far_first)], "w_query_grad",
        head_dims, [far_back[0], down_other.keep, up_other.keep, down_mine.came, up_mine.came],
    )
    query_chain = core_chain(query_made[0], query_made[1], far_first)
    back = [
        project_back(
            attended_back[0][0], attended_back[0][1], far_back[0], att_mine, att_other,
            [query_made[1], far_back[-1]],
        )
    ]
    down_mine.fold([back[0][2]])
    up_mine.fold([back[0][2]])
    back += [
        project_back(
            attended_back[s][0], attended_back[s][1], far_back[s], att_mine, att_other,
            [down_mine.keep, up_mine.keep],
        )
        for s in seqs[1:]
    ]
    input_got = [swap_tensor(back[s][3], ACROSS) for s in seqs]
    key_value_made = weight_grad(
        tokens, [back[s][0] for s in seqs], [back[s][1] for s in seqs],
        dp_place, [(head_dims, near_first), (head_dims, far_first)], "w_key_value_grad",
        deps=input_got[:1],
    )
    down_other.fold([key_value_made[0]])
    up_other.fold([key_value_made[0]])
    seconds = [down_other.keep, up_other.keep, input_got[-1]]
    key_chain = core_chain(key_value_made[0], key_value_made[1], near_first, seconds)
    value_chain = core_chain(key_value_made[2], key_value_made[3], far_first, seconds)
    out_chain = core_chain(out_made[0], out_made[1], near_first, [attended_back[-1][3]])
    out_chain.fold([key_value_made[0]])
    query_chain.fold([key_value_made[0]])
    for chain in (down_mine, up_mine, down_other, up_other):
        chain.fold([value_chain.keep, key_chain.keep])
    input_grad = jnp.stack(
        [
            (one_back[s][0] + (back[s][2] + input_got[s].astype(F32))).astype(BF16)
            for s in seqs
        ]
    )
    sums = add_up([attended_back[s][3] for s in seqs], [query_made[1]])
    small = sum_all(
        jnp.concatenate(
            [
                sum(two[s][3] for s in seqs).reshape(-1),
                sum(one_back[s][2] for s in seqs).reshape(-1),
                placed_in(
                    sum(fed_back[s][4] for s in seqs).reshape(-1),
                    sum(fed_back[s][5] for s in seqs).reshape(-1),
                    ACROSS,
                ),
                placed_in(sums[0, :head_dims], sums[1, :head_dims], CORE),
                placed_in(sums[0, head_dims:], sums[1, head_dims:], CORE),
            ]
        ),
        [[back[0][2]], [back[-1][2]], [key_chain.keep, value_chain.keep]],
    )

    def over_y(mine, other):
        return mine.finish() + swap_tensor(other.finish().astype(BF16), ACROSS).astype(F32)

    down_grad, up_grad = over_y(down_mine, down_other), over_y(up_mine, up_other)
    vectors = [small[i * width : (i + 1) * width] for i in range(6)]
    second_gain_grad, second_shift_grad, b_down_grad = vectors[:3]
    first_gain_grad, first_shift_grad, b_out_grad = vectors[3:]
    b_up_grad = small[6 * width : 6 * width + tensor_size * hidden]
    b_query_grad, b_value_grad = small[-2 * width : -width], small[-width:]

    output = jnp.stack([two[s][0] for s in seqs])
    return (
        output,
        input_grad,
        query_chain.finish(),
        key_chain.finish(),
        value_chain.finish(),
        out_chain.finish().T,
        up_grad,
        down_grad.T,
        b_query_grad,
        b_value_grad,
        b_out_grad,
        b_up_grad,
        b_down_grad,
        first_gain_grad,
        first_shift_grad,
        second_gain_grad,
        second_shift_grad,
    )


def solution(mesh):
    placed = (
        P("dp", "tensor", None),
        P("dp"),
        P("dp", "tensor"),
        P("dp", "tensor"),
        P("dp", "tensor"),
        P("tensor", "dp"),
        P("dp", "tensor"),
        P("tensor", "dp"),
        P("tensor"),
        P("tensor"),
        P(),
        P("tensor"),
        P(),
        P(),
        P(),
        P(),
        P(),
        P("dp", "tensor", None),
    )
    return jax.shard_map(
        shards,
        mesh=mesh,
        in_specs=placed,
        out_specs=(
            P("dp", "tensor", None),
            P("dp", "tensor", None),
            P("dp", "tensor"),
            P("dp", "tensor"),
            P("dp", "tensor"),
            P("tensor", "dp"),
            P("dp", "tensor"),
            P("tensor", "dp"),
            P(),
            P(),
            P(),
            P(),
            P(),
            P(),
            P(),
            P(),
            P(),
        ),
        check_vma=False,
    )
```

```python
import math

import jax
import jax.numpy as jnp
from jax import lax
from jax.experimental import pallas as pl
from jax.experimental.pallas import tpu as pltpu
from jax.sharding import PartitionSpec as P

HEADS = 16
NORM_EPS = 1e-12
MASKED = -1000000000.0
MIB = 1024 * 1024
VMEM_LIMIT = 56 * MIB
SMALL_LIMIT = 16 * MIB
FOLD_LIMIT = 24 * MIB
UNDERSTATED = 1000

F32 = jnp.float32
BF16 = jnp.bfloat16

CORE = 1
ACROSS = 2


def dot(one, two):
    return lax.dot_general(one, two, (((1,), (0,)), ((), ())), preferred_element_type=F32)


def dot_nt(one, two):
    return lax.dot_general(one, two, (((1,), (1,)), ((), ())), preferred_element_type=F32)


def shape(dims, kind):
    return jax.ShapeDtypeStruct(dims, kind)


def after(kernel, count, deps):
    def body(*refs):
        kernel(*refs[:count], *refs[count + len(deps) :])

    return body


def whole_call(kernel, outs, args, flops, name, scratch=(), deps=(), limit=VMEM_LIMIT):
    moved = sum(math.prod(a.shape) * a.dtype.itemsize for a in (*args, *outs))
    return pl.pallas_call(
        after(kernel, len(args), deps),
        out_shape=tuple(outs),
        in_specs=[pl.BlockSpec(memory_space=pltpu.VMEM)] * len(args)
        + [pl.BlockSpec(memory_space=pl.ANY)] * len(deps),
        out_specs=tuple([pl.BlockSpec(memory_space=pltpu.VMEM)] * len(outs)),
        scratch_shapes=list(scratch),
        compiler_params=pltpu.CompilerParams(vmem_limit_bytes=limit),
        cost_estimate=pl.CostEstimate(
            flops=flops // UNDERSTATED, bytes_accessed=moved // UNDERSTATED, transcendentals=0
        ),
        name=name,
    )(*args, *deps)


def streamed_call(kernel, grid, outs, out_specs, args, in_specs, flops, name, scratch, deps=()):
    moved = sum(math.prod(a.shape) * a.dtype.itemsize for a in (*args, *outs))
    return pl.pallas_call(
        after(kernel, len(args), deps),
        grid=grid,
        out_shape=tuple(outs),
        in_specs=list(in_specs) + [pl.BlockSpec(memory_space=pl.ANY)] * len(deps),
        out_specs=tuple(out_specs),
        scratch_shapes=list(scratch),
        compiler_params=pltpu.CompilerParams(
            vmem_limit_bytes=VMEM_LIMIT, dimension_semantics=("arbitrary",)
        ),
        cost_estimate=pl.CostEstimate(
            flops=flops // UNDERSTATED, bytes_accessed=moved // UNDERSTATED, transcendentals=0
        ),
        name=name,
    )(*args, *deps)


def const_spec(dims):
    return pl.BlockSpec(dims, lambda i: (0,) * len(dims))


def swap_tensor(array, bit):
    size = lax.axis_size("tensor")
    return lax.ppermute(array, "tensor", [(i, i ^ bit) for i in range(size)])


def swap_dp(array, bit):
    size = lax.axis_size("dp")
    return lax.ppermute(array, "dp", [(i, i ^ bit) for i in range(size)])


def pack(parts, name, deps=()):
    def kernel(*refs):
        at = 0
        for ref in refs[:-1]:
            refs[-1][:, at : at + ref.shape[1]] = ref[...]
            at += ref.shape[1]

    out = shape((parts[0].shape[0], sum(p.shape[1] for p in parts)), parts[0].dtype)
    return whole_call(kernel, [out], parts, 0, name, deps=deps)[0]


def gather_far(rows):
    held = (rows, [0])
    steps = []
    step = lax.axis_size("dp") // 2
    while step > 1:
        steps.append(step)
        step //= 2
    first = []
    for step in steps[:-1]:
        came = (swap_dp(held[0], step), [o ^ step for o in held[1]])
        first.append(came[0])
        held = merged([held, came])
    pieces = [held]
    if steps:
        pieces.append((swap_dp(held[0], steps[-1]), [o ^ steps[-1] for o in held[1]]))
    return pieces, first[:1]


def merged(pieces):
    return (
        jnp.concatenate([p for p, _ in pieces], axis=0),
        [o for _, offsets in pieces for o in offsets],
    )


def gather_near(pieces):
    return [(swap_dp(p, 1), [o ^ 1 for o in offsets]) for p, offsets in pieces]


def other_core(pieces):
    return [(swap_tensor(p, CORE), offsets) for p, offsets in pieces]


def assemble(pieces, dp_place, name, deps=()):
    rows = pieces[0][0].shape[0] // len(pieces[0][1])
    width = pieces[0][0].shape[1]
    size = lax.axis_size("dp")

    def kernel(*refs):
        place = refs[0][0]
        for ref, (_, offsets) in zip(refs[1:-1], pieces):
            for i, offset in enumerate(offsets):
                start = pl.multiple_of((place ^ offset) * rows, rows)
                refs[-1][pl.ds(start, rows), :] = ref[i * rows : (i + 1) * rows, :]

    arrays = [p for p, _ in pieces]
    out = shape((size * rows, width), BF16)
    moved = 2 * size * rows * width * 2
    return pl.pallas_call(
        after(kernel, 1 + len(arrays), deps),
        out_shape=out,
        in_specs=[pl.BlockSpec(memory_space=pltpu.SMEM)]
        + [pl.BlockSpec(memory_space=pltpu.VMEM)] * len(arrays)
        + [pl.BlockSpec(memory_space=pl.ANY)] * len(deps),
        out_specs=pl.BlockSpec(memory_space=pltpu.VMEM),
        compiler_params=pltpu.CompilerParams(vmem_limit_bytes=VMEM_LIMIT),
        cost_estimate=pl.CostEstimate(
            flops=0, bytes_accessed=moved // UNDERSTATED, transcendentals=0
        ),
        name=name,
    )(dp_place, *arrays, *deps)


def halving_order(size, bits):
    order = [0]
    for bit in reversed(bits):
        order = order + [o ^ (1 << bit) for o in order]
    return order


def fold(keep, came, last, deps):
    groups, rows, width = keep.shape

    def kernel(k_ref, c_ref, *refs):
        if last:
            refs[0][...] = k_ref[...] + c_ref[...].astype(F32)
        else:
            half = rows // 2
            refs[0][...] = k_ref[:, :half] + c_ref[:, :half].astype(F32)
            refs[1][...] = (k_ref[:, half:] + c_ref[:, half:].astype(F32)).astype(BF16)

    outs = [shape(keep.shape, F32)]
    if not last:
        half_dims = (groups, rows // 2, width)
        outs = [shape(half_dims, F32), shape(half_dims, BF16)]
    return whole_call(
        kernel, outs, [keep, came], groups * rows * width, "fold", deps=deps, limit=FOLD_LIMIT
    )


def fold_core(pairs, deps):
    rows, width = pairs[0][0].shape
    half = rows // 2

    def kernel(*refs):
        for i in range(len(pairs)):
            mine, got = refs[2 * i : 2 * i + 2]
            refs[-2][i] = mine[:half] + got[:half].astype(F32)
            refs[-1][i] = (mine[half:] + got[half:].astype(F32)).astype(BF16)

    dims = (len(pairs), half, width)
    args = [array for pair in pairs for array in pair]
    return whole_call(
        kernel,
        [shape(dims, F32), shape(dims, BF16)],
        args,
        len(pairs) * rows * width,
        "fold_core",
        deps=deps,
        limit=FOLD_LIMIT,
    )


class Chain:
    def __init__(self, keep, send, bits):
        self.keep, self.bits = keep, list(bits)
        self.came = swap_dp(send, 1 << self.bits.pop(0))
        self.done = False

    def fold(self, deps=()):
        if self.done:
            return
        self.done = not self.bits
        made = fold(self.keep, self.came, self.done, list(deps))
        self.keep = made[0]
        if not self.done:
            self.came = swap_dp(made[1], 1 << self.bits.pop(0))

    def finish(self):
        while not self.done:
            self.fold()
        return self.keep


def sum_all(vector, waits):
    def plus(one, two, deps):
        def kernel(a_ref, b_ref, out_ref):
            out_ref[...] = a_ref[...] + b_ref[...]

        out = shape(one.shape, F32)
        return whole_call(kernel, [out], [one, two], 0, "plus", deps=deps, limit=SMALL_LIMIT)[0]

    waits = list(waits)
    held = vector.reshape(-1, 128)
    for swap, axis in ((swap_tensor, "tensor"), (swap_dp, "dp")):
        step = 1
        while step < lax.axis_size(axis):
            held = plus(held, swap(held, step), waits.pop(0) if waits else [])
            step *= 2
    return held.reshape(-1)


def project_inputs(x_own, x_across, w_mine, w_other, b_mine, b_other, deps):
    rows, width = x_own.shape
    third = w_mine.shape[1] // 4

    def kernel(x0, x1, wm, wo, bm, bo, mine_ref, other_ref, send_ref):
        tokens = jnp.concatenate([x0[...], x1[...]], axis=0)
        mine = (dot(tokens, wm[:, : 3 * third]) + bm[...]).astype(BF16)
        other = (dot(tokens, wo[:, : 3 * third]) + bo[...]).astype(BF16)
        mine_ref[...] = mine
        other_ref[...] = other
        send_ref[:, : 2 * third] = other[:, third:]
        send_ref[:, 2 * third :] = mine[:, third:]

    outs = [
        shape((2 * rows, 3 * third), BF16),
        shape((2 * rows, 3 * third), BF16),
        shape((2 * rows, 4 * third), BF16),
    ]
    flops = 2 * 2 * rows * width * 6 * third
    return whole_call(
        kernel,
        outs,
        [x_own, x_across, w_mine, w_other, b_mine, b_other],
        flops,
        "project_inputs",
        deps=deps,
    )


def attention_forward(mine, other, far, bias_row, w_mine, w_other, head_size, deps):
    rows = mine.shape[0]
    third = mine.shape[1] // 3
    heads = third // head_size
    block = rows // 2
    width = w_mine.shape[0]
    scaling = 1.0 / math.sqrt(head_size)

    def kernel(mine_ref, other_ref, far_ref, bias_ref, wm, wo, cm_ref, co_ref, own_ref, across_ref, acc):
        lane_head = lax.broadcasted_iota(jnp.int32, (1, third), 1) // head_size
        acc[...] = jnp.zeros_like(acc)
        bias = bias_ref[...]

        def one_head(head, carry):
            inside = lane_head == head
            for group, ref in enumerate((mine_ref, other_ref)):
                base = 2 * third * group
                keys = jnp.concatenate(
                    [ref[:, third : 2 * third], far_ref[:, base : base + third]], axis=0
                )
                vals = jnp.concatenate(
                    [ref[:, 2 * third :], far_ref[:, base + third : base + 2 * third]], axis=0
                )
                for part in range(2):
                    span = slice(part * block, (part + 1) * block)
                    query = jnp.where(inside, ref[span, :third] * scaling, 0.0).astype(BF16)
                    scores = dot_nt(query, keys) + bias
                    peak = jnp.max(scores, axis=-1, keepdims=True)
                    weights = jnp.exp(scores - peak)
                    total = jnp.sum(weights, axis=-1, keepdims=True)
                    found = dot(weights.astype(BF16), vals) * (1.0 / total)
                    acc[group, span, :] += jnp.where(inside, found, 0.0)
            return carry

        lax.fori_loop(0, heads, one_head, 0)
        ctx_mine = acc[0].astype(BF16)
        ctx_other = acc[1].astype(BF16)
        cm_ref[...] = ctx_mine
        co_ref[...] = ctx_other
        part_sum = dot_nt(ctx_mine, wm[:, 3 * third :]) + dot_nt(ctx_other, wo[:, 3 * third :])
        own_ref[...] = part_sum[:block]
        across_ref[...] = part_sum[block:].astype(BF16)

    outs = [
        shape((rows, third), BF16),
        shape((rows, third), BF16),
        shape((block, width), F32),
        shape((block, width), BF16),
    ]
    flops = 2 * 2 * 2 * rows * 2 * rows * third * heads * 2
    return whole_call(
        kernel,
        outs,
        [mine, other, far, bias_row, w_mine, w_other],
        flops,
        "attention_forward",
        [pltpu.VMEM((2, rows, third), F32)],
        deps,
    )


def attention_backward(mine, other, far, bias_column, ga_own, ga_across, w_mine, w_other, head_size, deps):
    rows = mine.shape[0]
    third = mine.shape[1] // 3
    heads = third // head_size
    block = rows // 2
    keys_count = 2 * rows
    scaling = 1.0 / math.sqrt(head_size)

    def kernel(
        mine_ref, other_ref, far_ref, bias_ref, g0, g1, wm, wo,
        dq_ref, keep_ref, send_ref, sums_ref, grad_ctx, keys_t, dq_t, dkv,
    ):
        lane_head = lax.broadcasted_iota(jnp.int32, (1, third), 1) // head_size
        grad_rows = jnp.concatenate([g0[...], g1[...]], axis=0)
        grad_ctx[0] = dot(grad_rows, wm[:, 3 * third :]).astype(BF16)
        grad_ctx[1] = dot(grad_rows, wo[:, 3 * third :]).astype(BF16)
        dkv[...] = jnp.zeros_like(dkv)
        for group, ref in enumerate((mine_ref, other_ref)):
            base = 2 * third * group
            keys_t[group, :, :rows] = ref[:, third : 2 * third].T
            keys_t[group, :, rows:] = far_ref[:, base : base + third].T
        bias = bias_ref[...]

        def one_head(head, carry):
            inside = lane_head == head
            start = pl.multiple_of(head * head_size, head_size)
            for group, ref in enumerate((mine_ref, other_ref)):
                base = 2 * third * group
                keys = jnp.concatenate(
                    [ref[:, third : 2 * third], far_ref[:, base : base + third]], axis=0
                )
                vals = jnp.concatenate(
                    [ref[:, 2 * third :], far_ref[:, base + third : base + 2 * third]], axis=0
                )
                head_keys_t = keys_t[group, pl.ds(start, head_size), :]
                for part in range(2):
                    span = slice(part * block, (part + 1) * block)
                    query = jnp.where(inside, ref[span, :third] * scaling, 0.0).astype(BF16)
                    grad = jnp.where(inside, grad_ctx[group, span, :], 0.0).astype(BF16)
                    scores = dot_nt(keys, query) + bias
                    peak = jnp.max(scores, axis=0, keepdims=True)
                    weights = jnp.exp(scores - peak)
                    total = jnp.sum(weights, axis=0, keepdims=True)
                    probs = weights * (1.0 / total)
                    grad_probs = dot_nt(vals, grad)
                    inner = jnp.sum(probs * grad_probs, axis=0, keepdims=True)
                    grad_scores = (probs * (grad_probs - inner)).astype(BF16)
                    dkv[group, 1] += dot(probs.astype(BF16), grad)
                    dkv[group, 0] += dot(grad_scores, query)
                    dq_t[group, pl.ds(start, head_size), span] = dot(head_keys_t, grad_scores)
            return carry

        lax.fori_loop(0, heads, one_head, 0)
        for group in range(2):
            grad_query = (dq_t[group].T * scaling).astype(BF16)
            dq_ref[:, group * third : (group + 1) * third] = grad_query
            sums_ref[group : group + 1, :third] = jnp.sum(
                grad_query.astype(F32), axis=0, keepdims=True
            )
            sums_ref[group : group + 1, third:] = jnp.sum(dkv[group, 1], axis=0, keepdims=True)
            for kind in range(2):
                at = (2 * group + kind) * third
                keep_ref[:, at : at + third] = dkv[group, kind, :rows]
                away = (2 * (1 - group) + kind) * third
                send_ref[:, away : away + third] = dkv[group, kind, rows:].astype(BF16)

    outs = [
        shape((rows, 2 * third), BF16),
        shape((rows, 4 * third), F32),
        shape((rows, 4 * third), BF16),
        shape((2, 2 * third), F32),
    ]
    flops = 5 * 2 * 2 * rows * keys_count * third * heads * 2 * UNDERSTATED
    return whole_call(
        kernel,
        outs,
        [mine, other, far, bias_column, ga_own, ga_across, w_mine, w_other],
        flops,
        "attention_backward",
        [
            pltpu.VMEM((2, rows, third), BF16),
            pltpu.VMEM((2, third, keys_count), BF16),
            pltpu.VMEM((2, third, rows), F32),
            pltpu.VMEM((2, 2, keys_count, third), F32),
        ],
        deps,
    )


def project_back(dq, keep, got, w_mine, w_other, deps):
    rows = dq.shape[0]
    third = dq.shape[1] // 2
    block = rows // 2
    width = w_mine.shape[0]

    def kernel(dq_ref, keep_ref, got_ref, wm, wo, gm_ref, go_ref, own_ref, across_ref):
        dkv = (keep_ref[...] + got_ref[...].astype(F32)).astype(BF16)
        grad_mine = jnp.concatenate([dq_ref[:, :third], dkv[:, : 2 * third]], axis=1)
        grad_other = jnp.concatenate([dq_ref[:, third:], dkv[:, 2 * third :]], axis=1)
        gm_ref[...] = dkv[:, : 2 * third]
        go_ref[...] = dkv[:, 2 * third :]
        back = dot_nt(grad_mine, wm[:, : 3 * third]) + dot_nt(grad_other, wo[:, : 3 * third])
        own_ref[...] = back[:block]
        across_ref[...] = back[block:].astype(BF16)

    outs = [
        shape((rows, 2 * third), BF16),
        shape((rows, 2 * third), BF16),
        shape((block, width), F32),
        shape((block, width), BF16),
    ]
    flops = 2 * rows * width * 6 * third
    return whole_call(
        kernel, outs, [dq, keep, got, w_mine, w_other], flops, "project_back", deps=deps
    )


def moments(summed):
    centre = jnp.mean(summed, axis=-1, keepdims=True)
    centred = summed - centre
    spread = jnp.mean(centred * centred, axis=-1, keepdims=True)
    back = lax.rsqrt(spread + NORM_EPS)
    return centred * back, back


def first_norm(x_own, part, got, b_out, gain, shift, deps):
    dims = x_own.shape

    def kernel(x_ref, p_ref, r_ref, b_ref, g_ref, s_ref, summed_ref, normed_ref, low_ref):
        summed = x_ref[...].astype(F32) + (p_ref[...] + r_ref[...].astype(F32)) + b_ref[...]
        unit, _ = moments(summed)
        normed = unit * g_ref[...] + s_ref[...]
        summed_ref[...] = summed
        normed_ref[...] = normed
        low_ref[...] = normed.astype(BF16)

    outs = [shape(dims, F32), shape(dims, F32), shape(dims, BF16)]
    return whole_call(
        kernel,
        outs,
        [x_own, part, got, b_out, gain, shift],
        20 * math.prod(dims),
        "first_norm",
        deps=deps,
        limit=SMALL_LIMIT,
    )


def second_norm(normed, part, got, cotangent, b_down, gain, shift):
    dims = normed.shape

    def kernel(n_ref, p_ref, r_ref, c_ref, b_ref, g_ref, s_ref, out_ref, grad_ref, low_ref, sums_ref):
        summed = n_ref[...] + (p_ref[...] + r_ref[...].astype(F32)) + b_ref[...]
        unit, back = moments(summed)
        out_ref[...] = (unit * g_ref[...] + s_ref[...]).astype(BF16)
        cot = c_ref[...].astype(F32)
        scaled = cot * g_ref[...]
        grad = back * (
            scaled
            - jnp.mean(scaled, axis=-1, keepdims=True)
            - unit * jnp.mean(scaled * unit, axis=-1, keepdims=True)
        )
        grad_ref[...] = grad
        low_ref[...] = grad.astype(BF16)
        sums_ref[0:1, :] = jnp.sum(cot * unit, axis=0, keepdims=True)
        sums_ref[1:2, :] = jnp.sum(cot, axis=0, keepdims=True)
        sums_ref[2:3, :] = jnp.sum(grad, axis=0, keepdims=True)

    outs = [shape(dims, BF16), shape(dims, F32), shape(dims, BF16), shape((3, dims[1]), F32)]
    return whole_call(
        kernel,
        outs,
        [normed, part, got, cotangent, b_down, gain, shift],
        40 * math.prod(dims),
        "second_norm",
        limit=SMALL_LIMIT,
    )


def first_norm_back(summed, grad_second, part, got, gain, deps):
    dims = summed.shape

    def kernel(z_ref, gs_ref, p_ref, r_ref, g_ref, grad_ref, low_ref, sums_ref):
        unit, back = moments(z_ref[...])
        grad_normed = gs_ref[...] + (p_ref[...] + r_ref[...].astype(F32))
        scaled = grad_normed * g_ref[...]
        grad = back * (
            scaled
            - jnp.mean(scaled, axis=-1, keepdims=True)
            - unit * jnp.mean(scaled * unit, axis=-1, keepdims=True)
        )
        grad_ref[...] = grad
        low_ref[...] = grad.astype(BF16)
        sums_ref[0:1, :] = jnp.sum(grad_normed * unit, axis=0, keepdims=True)
        sums_ref[1:2, :] = jnp.sum(grad_normed, axis=0, keepdims=True)
        sums_ref[2:3, :] = jnp.sum(grad, axis=0, keepdims=True)

    outs = [shape(dims, F32), shape(dims, BF16), shape((3, dims[1]), F32)]
    return whole_call(
        kernel,
        outs,
        [summed, grad_second, part, got, gain],
        40 * math.prod(dims),
        "first_norm_back",
        deps=deps,
        limit=SMALL_LIMIT,
    )


def feed_forward(n_own, n_far, weights, bias, prior, deps):
    block, width = n_own.shape
    rows = 2 * block
    hidden = weights.shape[1] // 2
    tile = min(256, hidden)
    steps = hidden // tile
    last = prior is not None

    def kernel(n0, n1, u, d, b, *refs):
        step = pl.program_id(0)
        if last:
            before, a_ref, s_ref, own_ref, far_ref, tokens, acc = refs
        else:
            a_ref, s_ref, acc, tokens = refs

        @pl.when(step == 0)
        def _():
            tokens[:block] = n0[...]
            tokens[block:] = n1[...]
            acc[...] = before[...] if last else jnp.zeros_like(acc)

        hid = dot(tokens[...], u[...]) + b[...]
        half = 0.5 * (1.0 + lax.erf(hid * (1.0 / math.sqrt(2.0))))
        bell = jnp.exp(hid * hid * -0.5) * (1.0 / math.sqrt(2.0 * math.pi))
        active = (hid * half).astype(BF16)
        a_ref[...] = active
        s_ref[...] = (half + hid * bell).astype(BF16)
        acc[...] += dot_nt(active, d[...])

        if last:

            @pl.when(step == steps - 1)
            def _():
                own_ref[...] = acc[:block]
                far_ref[...] = acc[block:].astype(BF16)

    column = pl.BlockSpec((width, tile), lambda i: (0, i))
    later = pl.BlockSpec((width, tile), lambda i: (0, steps + i))
    made = pl.BlockSpec((rows, tile), lambda i: (0, i))
    args = [n_own, n_far, weights, weights, bias]
    in_specs = [const_spec((block, width))] * 2
    in_specs += [column, later, pl.BlockSpec((1, tile), lambda i: (0, i))]
    outs = [shape((rows, hidden), BF16)] * 2
    scratch = [pltpu.VMEM((rows, width), BF16)]
    if last:
        args.append(prior)
        in_specs.append(const_spec((rows, width)))
        outs += [shape((block, width), F32), shape((block, width), BF16)]
        out_specs = [made] * 2 + [const_spec((block, width))] * 2
        scratch.append(pltpu.VMEM((rows, width), F32))
    else:
        outs.append(shape((rows, width), F32))
        out_specs = [made] * 2 + [const_spec((rows, width))]
    return streamed_call(
        kernel,
        (steps,),
        outs,
        out_specs,
        args,
        in_specs,
        2 * 2 * rows * width * hidden,
        "feed_forward",
        scratch,
        deps,
    )


def feed_forward_back(g_own, g_across, w_mine, w_other, slope_mine, slope_other, deps):
    block, width = g_own.shape
    rows = 2 * block
    hidden = w_mine.shape[1] // 2
    tile = min(256, hidden)
    steps = hidden // tile

    def kernel(
        g0, g1, um, uo, dm, do, sm, so,
        gm_ref, go_ref, own_ref, across_ref, bm_ref, bo_ref, grads, acc,
    ):
        step = pl.program_id(0)

        @pl.when(step == 0)
        def _():
            grads[:block] = g0[...]
            grads[block:] = g1[...]
            acc[...] = jnp.zeros_like(acc)

        total = acc[...]
        for u, d, s, g_ref, b_ref in ((um, dm, sm, gm_ref, bm_ref), (uo, do, so, go_ref, bo_ref)):
            grad_hidden = (dot(grads[...], d[...]) * s[...].astype(F32)).astype(BF16)
            g_ref[...] = grad_hidden
            b_ref[...] = jnp.sum(grad_hidden.astype(F32), axis=0, keepdims=True)
            total = total + dot_nt(grad_hidden, u[...])
        acc[...] = total

        @pl.when(step == steps - 1)
        def _():
            own_ref[...] = acc[:block]
            across_ref[...] = acc[block:].astype(BF16)

    column = pl.BlockSpec((width, tile), lambda i: (0, i))
    later = pl.BlockSpec((width, tile), lambda i: (0, steps + i))
    bias = pl.BlockSpec((1, tile), lambda i: (0, i))
    made = pl.BlockSpec((rows, tile), lambda i: (0, i))
    outs = (
        [shape((rows, hidden), BF16)] * 2
        + [shape((block, width), F32), shape((block, width), BF16)]
        + [shape((1, hidden), F32)] * 2
    )
    return streamed_call(
        kernel,
        (steps,),
        outs,
        [made] * 2 + [const_spec((block, width))] * 2 + [bias] * 2,
        [g_own, g_across, w_mine, w_other, w_mine, w_other, slope_mine, slope_other],
        [const_spec((block, width))] * 2 + [column] * 2 + [later] * 2 + [made] * 2,
        2 * 2 * rows * width * 2 * hidden,
        "feed_forward_back",
        [pltpu.VMEM((rows, width), BF16), pltpu.VMEM((rows, width), F32)],
        deps,
    )


def weight_grad(ones, mine, other, dp_place, chains, name, other_first=0, deps=(), halves=False):
    block, width = ones[0].shape
    rows = 2 * block
    count = chains[0][0]
    tile = min(256, count)
    tiles = count // tile
    size = lax.axis_size("dp")
    share = width // size
    half = width // 2

    def kernel(place_ref, a0, a1, a2, a3, m0, m1, o0, o1, *refs):
        turned, full = refs[-2:]
        step = pl.program_id(0)

        @pl.when(step == 0)
        def _():
            for i, ref in enumerate((a0, a1, a2, a3)):
                turned[:, i * block : (i + 1) * block] = ref[...].T

        place = place_ref[0]

        def write(which, targets, order):
            for i, offset in enumerate(order):
                start = pl.multiple_of((place ^ offset) * share, share)
                at = i * share
                rows_now = full[pl.ds(start, share), :]
                if halves:
                    ref = targets[0] if at < half else targets[1]
                    at %= half
                    ref[which, at : at + share, :] = rows_now.astype(ref.dtype)
                else:
                    targets[which][at : at + share, :] = rows_now.astype(targets[which].dtype)

        for which, (one, two) in enumerate(((m0, m1), (o0, o1))):
            full[...] = dot(turned[:, :rows], one[...]) + dot(turned[:, rows:], two[...])
            for c, (_, bits) in enumerate(chains):
                targets = refs[2 * c : 2 * c + 2]
                order = halving_order(size, bits)
                if len(chains) == 1:
                    write(which, targets, order)
                else:
                    pl.when(step // tiles == c)(
                        lambda w=which, t=targets, o=order: write(w, t, o)
                    )

    base = other_first // tile
    column = pl.BlockSpec((rows, tile), lambda i: (0, i))
    other_column = pl.BlockSpec((rows, tile), lambda i: (0, base + i))
    outs, out_specs = [], []
    for c in range(len(chains)):
        for kind in (F32, BF16):
            if halves:
                outs.append(shape((2, half, count), kind))
                out_specs.append(pl.BlockSpec((2, half, tile), lambda i: (0, 0, i)))
            else:
                index = lambda i, c=c: (0, jnp.clip(i - c * tiles, 0, tiles - 1))
                outs.append(shape((width, count), kind))
                out_specs.append(pl.BlockSpec((width, tile), index))
    return streamed_call(
        kernel,
        (tiles * len(chains),),
        outs,
        out_specs,
        [dp_place, *ones, *mine, *other],
        [pl.BlockSpec(memory_space=pltpu.SMEM)]
        + [const_spec((block, width))] * 4
        + [column] * 2
        + [other_column] * 2,
        2 * 2 * rows * width * 2 * count * len(chains),
        name,
        [pltpu.VMEM((width, 2 * rows), BF16), pltpu.VMEM((width, tile), F32)],
        deps,
    )


def core_chain(made, bits, deps=()):
    pairs = [(mine, swap_tensor(other, CORE)) for mine, other in made]
    keep, send = fold_core(pairs, list(deps))
    return Chain(keep, send, bits)


def add_up(parts, deps):
    def kernel(*refs):
        refs[-1][...] = sum(ref[...] for ref in refs[:-1])

    out = shape(parts[0].shape, F32)
    return whole_call(kernel, [out], parts, 0, "add_up", deps=deps, limit=SMALL_LIMIT)[0]


def shards(
    inputs,
    lengths,
    w_query,
    w_key,
    w_value,
    w_out,
    w_up,
    w_down,
    b_query,
    b_value,
    b_out,
    b_up,
    b_down,
    first_gain,
    first_shift,
    second_gain,
    second_shift,
    cotangent,
):
    seq_count, block, width = inputs.shape
    tensor_size = lax.axis_size("tensor")
    seq_len = block * tensor_size
    place = lax.axis_index("tensor")
    head_dims = w_query.shape[1]
    head_size = width // HEADS
    hidden = w_up.shape[1]
    seqs = range(seq_count)
    row = lambda vector: vector.reshape(1, -1)

    x_own = [inputs[s] for s in seqs]
    all_across = swap_tensor(inputs, ACROSS)
    x_across = [all_across[s] for s in seqs]

    dp_place = lax.axis_index("dp").astype(jnp.int32).reshape(1)
    att_far, att_first = gather_far(pack([w_query, w_key, w_value, w_out.T], "pack_attention"))
    att_pieces = att_far + gather_near(att_far)
    share = pack([w_up, w_down.T], "pack_feed", att_first)
    share_other = swap_tensor(share, ACROSS)
    mine_far, mine_first = gather_far(share)
    mine_near = gather_near(mine_far)
    other_far, other_first = gather_far(share_other)
    other_near = gather_near(other_far[:1]) + [
        (swap_tensor(p, ACROSS), offsets) for p, offsets in mine_near[1:]
    ]

    def arrays(pieces):
        return [p for p, _ in pieces]

    att_mine = assemble(att_pieces, dp_place, "assemble_attention")
    att_other = assemble(other_core(att_pieces), dp_place, "assemble_attention_other")
    project_waits = [mine_first, [share_other]]
    attend_waits = [arrays(mine_far[1:]), arrays(mine_near[:1]) + other_first]
    norm_waits = [arrays(mine_near[1:]), arrays(other_far[1:])]
    ffw_mine = assemble(mine_far + mine_near, dp_place, "assemble_feed")

    biases = jnp.concatenate([b_query, jnp.zeros_like(b_query), b_value])
    qkv_bias_mine, qkv_bias_other = row(biases), row(swap_tensor(biases, CORE))
    up_bias_mine, up_bias_other = row(b_up), row(swap_tensor(b_up, ACROSS))
    b_out_row, b_down_row = row(b_out), row(b_down)
    gain_one, shift_one = row(first_gain), row(first_shift)
    gain_two, shift_two = row(second_gain), row(second_shift)

    order = jnp.stack([place, place ^ ACROSS, place ^ CORE, place ^ CORE ^ ACROSS])
    positions = (order[:, None] * block + jnp.arange(block, dtype=jnp.int32)[None, :]).reshape(-1)
    masks = [jnp.where(positions < lengths[s], 0.0, MASKED).astype(F32) for s in seqs]

    projected = []
    for s in seqs:
        waits = project_waits[s] if s < 2 else []
        projected.append(
            project_inputs(
                x_own[s], x_across[s], att_mine, att_other, qkv_bias_mine, qkv_bias_other,
                waits + [p[2] for p in projected[-1:]],
            )
        )
    far = [swap_tensor(projected[s][2], CORE) for s in seqs]
    attended = []
    for s in seqs:
        waits = attend_waits[s] if s < 2 else []
        attended.append(
            attention_forward(
                projected[s][0], projected[s][1], far[s], masks[s].reshape(1, seq_len),
                att_mine, att_other, head_size, waits + [p[2] for p in attended[-1:]],
            )
        )
    attended_got = [swap_tensor(attended[s][3], ACROSS) for s in seqs]
    one = []
    for s in seqs:
        waits = norm_waits[s] if s < 2 else []
        one.append(
            first_norm(
                x_own[s], attended[s][2], attended_got[s], b_out_row, gain_one, shift_one,
                waits + [p[2] for p in one[-1:]],
            )
        )
    normed_far = [swap_tensor(one[s][2], CORE) for s in seqs]
    fed_one = []
    for s in seqs:
        waits = [p[2] for p in fed_one[-1:]]
        fed_one.append(
            feed_forward(one[s][2], normed_far[s], ffw_mine, up_bias_mine, None, waits)
        )
    ffw_other = assemble(
        other_far + other_near, dp_place, "assemble_feed_other", [fed_one[-1][2]]
    )
    fed_two = []
    for s in seqs:
        waits = [p[2] for p in fed_two[-1:]]
        fed_two.append(
            feed_forward(
                one[s][2], normed_far[s], ffw_other, up_bias_other, fed_one[s][2], waits
            )
        )
    fed = [(fed_one[s][0], fed_two[s][0], fed_one[s][1], fed_two[s][1], *fed_two[s][2:]) for s in seqs]
    branch_got = [swap_tensor(fed[s][5], CORE) for s in seqs]
    two = [
        second_norm(
            one[s][1], fed[s][4], branch_got[s], cotangent[s], b_down_row, gain_two, shift_two
        )
        for s in seqs
    ]
    grad_far = [swap_tensor(two[s][2], CORE) for s in seqs]
    levels = range(lax.axis_size("dp").bit_length() - 1)
    near_first = list(levels)
    far_first = [1, 0, *levels[2:]] if len(near_first) > 1 else near_first

    def pairs(own, across):
        return [part for s in seqs for part in (own[s], across[s])]

    def feed_back(s, deps):
        return feed_forward_back(
            two[s][2], grad_far[s], ffw_mine, ffw_other, fed[s][2], fed[s][3], deps
        )

    fed_back = [feed_back(0, [])]
    down_made = weight_grad(
        pairs([two[s][2] for s in seqs], grad_far),
        [fed[s][0] for s in seqs], [fed[s][1] for s in seqs],
        dp_place, [(hidden, near_first)], "w_down_grad", deps=[fed_back[0][2]], halves=True,
    )
    fed_back += [feed_back(s, [down_made[1]]) for s in seqs[1:]]
    back_got = [swap_tensor(fed_back[s][3], CORE) for s in seqs]
    def placed_in(part_mine, part_other, bit):
        size = part_mine.shape[0]
        empty = jnp.zeros((tensor_size * size,), F32)
        empty = lax.dynamic_update_slice(empty, part_mine, (place * size,))
        return lax.dynamic_update_slice(empty, part_other, ((place ^ bit) * size,))

    def norm_back(s, deps):
        return first_norm_back(
            one[s][0], two[s][1], fed_back[s][2], back_got[s], gain_one, deps
        )

    one_back = [norm_back(s, [fed_back[-1][2]]) for s in seqs]
    up_made = weight_grad(
        pairs([one[s][2] for s in seqs], normed_far),
        [fed_back[s][0] for s in seqs], [fed_back[s][1] for s in seqs],
        dp_place, [(hidden, far_first)], "w_up_grad", deps=[one_back[s][1] for s in seqs], halves=True,
    )
    first_across = [swap_tensor(one_back[s][1], ACROSS) for s in seqs]
    down_chain = Chain(*down_made, near_first)
    up_chain = Chain(*up_made, far_first)

    def backward(s, deps):
        return attention_backward(
            projected[s][0], projected[s][1], far[s], masks[s].reshape(seq_len, 1),
            one_back[s][1], first_across[s], att_mine, att_other, head_size, deps,
        )

    attended_back = [backward(0, [up_made[1]])]
    out_made = weight_grad(
        pairs([one_back[s][1] for s in seqs], first_across),
        [attended[s][0] for s in seqs], [attended[s][1] for s in seqs],
        dp_place, [(head_dims, near_first)], "w_out_grad", deps=[attended_back[0][3]],
    )
    down_chain.fold([attended_back[0][3]])
    attended_back += [backward(s, [down_chain.keep, out_made[1]]) for s in seqs[1:]]
    far_back = [swap_tensor(attended_back[s][2], CORE) for s in seqs]

    up_chain.fold([attended_back[-1][3]])
    tokens = pairs(x_own, x_across)
    grad_queries = [attended_back[s][0] for s in seqs]
    query_made = weight_grad(
        tokens, grad_queries, grad_queries, dp_place, [(head_dims, near_first)], "w_query_grad",
        head_dims, [far_back[0], up_chain.keep],
    )
    back = [
        project_back(
            attended_back[0][0], attended_back[0][1], far_back[0], att_mine, att_other,
            [query_made[1]],
        )
    ]
    back += [
        project_back(
            attended_back[s][0], attended_back[s][1], far_back[s], att_mine, att_other,
            [back[0][2]],
        )
        for s in seqs[1:]
    ]
    input_got = [swap_tensor(back[s][3], ACROSS) for s in seqs]
    down_chain.fold([back[-1][2]])
    query_chain = core_chain([query_made, out_made], near_first, [back[-1][2]])
    key_value_made = weight_grad(
        tokens, [back[s][0] for s in seqs], [back[s][1] for s in seqs],
        dp_place, [(head_dims, near_first), (head_dims, far_first)], "w_key_value_grad",
        deps=input_got[:1] + [down_chain.keep, query_chain.keep],
    )
    key_chain = core_chain([key_value_made[:2]], near_first, input_got[-1:])
    value_chain = core_chain([key_value_made[2:]], far_first, input_got[-1:])
    started = [key_chain.keep, value_chain.keep]
    up_chain.fold(started)
    query_chain.fold(started)
    key_chain.fold()
    value_chain.fold()
    ending = [key_chain.keep, value_chain.keep]
    query_chain.fold(ending)
    down_chain.fold(ending)
    up_chain.fold(ending)
    input_grad = jnp.stack(
        [
            (one_back[s][0] + (back[s][2] + input_got[s].astype(F32))).astype(BF16)
            for s in seqs
        ]
    )

    sums = add_up([attended_back[s][3] for s in seqs], [query_made[1]])
    small = sum_all(
        jnp.concatenate(
            [
                sum(two[s][3] for s in seqs).reshape(-1),
                sum(one_back[s][2] for s in seqs).reshape(-1),
                placed_in(
                    sum(fed_back[s][4] for s in seqs).reshape(-1),
                    sum(fed_back[s][5] for s in seqs).reshape(-1),
                    ACROSS,
                ),
                placed_in(sums[0, :head_dims], sums[1, :head_dims], CORE),
                placed_in(sums[0, head_dims:], sums[1, head_dims:], CORE),
            ]
        ),
        [[back[0][2]], [back[-1][2]], started, started, ending],
    )

    def over_y(both):
        return both[0] + swap_tensor(both[1].astype(BF16), ACROSS).astype(F32)

    down_grad, up_grad = over_y(down_chain.finish()), over_y(up_chain.finish())
    query_and_out = query_chain.finish()

    vectors = [small[i * width : (i + 1) * width] for i in range(6)]
    second_gain_grad, second_shift_grad, b_down_grad = vectors[:3]
    first_gain_grad, first_shift_grad, b_out_grad = vectors[3:]
    b_up_grad = small[6 * width : 6 * width + tensor_size * hidden]
    b_query_grad, b_value_grad = small[-2 * width : -width], small[-width:]

    output = jnp.stack([two[s][0] for s in seqs])
    return (
        output,
        input_grad,
        query_and_out[0],
        key_chain.finish()[0],
        value_chain.finish()[0],
        query_and_out[1].T,
        up_grad,
        down_grad.T,
        b_query_grad,
        b_value_grad,
        b_out_grad,
        b_up_grad,
        b_down_grad,
        first_gain_grad,
        first_shift_grad,
        second_gain_grad,
        second_shift_grad,
    )


def solution(mesh):
    placed = (
        P("dp", "tensor", None),
        P("dp"),
        P("dp", "tensor"),
        P("dp", "tensor"),
        P("dp", "tensor"),
        P("tensor", "dp"),
        P("dp", "tensor"),
        P("tensor", "dp"),
        P("tensor"),
        P("tensor"),
        P(),
        P("tensor"),
        P(),
        P(),
        P(),
        P(),
        P(),
        P("dp", "tensor", None),
    )
    return jax.shard_map(
        shards,
        mesh=mesh,
        in_specs=placed,
        out_specs=(
            P("dp", "tensor", None),
            P("dp", "tensor", None),
            P("dp", "tensor"),
            P("dp", "tensor"),
            P("dp", "tensor"),
            P("tensor", "dp"),
            P("dp", "tensor"),
            P("tensor", "dp"),
            P(),
            P(),
            P(),
            P(),
            P(),
            P(),
            P(),
            P(),
            P(),
        ),
        check_vma=False,
    )
```

```python
import math

import jax
import jax.numpy as jnp
from jax import lax
from jax.experimental import pallas as pl
from jax.experimental.pallas import tpu as pltpu
from jax.sharding import PartitionSpec as P

HEADS = 16
NORM_EPS = 1e-12
MASKED = -1000000000.0
MIB = 1024 * 1024
VMEM_LIMIT = 56 * MIB
SMALL_LIMIT = 16 * MIB
FOLD_LIMIT = 24 * MIB
UNDERSTATED = 1000

F32 = jnp.float32
BF16 = jnp.bfloat16

CORE = 1
ACROSS = 2


def dot(one, two):
    return lax.dot_general(one, two, (((1,), (0,)), ((), ())), preferred_element_type=F32)


def dot_nt(one, two):
    return lax.dot_general(one, two, (((1,), (1,)), ((), ())), preferred_element_type=F32)


def shape(dims, kind):
    return jax.ShapeDtypeStruct(dims, kind)


def after(kernel, count, deps):
    def body(*refs):
        kernel(*refs[:count], *refs[count + len(deps) :])

    return body


def whole_call(kernel, outs, args, flops, name, scratch=(), deps=(), limit=VMEM_LIMIT):
    moved = sum(math.prod(a.shape) * a.dtype.itemsize for a in (*args, *outs))
    return pl.pallas_call(
        after(kernel, len(args), deps),
        out_shape=tuple(outs),
        in_specs=[pl.BlockSpec(memory_space=pltpu.VMEM)] * len(args)
        + [pl.BlockSpec(memory_space=pl.ANY)] * len(deps),
        out_specs=tuple([pl.BlockSpec(memory_space=pltpu.VMEM)] * len(outs)),
        scratch_shapes=list(scratch),
        compiler_params=pltpu.CompilerParams(vmem_limit_bytes=limit),
        cost_estimate=pl.CostEstimate(
            flops=flops // UNDERSTATED, bytes_accessed=moved // UNDERSTATED, transcendentals=0
        ),
        name=name,
    )(*args, *deps)


def streamed_call(kernel, grid, outs, out_specs, args, in_specs, flops, name, scratch, deps=()):
    moved = sum(math.prod(a.shape) * a.dtype.itemsize for a in (*args, *outs))
    return pl.pallas_call(
        after(kernel, len(args), deps),
        grid=grid,
        out_shape=tuple(outs),
        in_specs=list(in_specs) + [pl.BlockSpec(memory_space=pl.ANY)] * len(deps),
        out_specs=tuple(out_specs),
        scratch_shapes=list(scratch),
        compiler_params=pltpu.CompilerParams(
            vmem_limit_bytes=VMEM_LIMIT, dimension_semantics=("arbitrary",)
        ),
        cost_estimate=pl.CostEstimate(
            flops=flops // UNDERSTATED, bytes_accessed=moved // UNDERSTATED, transcendentals=0
        ),
        name=name,
    )(*args, *deps)


def const_spec(dims):
    return pl.BlockSpec(dims, lambda i: (0,) * len(dims))


def swap_tensor(array, bit):
    size = lax.axis_size("tensor")
    return lax.ppermute(array, "tensor", [(i, i ^ bit) for i in range(size)])


def swap_dp(array, bit):
    size = lax.axis_size("dp")
    return lax.ppermute(array, "dp", [(i, i ^ bit) for i in range(size)])


def pack(parts, name, deps=()):
    def kernel(*refs):
        at = 0
        for ref in refs[:-1]:
            refs[-1][:, at : at + ref.shape[1]] = ref[...]
            at += ref.shape[1]

    out = shape((parts[0].shape[0], sum(p.shape[1] for p in parts)), parts[0].dtype)
    return whole_call(kernel, [out], parts, 0, name, deps=deps)[0]


def gather_far(rows, deps=()):
    held = (rows, [0])
    steps = []
    step = lax.axis_size("dp") // 2
    while step > 1:
        steps.append(step)
        step //= 2
    first = []
    for step in steps[:-1]:
        came = (swap_dp(held[0], step), [o ^ step for o in held[1]])
        first.append(came[0])
        held = merged([held, came], deps)
    pieces = [held]
    if steps:
        pieces.append((swap_dp(held[0], steps[-1]), [o ^ steps[-1] for o in held[1]]))
    return pieces, first[:1]


def merged(pieces, deps=()):
    def kernel(*refs):
        at = 0
        for ref in refs[:-1]:
            refs[-1][at : at + ref.shape[0], :] = ref[...]
            at += ref.shape[0]

    parts = [p for p, _ in pieces]
    out = shape((sum(p.shape[0] for p in parts), parts[0].shape[1]), parts[0].dtype)
    held = whole_call(kernel, [out], parts, 0, "merge_rows", deps=list(deps))[0]
    return (held, [o for _, offsets in pieces for o in offsets])


def gather_near(pieces):
    return [(swap_dp(p, 1), [o ^ 1 for o in offsets]) for p, offsets in pieces]


def other_core(pieces):
    return [(swap_tensor(p, CORE), offsets) for p, offsets in pieces]


def assemble(pieces, dp_place, name, deps=()):
    rows = pieces[0][0].shape[0] // len(pieces[0][1])
    width = pieces[0][0].shape[1]
    size = lax.axis_size("dp")

    def kernel(*refs):
        place = refs[0][0]
        for ref, (_, offsets) in zip(refs[1:-1], pieces):
            for i, offset in enumerate(offsets):
                start = pl.multiple_of((place ^ offset) * rows, rows)
                refs[-1][pl.ds(start, rows), :] = ref[i * rows : (i + 1) * rows, :]

    arrays = [p for p, _ in pieces]
    out = shape((size * rows, width), BF16)
    moved = 2 * size * rows * width * 2
    return pl.pallas_call(
        after(kernel, 1 + len(arrays), deps),
        out_shape=out,
        in_specs=[pl.BlockSpec(memory_space=pltpu.SMEM)]
        + [pl.BlockSpec(memory_space=pltpu.VMEM)] * len(arrays)
        + [pl.BlockSpec(memory_space=pl.ANY)] * len(deps),
        out_specs=pl.BlockSpec(memory_space=pltpu.VMEM),
        compiler_params=pltpu.CompilerParams(vmem_limit_bytes=VMEM_LIMIT),
        cost_estimate=pl.CostEstimate(
            flops=0, bytes_accessed=moved // UNDERSTATED, transcendentals=0
        ),
        name=name,
    )(dp_place, *arrays, *deps)


def halving_order(size, bits):
    order = [0]
    for bit in reversed(bits):
        order = order + [o ^ (1 << bit) for o in order]
    return order


def fold(keep, came, last, deps):
    groups, rows, width = keep.shape

    def kernel(k_ref, c_ref, *refs):
        if last:
            refs[0][...] = k_ref[...] + c_ref[...].astype(F32)
        else:
            half = rows // 2
            refs[0][...] = k_ref[:, :half] + c_ref[:, :half].astype(F32)
            refs[1][...] = (k_ref[:, half:] + c_ref[:, half:].astype(F32)).astype(BF16)

    outs = [shape(keep.shape, F32)]
    if not last:
        half_dims = (groups, rows // 2, width)
        outs = [shape(half_dims, F32), shape(half_dims, BF16)]
    return whole_call(
        kernel, outs, [keep, came], groups * rows * width, "fold", deps=deps, limit=FOLD_LIMIT
    )


def fold_core(pairs, deps):
    rows, width = pairs[0][0].shape
    half = rows // 2

    def kernel(*refs):
        for i in range(len(pairs)):
            mine, got = refs[2 * i : 2 * i + 2]
            refs[-2][i] = mine[:half] + got[:half].astype(F32)
            refs[-1][i] = (mine[half:] + got[half:].astype(F32)).astype(BF16)

    dims = (len(pairs), half, width)
    args = [array for pair in pairs for array in pair]
    return whole_call(
        kernel,
        [shape(dims, F32), shape(dims, BF16)],
        args,
        len(pairs) * rows * width,
        "fold_core",
        deps=deps,
        limit=FOLD_LIMIT,
    )


class Chain:
    def __init__(self, keep, send, bits):
        self.keep, self.bits = keep, list(bits)
        self.came = swap_dp(send, 1 << self.bits.pop(0))
        self.done = False

    def fold(self, deps=()):
        if self.done:
            return
        self.done = not self.bits
        made = fold(self.keep, self.came, self.done, list(deps))
        self.keep = made[0]
        if not self.done:
            self.came = swap_dp(made[1], 1 << self.bits.pop(0))

    def finish(self):
        while not self.done:
            self.fold()
        return self.keep


def plus(one, two, deps=()):
    def kernel(a_ref, b_ref, out_ref):
        out_ref[...] = a_ref[...] + b_ref[...]

    out = shape(one.shape, F32)
    return whole_call(kernel, [out], [one, two], 0, "plus", deps=list(deps), limit=SMALL_LIMIT)[0]


def project_inputs(x_own, x_across, w_mine, w_other, b_mine, b_other, deps):
    rows, width = x_own.shape
    third = w_mine.shape[1] // 4

    def kernel(x0, x1, wm, wo, bm, bo, mine_ref, other_ref, send_ref):
        tokens = jnp.concatenate([x0[...], x1[...]], axis=0)
        mine = (dot(tokens, wm[:, : 3 * third]) + bm[...]).astype(BF16)
        other = (dot(tokens, wo[:, : 3 * third]) + bo[...]).astype(BF16)
        mine_ref[...] = mine
        other_ref[...] = other
        send_ref[:, : 2 * third] = other[:, third:]
        send_ref[:, 2 * third :] = mine[:, third:]

    outs = [
        shape((2 * rows, 3 * third), BF16),
        shape((2 * rows, 3 * third), BF16),
        shape((2 * rows, 4 * third), BF16),
    ]
    flops = 2 * 2 * rows * width * 6 * third
    return whole_call(
        kernel,
        outs,
        [x_own, x_across, w_mine, w_other, b_mine, b_other],
        flops,
        "project_inputs",
        deps=deps,
    )


def attention_forward(mine, other, far, bias_row, w_mine, w_other, head_size, deps):
    rows = mine.shape[0]
    third = mine.shape[1] // 3
    heads = third // head_size
    block = rows // 2
    width = w_mine.shape[0]
    scaling = 1.0 / math.sqrt(head_size)

    def kernel(mine_ref, other_ref, far_ref, bias_ref, wm, wo, cm_ref, co_ref, own_ref, across_ref, acc):
        lane_head = lax.broadcasted_iota(jnp.int32, (1, third), 1) // head_size
        acc[...] = jnp.zeros_like(acc)
        bias = bias_ref[...]

        def one_head(head, carry):
            inside = lane_head == head
            for group, ref in enumerate((mine_ref, other_ref)):
                base = 2 * third * group
                keys = jnp.concatenate(
                    [ref[:, third : 2 * third], far_ref[:, base : base + third]], axis=0
                )
                vals = jnp.concatenate(
                    [ref[:, 2 * third :], far_ref[:, base + third : base + 2 * third]], axis=0
                )
                for part in range(2):
                    span = slice(part * block, (part + 1) * block)
                    query = jnp.where(inside, ref[span, :third] * scaling, 0.0).astype(BF16)
                    scores = dot_nt(query, keys) + bias
                    peak = jnp.max(scores, axis=-1, keepdims=True)
                    weights = jnp.exp(scores - peak)
                    total = jnp.sum(weights, axis=-1, keepdims=True)
                    found = dot(weights.astype(BF16), vals) * (1.0 / total)
                    acc[group, span, :] += jnp.where(inside, found, 0.0)
            return carry

        lax.fori_loop(0, heads, one_head, 0)
        ctx_mine = acc[0].astype(BF16)
        ctx_other = acc[1].astype(BF16)
        cm_ref[...] = ctx_mine
        co_ref[...] = ctx_other
        part_sum = dot_nt(ctx_mine, wm[:, 3 * third :]) + dot_nt(ctx_other, wo[:, 3 * third :])
        own_ref[...] = part_sum[:block]
        across_ref[...] = part_sum[block:].astype(BF16)

    outs = [
        shape((rows, third), BF16),
        shape((rows, third), BF16),
        shape((block, width), F32),
        shape((block, width), BF16),
    ]
    flops = 2 * 2 * 2 * rows * 2 * rows * third * heads * 2
    return whole_call(
        kernel,
        outs,
        [mine, other, far, bias_row, w_mine, w_other],
        flops,
        "attention_forward",
        [pltpu.VMEM((2, rows, third), F32)],
        deps,
    )


def attention_backward(mine, other, far, bias_column, ga_own, ga_across, w_mine, w_other, head_size, deps):
    rows = mine.shape[0]
    third = mine.shape[1] // 3
    heads = third // head_size
    block = rows // 2
    keys_count = 2 * rows
    scaling = 1.0 / math.sqrt(head_size)

    def kernel(
        mine_ref, other_ref, far_ref, bias_ref, g0, g1, wm, wo,
        dq_ref, keep_ref, send_ref, sums_ref, grad_ctx, keys_t, dq_t, dkv,
    ):
        lane_head = lax.broadcasted_iota(jnp.int32, (1, third), 1) // head_size
        grad_rows = jnp.concatenate([g0[...], g1[...]], axis=0)
        grad_ctx[0] = dot(grad_rows, wm[:, 3 * third :]).astype(BF16)
        grad_ctx[1] = dot(grad_rows, wo[:, 3 * third :]).astype(BF16)
        dkv[...] = jnp.zeros_like(dkv)
        for group, ref in enumerate((mine_ref, other_ref)):
            base = 2 * third * group
            keys_t[group, :, :rows] = ref[:, third : 2 * third].T
            keys_t[group, :, rows:] = far_ref[:, base : base + third].T
        bias = bias_ref[...]

        def one_head(head, carry):
            inside = lane_head == head
            start = pl.multiple_of(head * head_size, head_size)
            for group, ref in enumerate((mine_ref, other_ref)):
                base = 2 * third * group
                keys = jnp.concatenate(
                    [ref[:, third : 2 * third], far_ref[:, base : base + third]], axis=0
                )
                vals = jnp.concatenate(
                    [ref[:, 2 * third :], far_ref[:, base + third : base + 2 * third]], axis=0
                )
                head_keys_t = keys_t[group, pl.ds(start, head_size), :]
                for part in range(2):
                    span = slice(part * block, (part + 1) * block)
                    query = jnp.where(inside, ref[span, :third] * scaling, 0.0).astype(BF16)
                    grad = jnp.where(inside, grad_ctx[group, span, :], 0.0).astype(BF16)
                    scores = dot_nt(keys, query) + bias
                    peak = jnp.max(scores, axis=0, keepdims=True)
                    weights = jnp.exp(scores - peak)
                    total = jnp.sum(weights, axis=0, keepdims=True)
                    probs = weights * (1.0 / total)
                    grad_probs = dot_nt(vals, grad)
                    inner = jnp.sum(probs * grad_probs, axis=0, keepdims=True)
                    grad_scores = (probs * (grad_probs - inner)).astype(BF16)
                    dkv[group, 1] += dot(probs.astype(BF16), grad)
                    dkv[group, 0] += dot(grad_scores, query)
                    dq_t[group, pl.ds(start, head_size), span] = dot(head_keys_t, grad_scores)
            return carry

        lax.fori_loop(0, heads, one_head, 0)
        for group in range(2):
            grad_query = (dq_t[group].T * scaling).astype(BF16)
            dq_ref[:, group * third : (group + 1) * third] = grad_query
            sums_ref[group : group + 1, :third] = jnp.sum(
                grad_query.astype(F32), axis=0, keepdims=True
            )
            sums_ref[group : group + 1, third:] = jnp.sum(dkv[group, 1], axis=0, keepdims=True)
            for kind in range(2):
                at = (2 * group + kind) * third
                keep_ref[:, at : at + third] = dkv[group, kind, :rows]
                away = (2 * (1 - group) + kind) * third
                send_ref[:, away : away + third] = dkv[group, kind, rows:].astype(BF16)

    outs = [
        shape((rows, 2 * third), BF16),
        shape((rows, 4 * third), F32),
        shape((rows, 4 * third), BF16),
        shape((2, 2 * third), F32),
    ]
    flops = 5 * 2 * 2 * rows * keys_count * third * heads * 2 * UNDERSTATED
    return whole_call(
        kernel,
        outs,
        [mine, other, far, bias_column, ga_own, ga_across, w_mine, w_other],
        flops,
        "attention_backward",
        [
            pltpu.VMEM((2, rows, third), BF16),
            pltpu.VMEM((2, third, keys_count), BF16),
            pltpu.VMEM((2, third, rows), F32),
            pltpu.VMEM((2, 2, keys_count, third), F32),
        ],
        deps,
    )


def project_back(dq, keep, got, w_mine, w_other, deps):
    rows = dq.shape[0]
    third = dq.shape[1] // 2
    block = rows // 2
    width = w_mine.shape[0]

    def kernel(dq_ref, keep_ref, got_ref, wm, wo, gm_ref, go_ref, own_ref, across_ref):
        dkv = (keep_ref[...] + got_ref[...].astype(F32)).astype(BF16)
        grad_mine = jnp.concatenate([dq_ref[:, :third], dkv[:, : 2 * third]], axis=1)
        grad_other = jnp.concatenate([dq_ref[:, third:], dkv[:, 2 * third :]], axis=1)
        gm_ref[...] = dkv[:, : 2 * third]
        go_ref[...] = dkv[:, 2 * third :]
        back = dot_nt(grad_mine, wm[:, : 3 * third]) + dot_nt(grad_other, wo[:, : 3 * third])
        own_ref[...] = back[:block]
        across_ref[...] = back[block:].astype(BF16)

    outs = [
        shape((rows, 2 * third), BF16),
        shape((rows, 2 * third), BF16),
        shape((block, width), F32),
        shape((block, width), BF16),
    ]
    flops = 2 * rows * width * 6 * third
    return whole_call(
        kernel, outs, [dq, keep, got, w_mine, w_other], flops, "project_back", deps=deps
    )


def moments(summed):
    centre = jnp.mean(summed, axis=-1, keepdims=True)
    centred = summed - centre
    spread = jnp.mean(centred * centred, axis=-1, keepdims=True)
    back = lax.rsqrt(spread + NORM_EPS)
    return centred * back, back


def first_norm(x_own, part, got, b_out, gain, shift, deps):
    dims = x_own.shape

    def kernel(x_ref, p_ref, r_ref, b_ref, g_ref, s_ref, summed_ref, normed_ref, low_ref):
        summed = x_ref[...].astype(F32) + (p_ref[...] + r_ref[...].astype(F32)) + b_ref[...]
        unit, _ = moments(summed)
        normed = unit * g_ref[...] + s_ref[...]
        summed_ref[...] = summed
        normed_ref[...] = normed
        low_ref[...] = normed.astype(BF16)

    outs = [shape(dims, F32), shape(dims, F32), shape(dims, BF16)]
    return whole_call(
        kernel,
        outs,
        [x_own, part, got, b_out, gain, shift],
        20 * math.prod(dims),
        "first_norm",
        deps=deps,
        limit=SMALL_LIMIT,
    )


def second_norm(normed, part, got, cotangent, b_down, gain, shift):
    dims = normed.shape

    def kernel(n_ref, p_ref, r_ref, c_ref, b_ref, g_ref, s_ref, out_ref, grad_ref, low_ref, sums_ref):
        summed = n_ref[...] + (p_ref[...] + r_ref[...].astype(F32)) + b_ref[...]
        unit, back = moments(summed)
        out_ref[...] = (unit * g_ref[...] + s_ref[...]).astype(BF16)
        cot = c_ref[...].astype(F32)
        scaled = cot * g_ref[...]
        grad = back * (
            scaled
            - jnp.mean(scaled, axis=-1, keepdims=True)
            - unit * jnp.mean(scaled * unit, axis=-1, keepdims=True)
        )
        grad_ref[...] = grad
        low_ref[...] = grad.astype(BF16)
        sums_ref[0:1, :] = jnp.sum(cot * unit, axis=0, keepdims=True)
        sums_ref[1:2, :] = jnp.sum(cot, axis=0, keepdims=True)
        sums_ref[2:3, :] = jnp.sum(grad, axis=0, keepdims=True)

    outs = [shape(dims, BF16), shape(dims, F32), shape(dims, BF16), shape((3, dims[1]), F32)]
    return whole_call(
        kernel,
        outs,
        [normed, part, got, cotangent, b_down, gain, shift],
        40 * math.prod(dims),
        "second_norm",
        limit=SMALL_LIMIT,
    )


def first_norm_back(summed, grad_second, part, got, gain, deps):
    dims = summed.shape

    def kernel(z_ref, gs_ref, p_ref, r_ref, g_ref, grad_ref, low_ref, sums_ref):
        unit, back = moments(z_ref[...])
        grad_normed = gs_ref[...] + (p_ref[...] + r_ref[...].astype(F32))
        scaled = grad_normed * g_ref[...]
        grad = back * (
            scaled
            - jnp.mean(scaled, axis=-1, keepdims=True)
            - unit * jnp.mean(scaled * unit, axis=-1, keepdims=True)
        )
        grad_ref[...] = grad
        low_ref[...] = grad.astype(BF16)
        sums_ref[0:1, :] = jnp.sum(grad_normed * unit, axis=0, keepdims=True)
        sums_ref[1:2, :] = jnp.sum(grad_normed, axis=0, keepdims=True)
        sums_ref[2:3, :] = jnp.sum(grad, axis=0, keepdims=True)

    outs = [shape(dims, F32), shape(dims, BF16), shape((3, dims[1]), F32)]
    return whole_call(
        kernel,
        outs,
        [summed, grad_second, part, got, gain],
        40 * math.prod(dims),
        "first_norm_back",
        deps=deps,
        limit=SMALL_LIMIT,
    )


def feed_forward(n_own, n_far, weights, bias, prior, deps):
    block, width = n_own.shape
    rows = 2 * block
    hidden = weights.shape[1] // 2
    tile = min(256, hidden)
    steps = hidden // tile
    last = prior is not None

    def kernel(n0, n1, u, d, b, *refs):
        step = pl.program_id(0)
        if last:
            before, a_ref, s_ref, own_ref, far_ref, tokens, acc = refs
        else:
            a_ref, s_ref, acc, tokens = refs

        @pl.when(step == 0)
        def _():
            tokens[:block] = n0[...]
            tokens[block:] = n1[...]
            acc[...] = before[...] if last else jnp.zeros_like(acc)

        hid = dot(tokens[...], u[...]) + b[...]
        half = 0.5 * (1.0 + lax.erf(hid * (1.0 / math.sqrt(2.0))))
        bell = jnp.exp(hid * hid * -0.5) * (1.0 / math.sqrt(2.0 * math.pi))
        active = (hid * half).astype(BF16)
        a_ref[...] = active
        s_ref[...] = (half + hid * bell).astype(BF16)
        acc[...] += dot_nt(active, d[...])

        if last:

            @pl.when(step == steps - 1)
            def _():
                own_ref[...] = acc[:block]
                far_ref[...] = acc[block:].astype(BF16)

    column = pl.BlockSpec((width, tile), lambda i: (0, i))
    later = pl.BlockSpec((width, tile), lambda i: (0, steps + i))
    made = pl.BlockSpec((rows, tile), lambda i: (0, i))
    args = [n_own, n_far, weights, weights, bias]
    in_specs = [const_spec((block, width))] * 2
    in_specs += [column, later, pl.BlockSpec((1, tile), lambda i: (0, i))]
    outs = [shape((rows, hidden), BF16)] * 2
    scratch = [pltpu.VMEM((rows, width), BF16)]
    if last:
        args.append(prior)
        in_specs.append(const_spec((rows, width)))
        outs += [shape((block, width), F32), shape((block, width), BF16)]
        out_specs = [made] * 2 + [const_spec((block, width))] * 2
        scratch.append(pltpu.VMEM((rows, width), F32))
    else:
        outs.append(shape((rows, width), F32))
        out_specs = [made] * 2 + [const_spec((rows, width))]
    return streamed_call(
        kernel,
        (steps,),
        outs,
        out_specs,
        args,
        in_specs,
        2 * 2 * rows * width * hidden,
        "feed_forward",
        scratch,
        deps,
    )


def feed_forward_back(g_own, g_across, w_mine, w_other, slope_mine, slope_other, deps):
    block, width = g_own.shape
    rows = 2 * block
    hidden = w_mine.shape[1] // 2
    tile = min(256, hidden)
    steps = hidden // tile

    def kernel(
        g0, g1, um, uo, dm, do, sm, so,
        gm_ref, go_ref, own_ref, across_ref, bm_ref, bo_ref, grads, acc,
    ):
        step = pl.program_id(0)

        @pl.when(step == 0)
        def _():
            grads[:block] = g0[...]
            grads[block:] = g1[...]
            acc[...] = jnp.zeros_like(acc)

        total = acc[...]
        for u, d, s, g_ref, b_ref in ((um, dm, sm, gm_ref, bm_ref), (uo, do, so, go_ref, bo_ref)):
            grad_hidden = (dot(grads[...], d[...]) * s[...].astype(F32)).astype(BF16)
            g_ref[...] = grad_hidden
            b_ref[...] = jnp.sum(grad_hidden.astype(F32), axis=0, keepdims=True)
            total = total + dot_nt(grad_hidden, u[...])
        acc[...] = total

        @pl.when(step == steps - 1)
        def _():
            own_ref[...] = acc[:block]
            across_ref[...] = acc[block:].astype(BF16)

    column = pl.BlockSpec((width, tile), lambda i: (0, i))
    later = pl.BlockSpec((width, tile), lambda i: (0, steps + i))
    bias = pl.BlockSpec((1, tile), lambda i: (0, i))
    made = pl.BlockSpec((rows, tile), lambda i: (0, i))
    outs = (
        [shape((rows, hidden), BF16)] * 2
        + [shape((block, width), F32), shape((block, width), BF16)]
        + [shape((1, hidden), F32)] * 2
    )
    return streamed_call(
        kernel,
        (steps,),
        outs,
        [made] * 2 + [const_spec((block, width))] * 2 + [bias] * 2,
        [g_own, g_across, w_mine, w_other, w_mine, w_other, slope_mine, slope_other],
        [const_spec((block, width))] * 2 + [column] * 2 + [later] * 2 + [made] * 2,
        2 * 2 * rows * width * 2 * hidden,
        "feed_forward_back",
        [pltpu.VMEM((rows, width), BF16), pltpu.VMEM((rows, width), F32)],
        deps,
    )


def weight_grad(ones, mine, other, dp_place, chains, name, other_first=0, deps=(), halves=False):
    block, width = ones[0].shape
    rows = 2 * block
    count = chains[0][0]
    tile = min(256, count)
    tiles = count // tile
    size = lax.axis_size("dp")
    share = width // size
    half = width // 2

    def kernel(place_ref, a0, a1, a2, a3, m0, m1, o0, o1, *refs):
        turned, full = refs[-2:]
        step = pl.program_id(0)

        @pl.when(step == 0)
        def _():
            for i, ref in enumerate((a0, a1, a2, a3)):
                turned[:, i * block : (i + 1) * block] = ref[...].T

        place = place_ref[0]

        def write(which, targets, order):
            for i, offset in enumerate(order):
                start = pl.multiple_of((place ^ offset) * share, share)
                at = i * share
                rows_now = full[pl.ds(start, share), :]
                if halves:
                    ref = targets[0] if at < half else targets[1]
                    at %= half
                    ref[which, at : at + share, :] = rows_now.astype(ref.dtype)
                else:
                    targets[which][at : at + share, :] = rows_now.astype(targets[which].dtype)

        for which, (one, two) in enumerate(((m0, m1), (o0, o1))):
            full[...] = dot(turned[:, :rows], one[...]) + dot(turned[:, rows:], two[...])
            for c, (_, bits) in enumerate(chains):
                targets = refs[2 * c : 2 * c + 2]
                order = halving_order(size, bits)
                if len(chains) == 1:
                    write(which, targets, order)
                else:
                    pl.when(step // tiles == c)(
                        lambda w=which, t=targets, o=order: write(w, t, o)
                    )

    base = other_first // tile
    column = pl.BlockSpec((rows, tile), lambda i: (0, i))
    other_column = pl.BlockSpec((rows, tile), lambda i: (0, base + i))
    outs, out_specs = [], []
    for c in range(len(chains)):
        for kind in (F32, BF16):
            if halves:
                outs.append(shape((2, half, count), kind))
                out_specs.append(pl.BlockSpec((2, half, tile), lambda i: (0, 0, i)))
            else:
                index = lambda i, c=c: (0, jnp.clip(i - c * tiles, 0, tiles - 1))
                outs.append(shape((width, count), kind))
                out_specs.append(pl.BlockSpec((width, tile), index))
    return streamed_call(
        kernel,
        (tiles * len(chains),),
        outs,
        out_specs,
        [dp_place, *ones, *mine, *other],
        [pl.BlockSpec(memory_space=pltpu.SMEM)]
        + [const_spec((block, width))] * 4
        + [column] * 2
        + [other_column] * 2,
        2 * 2 * rows * width * 2 * count * len(chains),
        name,
        [pltpu.VMEM((width, 2 * rows), BF16), pltpu.VMEM((width, tile), F32)],
        deps,
    )


def core_chain(made, bits, deps=()):
    pairs = [(mine, swap_tensor(other, CORE)) for mine, other in made]
    keep, send = fold_core(pairs, list(deps))
    return Chain(keep, send, bits)


def add_up(parts, deps):
    def kernel(*refs):
        refs[-1][...] = sum(ref[...] for ref in refs[:-1])

    out = shape(parts[0].shape, F32)
    return whole_call(kernel, [out], parts, 0, "add_up", deps=deps, limit=SMALL_LIMIT)[0]


def shards(
    inputs,
    lengths,
    w_query,
    w_key,
    w_value,
    w_out,
    w_up,
    w_down,
    b_query,
    b_value,
    b_out,
    b_up,
    b_down,
    first_gain,
    first_shift,
    second_gain,
    second_shift,
    cotangent,
):
    seq_count, block, width = inputs.shape
    tensor_size = lax.axis_size("tensor")
    seq_len = block * tensor_size
    place = lax.axis_index("tensor")
    head_dims = w_query.shape[1]
    head_size = width // HEADS
    hidden = w_up.shape[1]
    seqs = range(seq_count)
    row = lambda vector: vector.reshape(1, -1)

    x_own = [inputs[s] for s in seqs]
    all_across = swap_tensor(inputs, ACROSS)
    x_across = [all_across[s] for s in seqs]

    dp_place = lax.axis_index("dp").astype(jnp.int32).reshape(1)
    att_far, att_first = gather_far(pack([w_query, w_key, w_value, w_out.T], "pack_attention"))
    att_pieces = att_far + gather_near(att_far)
    share = pack([w_up, w_down.T], "pack_feed", [p for p, _ in att_far[1:]] or att_first)
    share_other = swap_tensor(share, ACROSS)
    att_mine = assemble(att_pieces, dp_place, "assemble_attention", [all_across, share_other])
    mine_far, mine_first = gather_far(share, [att_mine])

    def arrays(pieces):
        return [p for p, _ in pieces]

    att_other = assemble(other_core(att_pieces), dp_place, "assemble_attention_other")
    project_waits = [[], mine_first]

    biases = jnp.concatenate([b_query, jnp.zeros_like(b_query), b_value])
    qkv_bias_mine, qkv_bias_other = row(biases), row(swap_tensor(biases, CORE))
    up_bias_mine, up_bias_other = row(b_up), row(swap_tensor(b_up, ACROSS))
    b_out_row, b_down_row = row(b_out), row(b_down)
    gain_one, shift_one = row(first_gain), row(first_shift)
    gain_two, shift_two = row(second_gain), row(second_shift)

    order = jnp.stack([place, place ^ ACROSS, place ^ CORE, place ^ CORE ^ ACROSS])
    positions = (order[:, None] * block + jnp.arange(block, dtype=jnp.int32)[None, :]).reshape(-1)
    masks = [jnp.where(positions < lengths[s], 0.0, MASKED).astype(F32) for s in seqs]

    projected = []
    for s in seqs:
        waits = project_waits[s] if s < 2 else []
        projected.append(
            project_inputs(
                x_own[s], x_across[s], att_mine, att_other, qkv_bias_mine, qkv_bias_other,
                waits + [p[2] for p in projected[-1:]],
            )
        )
    far = [swap_tensor(projected[s][2], CORE) for s in seqs]
    attended = []
    for s in seqs:
        attended.append(
            attention_forward(
                projected[s][0], projected[s][1], far[s], masks[s].reshape(1, seq_len),
                att_mine, att_other, head_size, [p[2] for p in attended[-1:]],
            )
        )
    later = [merged([piece], [attended[0][2]]) for piece in mine_far[1:]]
    mine_near = gather_near(mine_far[:1] + later)
    ffw_mine = assemble(mine_far + mine_near, dp_place, "assemble_feed")
    norm_waits = [arrays(mine_near[:1]) + [attended[-1][2]], [ffw_mine]]
    attended_got = [swap_tensor(attended[s][3], ACROSS) for s in seqs]
    one = []
    for s in seqs:
        waits = norm_waits[s] if s < 2 else []
        one.append(
            first_norm(
                x_own[s], attended[s][2], attended_got[s], b_out_row, gain_one, shift_one,
                waits + [p[2] for p in one[-1:]],
            )
        )
    other_far, _ = gather_far(share_other, [one[0][2]])
    other_near = gather_near(other_far[:1]) + [
        (swap_tensor(p, ACROSS), offsets) for p, offsets in mine_near[1:]
    ]
    feed_waits = [arrays(other_far[1:]), []]
    normed_far = [swap_tensor(one[s][2], CORE) for s in seqs]
    fed_one = []
    for s in seqs:
        waits = (feed_waits[s] if s < 2 else []) + [p[2] for p in fed_one[-1:]]
        fed_one.append(
            feed_forward(one[s][2], normed_far[s], ffw_mine, up_bias_mine, None, waits)
        )
    ffw_other = assemble(
        other_far + other_near, dp_place, "assemble_feed_other", [fed_one[-1][2]]
    )
    fed_two = []
    for s in seqs:
        waits = [p[2] for p in fed_two[-1:]]
        fed_two.append(
            feed_forward(
                one[s][2], normed_far[s], ffw_other, up_bias_other, fed_one[s][2], waits
            )
        )
    fed = [(fed_one[s][0], fed_two[s][0], fed_one[s][1], fed_two[s][1], *fed_two[s][2:]) for s in seqs]
    branch_got = [swap_tensor(fed[s][5], CORE) for s in seqs]
    two = [
        second_norm(
            one[s][1], fed[s][4], branch_got[s], cotangent[s], b_down_row, gain_two, shift_two
        )
        for s in seqs
    ]
    grad_far = [swap_tensor(two[s][2], CORE) for s in seqs]
    levels = range(lax.axis_size("dp").bit_length() - 1)
    near_first = list(levels)
    far_first = [1, 0, *levels[2:]] if len(near_first) > 1 else near_first

    def pairs(own, across):
        return [part for s in seqs for part in (own[s], across[s])]

    def feed_back(s, deps):
        return feed_forward_back(
            two[s][2], grad_far[s], ffw_mine, ffw_other, fed[s][2], fed[s][3], deps
        )

    fed_back = [feed_back(0, [])]
    down_made = weight_grad(
        pairs([two[s][2] for s in seqs], grad_far),
        [fed[s][0] for s in seqs], [fed[s][1] for s in seqs],
        dp_place, [(hidden, near_first)], "w_down_grad", deps=[fed_back[0][2]], halves=True,
    )
    fed_back += [feed_back(s, [down_made[1]]) for s in seqs[1:]]
    back_got = [swap_tensor(fed_back[s][3], CORE) for s in seqs]
    def placed_in(part_mine, part_other, bit):
        size = part_mine.shape[0]
        empty = jnp.zeros((tensor_size * size,), F32)
        empty = lax.dynamic_update_slice(empty, part_mine, (place * size,))
        return lax.dynamic_update_slice(empty, part_other, ((place ^ bit) * size,))

    def norm_back(s, deps):
        return first_norm_back(
            one[s][0], two[s][1], fed_back[s][2], back_got[s], gain_one, deps
        )

    one_back = [norm_back(s, [fed_back[-1][2]]) for s in seqs]
    up_made = weight_grad(
        pairs([one[s][2] for s in seqs], normed_far),
        [fed_back[s][0] for s in seqs], [fed_back[s][1] for s in seqs],
        dp_place, [(hidden, far_first)], "w_up_grad", deps=[one_back[s][1] for s in seqs], halves=True,
    )
    first_across = [swap_tensor(one_back[s][1], ACROSS) for s in seqs]
    down_chain = Chain(*down_made, near_first)
    up_chain = Chain(*up_made, far_first)

    def backward(s, deps):
        return attention_backward(
            projected[s][0], projected[s][1], far[s], masks[s].reshape(seq_len, 1),
            one_back[s][1], first_across[s], att_mine, att_other, head_size, deps,
        )

    attended_back = [backward(0, [up_made[1]])]
    out_made = weight_grad(
        pairs([one_back[s][1] for s in seqs], first_across),
        [attended[s][0] for s in seqs], [attended[s][1] for s in seqs],
        dp_place, [(head_dims, near_first)], "w_out_grad", deps=[attended_back[0][3]],
    )
    down_chain.fold([attended_back[0][3]])
    attended_back += [backward(s, [down_chain.keep, out_made[1]]) for s in seqs[1:]]
    far_back = [swap_tensor(attended_back[s][2], CORE) for s in seqs]

    sums = add_up([attended_back[s][3] for s in seqs], [])
    small = jnp.concatenate(
        [
            sum(two[s][3] for s in seqs).reshape(-1),
            sum(one_back[s][2] for s in seqs).reshape(-1),
            placed_in(
                sum(fed_back[s][4] for s in seqs).reshape(-1),
                sum(fed_back[s][5] for s in seqs).reshape(-1),
                ACROSS,
            ),
            placed_in(sums[0, :head_dims], sums[1, :head_dims], CORE),
            placed_in(sums[0, head_dims:], sums[1, head_dims:], CORE),
        ]
    ).reshape(-1, 128)
    bits = [1 << level for level in reversed(near_first)]
    up_chain.fold([attended_back[-1][3]])
    small = plus(small, swap_tensor(small, CORE), [up_chain.keep])

    tokens = pairs(x_own, x_across)
    grad_queries = [attended_back[s][0] for s in seqs]
    query_made = weight_grad(
        tokens, grad_queries, grad_queries, dp_place, [(head_dims, near_first)], "w_query_grad",
        head_dims, [far_back[0], small],
    )
    back = [
        project_back(
            attended_back[0][0], attended_back[0][1], far_back[0], att_mine, att_other,
            [query_made[1]],
        )
    ]
    small = plus(small, swap_tensor(small, ACROSS), [back[0][2]])
    back += [
        project_back(
            attended_back[s][0], attended_back[s][1], far_back[s], att_mine, att_other, [small]
        )
        for s in seqs[1:]
    ]
    input_got = [swap_tensor(back[s][3], ACROSS) for s in seqs]
    for bit in bits[:1]:
        small = plus(small, swap_dp(small, bit), [back[-1][2]])
    down_chain.fold([back[-1][2]])
    both_got = swap_tensor(jnp.stack([query_made[1], out_made[1]]), CORE)
    query_chain = Chain(
        *fold_core([(query_made[0], both_got[0]), (out_made[0], both_got[1])], [back[-1][2]]),
        near_first,
    )
    key_value_made = weight_grad(
        tokens, [back[s][0] for s in seqs], [back[s][1] for s in seqs],
        dp_place, [(head_dims, near_first), (head_dims, far_first)], "w_key_value_grad",
        deps=input_got[:1] + [down_chain.keep, query_chain.keep, small],
    )
    up_chain.fold([key_value_made[0]])
    waits = input_got[-1:] + [up_chain.keep]
    key_chain = core_chain([key_value_made[:2]], near_first, waits)
    value_chain = core_chain([key_value_made[2:]], far_first, waits)
    started = [key_chain.keep, value_chain.keep]
    query_chain.fold(started)
    key_chain.fold()
    value_chain.fold()
    ending = [key_chain.keep, value_chain.keep]
    query_chain.fold(ending)
    down_chain.fold(ending)
    up_chain.fold(ending)
    for bit in bits[1:]:
        small = plus(small, swap_dp(small, bit), ending)
    small = small.reshape(-1)

    input_grad = jnp.stack(
        [
            (one_back[s][0] + (back[s][2] + input_got[s].astype(F32))).astype(BF16)
            for s in seqs
        ]
    )

    def over_y(both):
        return both[0] + swap_tensor(both[1].astype(BF16), ACROSS).astype(F32)

    down_grad, up_grad = over_y(down_chain.finish()), over_y(up_chain.finish())
    query_and_out = query_chain.finish()

    vectors = [small[i * width : (i + 1) * width] for i in range(6)]
    second_gain_grad, second_shift_grad, b_down_grad = vectors[:3]
    first_gain_grad, first_shift_grad, b_out_grad = vectors[3:]
    b_up_grad = small[6 * width : 6 * width + tensor_size * hidden]
    b_query_grad, b_value_grad = small[-2 * width : -width], small[-width:]

    output = jnp.stack([two[s][0] for s in seqs])
    return (
        output,
        input_grad,
        query_and_out[0],
        key_chain.finish()[0],
        value_chain.finish()[0],
        query_and_out[1].T,
        up_grad,
        down_grad.T,
        b_query_grad,
        b_value_grad,
        b_out_grad,
        b_up_grad,
        b_down_grad,
        first_gain_grad,
        first_shift_grad,
        second_gain_grad,
        second_shift_grad,
    )


def solution(mesh):
    placed = (
        P("dp", "tensor", None),
        P("dp"),
        P("dp", "tensor"),
        P("dp", "tensor"),
        P("dp", "tensor"),
        P("tensor", "dp"),
        P("dp", "tensor"),
        P("tensor", "dp"),
        P("tensor"),
        P("tensor"),
        P(),
        P("tensor"),
        P(),
        P(),
        P(),
        P(),
        P(),
        P("dp", "tensor", None),
    )
    return jax.shard_map(
        shards,
        mesh=mesh,
        in_specs=placed,
        out_specs=(
            P("dp", "tensor", None),
            P("dp", "tensor", None),
            P("dp", "tensor"),
            P("dp", "tensor"),
            P("dp", "tensor"),
            P("tensor", "dp"),
            P("dp", "tensor"),
            P("tensor", "dp"),
            P(),
            P(),
            P(),
            P(),
            P(),
            P(),
            P(),
            P(),
            P(),
        ),
        check_vma=False,
    )
```

```python
import math

import jax
import jax.numpy as jnp
from jax import lax
from jax.experimental import pallas as pl
from jax.experimental.pallas import tpu as pltpu
from jax.sharding import PartitionSpec as P

HEADS = 16
NORM_EPS = 1e-12
MASKED = -1000000000.0
MIB = 1024 * 1024
VMEM_LIMIT = 56 * MIB
SMALL_LIMIT = 16 * MIB
FOLD_LIMIT = 24 * MIB
UNDERSTATED = 1000

F32 = jnp.float32
BF16 = jnp.bfloat16

CORE = 1
ACROSS = 2


def dot(one, two):
    return lax.dot_general(one, two, (((1,), (0,)), ((), ())), preferred_element_type=F32)


def dot_nt(one, two):
    return lax.dot_general(one, two, (((1,), (1,)), ((), ())), preferred_element_type=F32)


def shape(dims, kind):
    return jax.ShapeDtypeStruct(dims, kind)


def after(kernel, count, deps):
    def body(*refs):
        kernel(*refs[:count], *refs[count + len(deps) :])

    return body


def whole_call(kernel, outs, args, flops, name, scratch=(), deps=(), limit=VMEM_LIMIT):
    moved = sum(math.prod(a.shape) * a.dtype.itemsize for a in (*args, *outs))
    return pl.pallas_call(
        after(kernel, len(args), deps),
        out_shape=tuple(outs),
        in_specs=[pl.BlockSpec(memory_space=pltpu.VMEM)] * len(args)
        + [pl.BlockSpec(memory_space=pl.ANY)] * len(deps),
        out_specs=tuple([pl.BlockSpec(memory_space=pltpu.VMEM)] * len(outs)),
        scratch_shapes=list(scratch),
        compiler_params=pltpu.CompilerParams(vmem_limit_bytes=limit),
        cost_estimate=pl.CostEstimate(
            flops=flops // UNDERSTATED, bytes_accessed=moved // UNDERSTATED, transcendentals=0
        ),
        name=name,
    )(*args, *deps)


def streamed_call(kernel, grid, outs, out_specs, args, in_specs, flops, name, scratch, deps=()):
    moved = sum(math.prod(a.shape) * a.dtype.itemsize for a in (*args, *outs))
    return pl.pallas_call(
        after(kernel, len(args), deps),
        grid=grid,
        out_shape=tuple(outs),
        in_specs=list(in_specs) + [pl.BlockSpec(memory_space=pl.ANY)] * len(deps),
        out_specs=tuple(out_specs),
        scratch_shapes=list(scratch),
        compiler_params=pltpu.CompilerParams(
            vmem_limit_bytes=VMEM_LIMIT, dimension_semantics=("arbitrary",)
        ),
        cost_estimate=pl.CostEstimate(
            flops=flops // UNDERSTATED, bytes_accessed=moved // UNDERSTATED, transcendentals=0
        ),
        name=name,
    )(*args, *deps)


def const_spec(dims):
    return pl.BlockSpec(dims, lambda i: (0,) * len(dims))


def swap_tensor(array, bit):
    size = lax.axis_size("tensor")
    return lax.ppermute(array, "tensor", [(i, i ^ bit) for i in range(size)])


def swap_dp(array, bit):
    size = lax.axis_size("dp")
    return lax.ppermute(array, "dp", [(i, i ^ bit) for i in range(size)])


def pack(parts, name, deps=()):
    def kernel(*refs):
        at = 0
        for ref in refs[:-1]:
            refs[-1][:, at : at + ref.shape[1]] = ref[...]
            at += ref.shape[1]

    out = shape((parts[0].shape[0], sum(p.shape[1] for p in parts)), parts[0].dtype)
    return whole_call(kernel, [out], parts, 0, name, deps=deps)[0]


def gather_far(rows):
    held = (rows, [0])
    steps = []
    step = lax.axis_size("dp") // 2
    while step > 1:
        steps.append(step)
        step //= 2
    first = []
    for step in steps[:-1]:
        came = (swap_dp(held[0], step), [o ^ step for o in held[1]])
        first.append(came[0])
        held = merged([held, came])
    pieces = [held]
    if steps:
        pieces.append((swap_dp(held[0], steps[-1]), [o ^ steps[-1] for o in held[1]]))
    return pieces, first[:1]


def merged(pieces):
    return (
        jnp.concatenate([p for p, _ in pieces], axis=0),
        [o for _, offsets in pieces for o in offsets],
    )


def gather_near(pieces):
    return [(swap_dp(p, 1), [o ^ 1 for o in offsets]) for p, offsets in pieces]


def other_core(pieces):
    return [(swap_tensor(p, CORE), offsets) for p, offsets in pieces]


def assemble(pieces, dp_place, name, deps=()):
    rows = pieces[0][0].shape[0] // len(pieces[0][1])
    width = pieces[0][0].shape[1]
    size = lax.axis_size("dp")

    def kernel(*refs):
        place = refs[0][0]
        for ref, (_, offsets) in zip(refs[1:-1], pieces):
            for i, offset in enumerate(offsets):
                start = pl.multiple_of((place ^ offset) * rows, rows)
                refs[-1][pl.ds(start, rows), :] = ref[i * rows : (i + 1) * rows, :]

    arrays = [p for p, _ in pieces]
    out = shape((size * rows, width), BF16)
    moved = 2 * size * rows * width * 2
    return pl.pallas_call(
        after(kernel, 1 + len(arrays), deps),
        out_shape=out,
        in_specs=[pl.BlockSpec(memory_space=pltpu.SMEM)]
        + [pl.BlockSpec(memory_space=pltpu.VMEM)] * len(arrays)
        + [pl.BlockSpec(memory_space=pl.ANY)] * len(deps),
        out_specs=pl.BlockSpec(memory_space=pltpu.VMEM),
        compiler_params=pltpu.CompilerParams(vmem_limit_bytes=VMEM_LIMIT),
        cost_estimate=pl.CostEstimate(
            flops=0, bytes_accessed=moved // UNDERSTATED, transcendentals=0
        ),
        name=name,
    )(dp_place, *arrays, *deps)


def halving_order(size, bits):
    order = [0]
    for bit in reversed(bits):
        order = order + [o ^ (1 << bit) for o in order]
    return order


def fold(keep, came, last, deps):
    groups, rows, width = keep.shape

    def kernel(k_ref, c_ref, *refs):
        if last:
            refs[0][...] = k_ref[...] + c_ref[...].astype(F32)
        else:
            half = rows // 2
            refs[0][...] = k_ref[:, :half] + c_ref[:, :half].astype(F32)
            refs[1][...] = (k_ref[:, half:] + c_ref[:, half:].astype(F32)).astype(BF16)

    outs = [shape(keep.shape, F32)]
    if not last:
        half_dims = (groups, rows // 2, width)
        outs = [shape(half_dims, F32), shape(half_dims, BF16)]
    return whole_call(
        kernel, outs, [keep, came], groups * rows * width, "fold", deps=deps, limit=FOLD_LIMIT
    )


def fold_core(pairs, deps):
    rows, width = pairs[0][0].shape
    half = rows // 2

    def kernel(*refs):
        for i in range(len(pairs)):
            mine, got = refs[2 * i : 2 * i + 2]
            refs[-2][i] = mine[:half] + got[:half].astype(F32)
            refs[-1][i] = (mine[half:] + got[half:].astype(F32)).astype(BF16)

    dims = (len(pairs), half, width)
    args = [array for pair in pairs for array in pair]
    return whole_call(
        kernel,
        [shape(dims, F32), shape(dims, BF16)],
        args,
        len(pairs) * rows * width,
        "fold_core",
        deps=deps,
        limit=FOLD_LIMIT,
    )


class Chain:
    def __init__(self, keep, send, bits):
        self.keep, self.bits = keep, list(bits)
        self.came = swap_dp(send, 1 << self.bits.pop(0))
        self.done = False

    def fold(self, deps=()):
        if self.done:
            return
        self.done = not self.bits
        made = fold(self.keep, self.came, self.done, list(deps))
        self.keep = made[0]
        if not self.done:
            self.came = swap_dp(made[1], 1 << self.bits.pop(0))

    def finish(self):
        while not self.done:
            self.fold()
        return self.keep


def plus(one, two, deps=()):
    def kernel(a_ref, b_ref, out_ref):
        out_ref[...] = a_ref[...] + b_ref[...]

    out = shape(one.shape, F32)
    return whole_call(kernel, [out], [one, two], 0, "plus", deps=list(deps), limit=SMALL_LIMIT)[0]


def project_inputs(x_own, x_across, w_mine, w_other, b_mine, b_other, deps):
    rows, width = x_own.shape
    third = w_mine.shape[1] // 4

    def kernel(x0, x1, wm, wo, bm, bo, mine_ref, other_ref, send_ref):
        tokens = jnp.concatenate([x0[...], x1[...]], axis=0)
        mine = (dot(tokens, wm[:, : 3 * third]) + bm[...]).astype(BF16)
        other = (dot(tokens, wo[:, : 3 * third]) + bo[...]).astype(BF16)
        mine_ref[...] = mine
        other_ref[...] = other
        send_ref[:, : 2 * third] = other[:, third:]
        send_ref[:, 2 * third :] = mine[:, third:]

    outs = [
        shape((2 * rows, 3 * third), BF16),
        shape((2 * rows, 3 * third), BF16),
        shape((2 * rows, 4 * third), BF16),
    ]
    flops = 2 * 2 * rows * width * 6 * third
    return whole_call(
        kernel,
        outs,
        [x_own, x_across, w_mine, w_other, b_mine, b_other],
        flops,
        "project_inputs",
        deps=deps,
    )


def attention_forward(mine, other, far, bias_row, w_mine, w_other, head_size, deps):
    rows = mine.shape[0]
    third = mine.shape[1] // 3
    heads = third // head_size
    block = rows // 2
    width = w_mine.shape[0]
    scaling = 1.0 / math.sqrt(head_size)

    def kernel(mine_ref, other_ref, far_ref, bias_ref, wm, wo, cm_ref, co_ref, own_ref, across_ref, acc):
        lane_head = lax.broadcasted_iota(jnp.int32, (1, third), 1) // head_size
        acc[...] = jnp.zeros_like(acc)
        bias = bias_ref[...]

        def one_head(head, carry):
            inside = lane_head == head
            for group, ref in enumerate((mine_ref, other_ref)):
                base = 2 * third * group
                keys = jnp.concatenate(
                    [ref[:, third : 2 * third], far_ref[:, base : base + third]], axis=0
                )
                vals = jnp.concatenate(
                    [ref[:, 2 * third :], far_ref[:, base + third : base + 2 * third]], axis=0
                )
                for part in range(2):
                    span = slice(part * block, (part + 1) * block)
                    query = jnp.where(inside, ref[span, :third] * scaling, 0.0).astype(BF16)
                    scores = dot_nt(query, keys) + bias
                    peak = jnp.max(scores, axis=-1, keepdims=True)
                    weights = jnp.exp(scores - peak)
                    total = jnp.sum(weights, axis=-1, keepdims=True)
                    found = dot(weights.astype(BF16), vals) * (1.0 / total)
                    acc[group, span, :] += jnp.where(inside, found, 0.0)
            return carry

        lax.fori_loop(0, heads, one_head, 0)
        ctx_mine = acc[0].astype(BF16)
        ctx_other = acc[1].astype(BF16)
        cm_ref[...] = ctx_mine
        co_ref[...] = ctx_other
        part_sum = dot_nt(ctx_mine, wm[:, 3 * third :]) + dot_nt(ctx_other, wo[:, 3 * third :])
        own_ref[...] = part_sum[:block]
        across_ref[...] = part_sum[block:].astype(BF16)

    outs = [
        shape((rows, third), BF16),
        shape((rows, third), BF16),
        shape((block, width), F32),
        shape((block, width), BF16),
    ]
    flops = 2 * 2 * 2 * rows * 2 * rows * third * heads * 2
    return whole_call(
        kernel,
        outs,
        [mine, other, far, bias_row, w_mine, w_other],
        flops,
        "attention_forward",
        [pltpu.VMEM((2, rows, third), F32)],
        deps,
    )


def attention_backward(mine, other, far, bias_column, ga_own, ga_across, w_mine, w_other, head_size, deps):
    rows = mine.shape[0]
    third = mine.shape[1] // 3
    heads = third // head_size
    block = rows // 2
    keys_count = 2 * rows
    scaling = 1.0 / math.sqrt(head_size)

    def kernel(
        mine_ref, other_ref, far_ref, bias_ref, g0, g1, wm, wo,
        dq_ref, keep_ref, send_ref, sums_ref, grad_ctx, keys_t, dq_t, dkv,
    ):
        lane_head = lax.broadcasted_iota(jnp.int32, (1, third), 1) // head_size
        grad_rows = jnp.concatenate([g0[...], g1[...]], axis=0)
        grad_ctx[0] = dot(grad_rows, wm[:, 3 * third :]).astype(BF16)
        grad_ctx[1] = dot(grad_rows, wo[:, 3 * third :]).astype(BF16)
        dkv[...] = jnp.zeros_like(dkv)
        for group, ref in enumerate((mine_ref, other_ref)):
            base = 2 * third * group
            keys_t[group, :, :rows] = ref[:, third : 2 * third].T
            keys_t[group, :, rows:] = far_ref[:, base : base + third].T
        bias = bias_ref[...]

        def one_head(head, carry):
            inside = lane_head == head
            start = pl.multiple_of(head * head_size, head_size)
            for group, ref in enumerate((mine_ref, other_ref)):
                base = 2 * third * group
                keys = jnp.concatenate(
                    [ref[:, third : 2 * third], far_ref[:, base : base + third]], axis=0
                )
                vals = jnp.concatenate(
                    [ref[:, 2 * third :], far_ref[:, base + third : base + 2 * third]], axis=0
                )
                head_keys_t = keys_t[group, pl.ds(start, head_size), :]
                for part in range(2):
                    span = slice(part * block, (part + 1) * block)
                    query = jnp.where(inside, ref[span, :third] * scaling, 0.0).astype(BF16)
                    grad = jnp.where(inside, grad_ctx[group, span, :], 0.0).astype(BF16)
                    scores = dot_nt(keys, query) + bias
                    peak = jnp.max(scores, axis=0, keepdims=True)
                    weights = jnp.exp(scores - peak)
                    total = jnp.sum(weights, axis=0, keepdims=True)
                    probs = weights * (1.0 / total)
                    grad_probs = dot_nt(vals, grad)
                    inner = jnp.sum(probs * grad_probs, axis=0, keepdims=True)
                    grad_scores = (probs * (grad_probs - inner)).astype(BF16)
                    dkv[group, 1] += dot(probs.astype(BF16), grad)
                    dkv[group, 0] += dot(grad_scores, query)
                    dq_t[group, pl.ds(start, head_size), span] = dot(head_keys_t, grad_scores)
            return carry

        lax.fori_loop(0, heads, one_head, 0)
        for group in range(2):
            grad_query = (dq_t[group].T * scaling).astype(BF16)
            dq_ref[:, group * third : (group + 1) * third] = grad_query
            sums_ref[group : group + 1, :third] = jnp.sum(
                grad_query.astype(F32), axis=0, keepdims=True
            )
            sums_ref[group : group + 1, third:] = jnp.sum(dkv[group, 1], axis=0, keepdims=True)
            for kind in range(2):
                at = (2 * group + kind) * third
                keep_ref[:, at : at + third] = dkv[group, kind, :rows]
                away = (2 * (1 - group) + kind) * third
                send_ref[:, away : away + third] = dkv[group, kind, rows:].astype(BF16)

    outs = [
        shape((rows, 2 * third), BF16),
        shape((rows, 4 * third), F32),
        shape((rows, 4 * third), BF16),
        shape((2, 2 * third), F32),
    ]
    flops = 5 * 2 * 2 * rows * keys_count * third * heads * 2 * UNDERSTATED
    return whole_call(
        kernel,
        outs,
        [mine, other, far, bias_column, ga_own, ga_across, w_mine, w_other],
        flops,
        "attention_backward",
        [
            pltpu.VMEM((2, rows, third), BF16),
            pltpu.VMEM((2, third, keys_count), BF16),
            pltpu.VMEM((2, third, rows), F32),
            pltpu.VMEM((2, 2, keys_count, third), F32),
        ],
        deps,
    )


def project_back(dq, keep, got, w_mine, w_other, deps):
    rows = dq.shape[0]
    third = dq.shape[1] // 2
    block = rows // 2
    width = w_mine.shape[0]

    def kernel(dq_ref, keep_ref, got_ref, wm, wo, gm_ref, go_ref, own_ref, across_ref):
        dkv = (keep_ref[...] + got_ref[...].astype(F32)).astype(BF16)
        grad_mine = jnp.concatenate([dq_ref[:, :third], dkv[:, : 2 * third]], axis=1)
        grad_other = jnp.concatenate([dq_ref[:, third:], dkv[:, 2 * third :]], axis=1)
        gm_ref[...] = dkv[:, : 2 * third]
        go_ref[...] = dkv[:, 2 * third :]
        back = dot_nt(grad_mine, wm[:, : 3 * third]) + dot_nt(grad_other, wo[:, : 3 * third])
        own_ref[...] = back[:block]
        across_ref[...] = back[block:].astype(BF16)

    outs = [
        shape((rows, 2 * third), BF16),
        shape((rows, 2 * third), BF16),
        shape((block, width), F32),
        shape((block, width), BF16),
    ]
    flops = 2 * rows * width * 6 * third
    return whole_call(
        kernel, outs, [dq, keep, got, w_mine, w_other], flops, "project_back", deps=deps
    )


def moments(summed):
    centre = jnp.mean(summed, axis=-1, keepdims=True)
    centred = summed - centre
    spread = jnp.mean(centred * centred, axis=-1, keepdims=True)
    back = lax.rsqrt(spread + NORM_EPS)
    return centred * back, back


def first_norm(x_own, part, got, b_out, gain, shift, deps):
    dims = x_own.shape

    def kernel(x_ref, p_ref, r_ref, b_ref, g_ref, s_ref, summed_ref, normed_ref, low_ref):
        summed = x_ref[...].astype(F32) + (p_ref[...] + r_ref[...].astype(F32)) + b_ref[...]
        unit, _ = moments(summed)
        normed = unit * g_ref[...] + s_ref[...]
        summed_ref[...] = summed
        normed_ref[...] = normed
        low_ref[...] = normed.astype(BF16)

    outs = [shape(dims, F32), shape(dims, F32), shape(dims, BF16)]
    return whole_call(
        kernel,
        outs,
        [x_own, part, got, b_out, gain, shift],
        20 * math.prod(dims),
        "first_norm",
        deps=deps,
        limit=SMALL_LIMIT,
    )


def second_norm(normed, part, got, cotangent, b_down, gain, shift):
    dims = normed.shape

    def kernel(n_ref, p_ref, r_ref, c_ref, b_ref, g_ref, s_ref, out_ref, grad_ref, low_ref, sums_ref):
        summed = n_ref[...] + (p_ref[...] + r_ref[...].astype(F32)) + b_ref[...]
        unit, back = moments(summed)
        out_ref[...] = (unit * g_ref[...] + s_ref[...]).astype(BF16)
        cot = c_ref[...].astype(F32)
        scaled = cot * g_ref[...]
        grad = back * (
            scaled
            - jnp.mean(scaled, axis=-1, keepdims=True)
            - unit * jnp.mean(scaled * unit, axis=-1, keepdims=True)
        )
        grad_ref[...] = grad
        low_ref[...] = grad.astype(BF16)
        sums_ref[0:1, :] = jnp.sum(cot * unit, axis=0, keepdims=True)
        sums_ref[1:2, :] = jnp.sum(cot, axis=0, keepdims=True)
        sums_ref[2:3, :] = jnp.sum(grad, axis=0, keepdims=True)

    outs = [shape(dims, BF16), shape(dims, F32), shape(dims, BF16), shape((3, dims[1]), F32)]
    return whole_call(
        kernel,
        outs,
        [normed, part, got, cotangent, b_down, gain, shift],
        40 * math.prod(dims),
        "second_norm",
        limit=SMALL_LIMIT,
    )


def first_norm_back(summed, grad_second, part, got, gain, deps):
    dims = summed.shape

    def kernel(z_ref, gs_ref, p_ref, r_ref, g_ref, grad_ref, low_ref, sums_ref):
        unit, back = moments(z_ref[...])
        grad_normed = gs_ref[...] + (p_ref[...] + r_ref[...].astype(F32))
        scaled = grad_normed * g_ref[...]
        grad = back * (
            scaled
            - jnp.mean(scaled, axis=-1, keepdims=True)
            - unit * jnp.mean(scaled * unit, axis=-1, keepdims=True)
        )
        grad_ref[...] = grad
        low_ref[...] = grad.astype(BF16)
        sums_ref[0:1, :] = jnp.sum(grad_normed * unit, axis=0, keepdims=True)
        sums_ref[1:2, :] = jnp.sum(grad_normed, axis=0, keepdims=True)
        sums_ref[2:3, :] = jnp.sum(grad, axis=0, keepdims=True)

    outs = [shape(dims, F32), shape(dims, BF16), shape((3, dims[1]), F32)]
    return whole_call(
        kernel,
        outs,
        [summed, grad_second, part, got, gain],
        40 * math.prod(dims),
        "first_norm_back",
        deps=deps,
        limit=SMALL_LIMIT,
    )


def feed_forward(n_own, n_far, weights, bias, prior, deps):
    block, width = n_own.shape
    rows = 2 * block
    hidden = weights.shape[1] // 2
    tile = min(256, hidden)
    steps = hidden // tile
    last = prior is not None

    def kernel(n0, n1, u, d, b, *refs):
        step = pl.program_id(0)
        if last:
            before, a_ref, s_ref, own_ref, far_ref, tokens, acc = refs
        else:
            a_ref, s_ref, acc, tokens = refs

        @pl.when(step == 0)
        def _():
            tokens[:block] = n0[...]
            tokens[block:] = n1[...]
            acc[...] = before[...] if last else jnp.zeros_like(acc)

        hid = dot(tokens[...], u[...]) + b[...]
        half = 0.5 * (1.0 + lax.erf(hid * (1.0 / math.sqrt(2.0))))
        bell = jnp.exp(hid * hid * -0.5) * (1.0 / math.sqrt(2.0 * math.pi))
        active = (hid * half).astype(BF16)
        a_ref[...] = active
        s_ref[...] = (half + hid * bell).astype(BF16)
        acc[...] += dot_nt(active, d[...])

        if last:

            @pl.when(step == steps - 1)
            def _():
                own_ref[...] = acc[:block]
                far_ref[...] = acc[block:].astype(BF16)

    column = pl.BlockSpec((width, tile), lambda i: (0, i))
    later = pl.BlockSpec((width, tile), lambda i: (0, steps + i))
    made = pl.BlockSpec((rows, tile), lambda i: (0, i))
    args = [n_own, n_far, weights, weights, bias]
    in_specs = [const_spec((block, width))] * 2
    in_specs += [column, later, pl.BlockSpec((1, tile), lambda i: (0, i))]
    outs = [shape((rows, hidden), BF16)] * 2
    scratch = [pltpu.VMEM((rows, width), BF16)]
    if last:
        args.append(prior)
        in_specs.append(const_spec((rows, width)))
        outs += [shape((block, width), F32), shape((block, width), BF16)]
        out_specs = [made] * 2 + [const_spec((block, width))] * 2
        scratch.append(pltpu.VMEM((rows, width), F32))
    else:
        outs.append(shape((rows, width), F32))
        out_specs = [made] * 2 + [const_spec((rows, width))]
    return streamed_call(
        kernel,
        (steps,),
        outs,
        out_specs,
        args,
        in_specs,
        2 * 2 * rows * width * hidden,
        "feed_forward",
        scratch,
        deps,
    )


def feed_forward_back(g_own, g_across, w_mine, w_other, slope_mine, slope_other, deps):
    block, width = g_own.shape
    rows = 2 * block
    hidden = w_mine.shape[1] // 2
    tile = min(256, hidden)
    steps = hidden // tile

    def kernel(
        g0, g1, um, uo, dm, do, sm, so,
        gm_ref, go_ref, own_ref, across_ref, bm_ref, bo_ref, grads, acc,
    ):
        step = pl.program_id(0)

        @pl.when(step == 0)
        def _():
            grads[:block] = g0[...]
            grads[block:] = g1[...]
            acc[...] = jnp.zeros_like(acc)

        total = acc[...]
        for u, d, s, g_ref, b_ref in ((um, dm, sm, gm_ref, bm_ref), (uo, do, so, go_ref, bo_ref)):
            grad_hidden = (dot(grads[...], d[...]) * s[...].astype(F32)).astype(BF16)
            g_ref[...] = grad_hidden
            b_ref[...] = jnp.sum(grad_hidden.astype(F32), axis=0, keepdims=True)
            total = total + dot_nt(grad_hidden, u[...])
        acc[...] = total

        @pl.when(step == steps - 1)
        def _():
            own_ref[...] = acc[:block]
            across_ref[...] = acc[block:].astype(BF16)

    column = pl.BlockSpec((width, tile), lambda i: (0, i))
    later = pl.BlockSpec((width, tile), lambda i: (0, steps + i))
    bias = pl.BlockSpec((1, tile), lambda i: (0, i))
    made = pl.BlockSpec((rows, tile), lambda i: (0, i))
    outs = (
        [shape((rows, hidden), BF16)] * 2
        + [shape((block, width), F32), shape((block, width), BF16)]
        + [shape((1, hidden), F32)] * 2
    )
    return streamed_call(
        kernel,
        (steps,),
        outs,
        [made] * 2 + [const_spec((block, width))] * 2 + [bias] * 2,
        [g_own, g_across, w_mine, w_other, w_mine, w_other, slope_mine, slope_other],
        [const_spec((block, width))] * 2 + [column] * 2 + [later] * 2 + [made] * 2,
        2 * 2 * rows * width * 2 * hidden,
        "feed_forward_back",
        [pltpu.VMEM((rows, width), BF16), pltpu.VMEM((rows, width), F32)],
        deps,
    )


def weight_grad(ones, mine, other, dp_place, chains, name, other_first=0, deps=(), halves=False):
    block, width = ones[0].shape
    rows = 2 * block
    count = chains[0][0]
    tile = min(256, count)
    tiles = count // tile
    size = lax.axis_size("dp")
    share = width // size
    half = width // 2

    def kernel(place_ref, a0, a1, a2, a3, m0, m1, o0, o1, *refs):
        turned, full = refs[-2:]
        step = pl.program_id(0)

        @pl.when(step == 0)
        def _():
            for i, ref in enumerate((a0, a1, a2, a3)):
                turned[:, i * block : (i + 1) * block] = ref[...].T

        place = place_ref[0]

        def write(which, targets, order):
            for i, offset in enumerate(order):
                start = pl.multiple_of((place ^ offset) * share, share)
                at = i * share
                rows_now = full[pl.ds(start, share), :]
                if halves:
                    ref = targets[0] if at < half else targets[1]
                    at %= half
                    ref[which, at : at + share, :] = rows_now.astype(ref.dtype)
                else:
                    targets[which][at : at + share, :] = rows_now.astype(targets[which].dtype)

        for which, (one, two) in enumerate(((m0, m1), (o0, o1))):
            full[...] = dot(turned[:, :rows], one[...]) + dot(turned[:, rows:], two[...])
            for c, (_, bits) in enumerate(chains):
                targets = refs[2 * c : 2 * c + 2]
                order = halving_order(size, bits)
                if len(chains) == 1:
                    write(which, targets, order)
                else:
                    pl.when(step // tiles == c)(
                        lambda w=which, t=targets, o=order: write(w, t, o)
                    )

    base = other_first // tile
    column = pl.BlockSpec((rows, tile), lambda i: (0, i))
    other_column = pl.BlockSpec((rows, tile), lambda i: (0, base + i))
    outs, out_specs = [], []
    for c in range(len(chains)):
        for kind in (F32, BF16):
            if halves:
                outs.append(shape((2, half, count), kind))
                out_specs.append(pl.BlockSpec((2, half, tile), lambda i: (0, 0, i)))
            else:
                index = lambda i, c=c: (0, jnp.clip(i - c * tiles, 0, tiles - 1))
                outs.append(shape((width, count), kind))
                out_specs.append(pl.BlockSpec((width, tile), index))
    return streamed_call(
        kernel,
        (tiles * len(chains),),
        outs,
        out_specs,
        [dp_place, *ones, *mine, *other],
        [pl.BlockSpec(memory_space=pltpu.SMEM)]
        + [const_spec((block, width))] * 4
        + [column] * 2
        + [other_column] * 2,
        2 * 2 * rows * width * 2 * count * len(chains),
        name,
        [pltpu.VMEM((width, 2 * rows), BF16), pltpu.VMEM((width, tile), F32)],
        deps,
    )


def core_chain(made, bits, deps=()):
    pairs = [(mine, swap_tensor(other, CORE)) for mine, other in made]
    keep, send = fold_core(pairs, list(deps))
    return Chain(keep, send, bits)


def add_up(parts, deps):
    def kernel(*refs):
        refs[-1][...] = sum(ref[...] for ref in refs[:-1])

    out = shape(parts[0].shape, F32)
    return whole_call(kernel, [out], parts, 0, "add_up", deps=deps, limit=SMALL_LIMIT)[0]


def shards(
    inputs,
    lengths,
    w_query,
    w_key,
    w_value,
    w_out,
    w_up,
    w_down,
    b_query,
    b_value,
    b_out,
    b_up,
    b_down,
    first_gain,
    first_shift,
    second_gain,
    second_shift,
    cotangent,
):
    seq_count, block, width = inputs.shape
    tensor_size = lax.axis_size("tensor")
    seq_len = block * tensor_size
    place = lax.axis_index("tensor")
    head_dims = w_query.shape[1]
    head_size = width // HEADS
    hidden = w_up.shape[1]
    seqs = range(seq_count)
    row = lambda vector: vector.reshape(1, -1)

    x_own = [inputs[s] for s in seqs]
    all_across = swap_tensor(inputs, ACROSS)
    x_across = [all_across[s] for s in seqs]

    dp_place = lax.axis_index("dp").astype(jnp.int32).reshape(1)
    att_far, att_first = gather_far(pack([w_query, w_key, w_value, w_out.T], "pack_attention"))
    att_pieces = att_far + gather_near(att_far)
    share = pack([w_up, w_down.T], "pack_feed", att_first)
    share_other = swap_tensor(share, ACROSS)
    mine_far, mine_first = gather_far(share)
    mine_near = gather_near(mine_far)
    other_far, other_first = gather_far(share_other)
    other_near = gather_near(other_far[:1]) + [
        (swap_tensor(p, ACROSS), offsets) for p, offsets in mine_near[1:]
    ]

    def arrays(pieces):
        return [p for p, _ in pieces]

    att_mine = assemble(att_pieces, dp_place, "assemble_attention")
    att_other = assemble(other_core(att_pieces), dp_place, "assemble_attention_other")
    ffw_mine = assemble(mine_far + mine_near, dp_place, "assemble_feed")
    project_waits = [mine_first, [share_other]]
    attend_waits = [arrays(mine_far[1:]), arrays(mine_near[:1]) + other_first]
    norm_waits = [arrays(mine_near[1:]), arrays(other_far[1:]) + [ffw_mine]]

    biases = jnp.concatenate([b_query, jnp.zeros_like(b_query), b_value])
    qkv_bias_mine, qkv_bias_other = row(biases), row(swap_tensor(biases, CORE))
    up_bias_mine, up_bias_other = row(b_up), row(swap_tensor(b_up, ACROSS))
    b_out_row, b_down_row = row(b_out), row(b_down)
    gain_one, shift_one = row(first_gain), row(first_shift)
    gain_two, shift_two = row(second_gain), row(second_shift)

    order = jnp.stack([place, place ^ ACROSS, place ^ CORE, place ^ CORE ^ ACROSS])
    positions = (order[:, None] * block + jnp.arange(block, dtype=jnp.int32)[None, :]).reshape(-1)
    masks = [jnp.where(positions < lengths[s], 0.0, MASKED).astype(F32) for s in seqs]

    projected = []
    for s in seqs:
        waits = project_waits[s] if s < 2 else []
        projected.append(
            project_inputs(
                x_own[s], x_across[s], att_mine, att_other, qkv_bias_mine, qkv_bias_other,
                waits + [p[2] for p in projected[-1:]],
            )
        )
    far = [swap_tensor(projected[s][2], CORE) for s in seqs]
    attended = []
    for s in seqs:
        waits = attend_waits[s] if s < 2 else []
        attended.append(
            attention_forward(
                projected[s][0], projected[s][1], far[s], masks[s].reshape(1, seq_len),
                att_mine, att_other, head_size, waits + [p[2] for p in attended[-1:]],
            )
        )
    attended_got = [swap_tensor(attended[s][3], ACROSS) for s in seqs]
    one = []
    for s in seqs:
        waits = norm_waits[s] if s < 2 else []
        one.append(
            first_norm(
                x_own[s], attended[s][2], attended_got[s], b_out_row, gain_one, shift_one,
                waits + [p[2] for p in one[-1:]],
            )
        )
    normed_far = [swap_tensor(one[s][2], CORE) for s in seqs]
    fed_one = []
    for s in seqs:
        waits = [p[2] for p in fed_one[-1:]]
        fed_one.append(
            feed_forward(one[s][2], normed_far[s], ffw_mine, up_bias_mine, None, waits)
        )
    ffw_other = assemble(
        other_far + other_near, dp_place, "assemble_feed_other", [fed_one[-1][2]]
    )
    fed_two = []
    for s in seqs:
        waits = [p[2] for p in fed_two[-1:]]
        fed_two.append(
            feed_forward(
                one[s][2], normed_far[s], ffw_other, up_bias_other, fed_one[s][2], waits
            )
        )
    fed = [(fed_one[s][0], fed_two[s][0], fed_one[s][1], fed_two[s][1], *fed_two[s][2:]) for s in seqs]
    branch_got = [swap_tensor(fed[s][5], CORE) for s in seqs]
    two = [
        second_norm(
            one[s][1], fed[s][4], branch_got[s], cotangent[s], b_down_row, gain_two, shift_two
        )
        for s in seqs
    ]
    grad_far = [swap_tensor(two[s][2], CORE) for s in seqs]
    levels = range(lax.axis_size("dp").bit_length() - 1)
    near_first = list(levels)
    far_first = [1, 0, *levels[2:]] if len(near_first) > 1 else near_first

    def pairs(own, across):
        return [part for s in seqs for part in (own[s], across[s])]

    def feed_back(s, deps):
        return feed_forward_back(
            two[s][2], grad_far[s], ffw_mine, ffw_other, fed[s][2], fed[s][3], deps
        )

    fed_back = [feed_back(0, [])]
    down_made = weight_grad(
        pairs([two[s][2] for s in seqs], grad_far),
        [fed[s][0] for s in seqs], [fed[s][1] for s in seqs],
        dp_place, [(hidden, near_first)], "w_down_grad", deps=[fed_back[0][2]], halves=True,
    )
    fed_back += [feed_back(s, [down_made[1]]) for s in seqs[1:]]
    back_got = [swap_tensor(fed_back[s][3], CORE) for s in seqs]
    def placed_in(part_mine, part_other, bit):
        size = part_mine.shape[0]
        empty = jnp.zeros((tensor_size * size,), F32)
        empty = lax.dynamic_update_slice(empty, part_mine, (place * size,))
        return lax.dynamic_update_slice(empty, part_other, ((place ^ bit) * size,))

    def norm_back(s, deps):
        return first_norm_back(
            one[s][0], two[s][1], fed_back[s][2], back_got[s], gain_one, deps
        )

    one_back = [norm_back(s, [fed_back[-1][2]]) for s in seqs]
    up_made = weight_grad(
        pairs([one[s][2] for s in seqs], normed_far),
        [fed_back[s][0] for s in seqs], [fed_back[s][1] for s in seqs],
        dp_place, [(hidden, far_first)], "w_up_grad", deps=[one_back[s][1] for s in seqs], halves=True,
    )
    first_across = [swap_tensor(one_back[s][1], ACROSS) for s in seqs]
    down_chain = Chain(*down_made, near_first)
    up_chain = Chain(*up_made, far_first)

    def backward(s, deps):
        return attention_backward(
            projected[s][0], projected[s][1], far[s], masks[s].reshape(seq_len, 1),
            one_back[s][1], first_across[s], att_mine, att_other, head_size, deps,
        )

    attended_back = [backward(0, [up_made[1]])]
    out_made = weight_grad(
        pairs([one_back[s][1] for s in seqs], first_across),
        [attended[s][0] for s in seqs], [attended[s][1] for s in seqs],
        dp_place, [(head_dims, near_first)], "w_out_grad", deps=[attended_back[0][3]],
    )
    down_chain.fold([attended_back[0][3]])
    attended_back += [backward(s, [down_chain.keep, out_made[1]]) for s in seqs[1:]]
    far_back = [swap_tensor(attended_back[s][2], CORE) for s in seqs]

    sums = add_up([attended_back[s][3] for s in seqs], [])
    small = jnp.concatenate(
        [
            sum(two[s][3] for s in seqs).reshape(-1),
            sum(one_back[s][2] for s in seqs).reshape(-1),
            placed_in(
                sum(fed_back[s][4] for s in seqs).reshape(-1),
                sum(fed_back[s][5] for s in seqs).reshape(-1),
                ACROSS,
            ),
            placed_in(sums[0, :head_dims], sums[1, :head_dims], CORE),
            placed_in(sums[0, head_dims:], sums[1, head_dims:], CORE),
        ]
    ).reshape(-1, 128)
    bits = [1 << level for level in reversed(near_first)]
    up_chain.fold([attended_back[-1][3]])
    small = plus(small, swap_tensor(small, CORE), [up_chain.keep])

    tokens = pairs(x_own, x_across)
    grad_queries = [attended_back[s][0] for s in seqs]
    query_made = weight_grad(
        tokens, grad_queries, grad_queries, dp_place, [(head_dims, near_first)], "w_query_grad",
        head_dims, [far_back[0], small],
    )
    back = [
        project_back(
            attended_back[0][0], attended_back[0][1], far_back[0], att_mine, att_other,
            [query_made[1]],
        )
    ]
    small = plus(small, swap_tensor(small, ACROSS), [back[0][2]])
    back += [
        project_back(
            attended_back[s][0], attended_back[s][1], far_back[s], att_mine, att_other, [small]
        )
        for s in seqs[1:]
    ]
    input_got = [swap_tensor(back[s][3], ACROSS) for s in seqs]
    for bit in bits[:1]:
        small = plus(small, swap_dp(small, bit), [back[-1][2]])
    down_chain.fold([back[-1][2]])
    up_chain.fold([down_chain.keep])
    both_got = swap_tensor(jnp.stack([query_made[1], out_made[1]]), CORE)
    query_chain = Chain(
        *fold_core([(query_made[0], both_got[0]), (out_made[0], both_got[1])], [back[-1][2]]),
        near_first,
    )
    key_value_made = weight_grad(
        tokens, [back[s][0] for s in seqs], [back[s][1] for s in seqs],
        dp_place, [(head_dims, near_first), (head_dims, far_first)], "w_key_value_grad",
        deps=input_got[:1] + [up_chain.keep, query_chain.keep, small],
    )
    waits = input_got[-1:] + [down_chain.came]
    key_chain = core_chain([key_value_made[:2]], near_first, waits)
    value_chain = core_chain([key_value_made[2:]], far_first, waits)
    started = [key_chain.keep, value_chain.keep]
    query_chain.fold(started)
    key_chain.fold()
    value_chain.fold()
    ending = [key_chain.keep, value_chain.keep]
    query_chain.fold(ending)
    down_chain.fold(ending)
    up_chain.fold(ending)
    for bit in bits[1:]:
        small = plus(small, swap_dp(small, bit), ending)
    small = small.reshape(-1)

    input_grad = jnp.stack(
        [
            (one_back[s][0] + (back[s][2] + input_got[s].astype(F32))).astype(BF16)
            for s in seqs
        ]
    )

    def over_y(both):
        return both[0] + swap_tensor(both[1].astype(BF16), ACROSS).astype(F32)

    down_grad, up_grad = over_y(down_chain.finish()), over_y(up_chain.finish())
    query_and_out = query_chain.finish()

    vectors = [small[i * width : (i + 1) * width] for i in range(6)]
    second_gain_grad, second_shift_grad, b_down_grad = vectors[:3]
    first_gain_grad, first_shift_grad, b_out_grad = vectors[3:]
    b_up_grad = small[6 * width : 6 * width + tensor_size * hidden]
    b_query_grad, b_value_grad = small[-2 * width : -width], small[-width:]

    output = jnp.stack([two[s][0] for s in seqs])
    return (
        output,
        input_grad,
        query_and_out[0],
        key_chain.finish()[0],
        value_chain.finish()[0],
        query_and_out[1].T,
        up_grad,
        down_grad.T,
        b_query_grad,
        b_value_grad,
        b_out_grad,
        b_up_grad,
        b_down_grad,
        first_gain_grad,
        first_shift_grad,
        second_gain_grad,
        second_shift_grad,
    )


def solution(mesh):
    placed = (
        P("dp", "tensor", None),
        P("dp"),
        P("dp", "tensor"),
        P("dp", "tensor"),
        P("dp", "tensor"),
        P("tensor", "dp"),
        P("dp", "tensor"),
        P("tensor", "dp"),
        P("tensor"),
        P("tensor"),
        P(),
        P("tensor"),
        P(),
        P(),
        P(),
        P(),
        P(),
        P("dp", "tensor", None),
    )
    return jax.shard_map(
        shards,
        mesh=mesh,
        in_specs=placed,
        out_specs=(
            P("dp", "tensor", None),
            P("dp", "tensor", None),
            P("dp", "tensor"),
            P("dp", "tensor"),
            P("dp", "tensor"),
            P("tensor", "dp"),
            P("dp", "tensor"),
            P("tensor", "dp"),
            P(),
            P(),
            P(),
            P(),
            P(),
            P(),
            P(),
            P(),
            P(),
        ),
        check_vma=False,
    )
```

```python
import math

import jax
import jax.numpy as jnp
from jax import lax
from jax.experimental import pallas as pl
from jax.experimental.pallas import tpu as pltpu
from jax.sharding import PartitionSpec as P

HEADS = 16
NORM_EPS = 1e-12
MASKED = -1000000000.0
MIB = 1024 * 1024
VMEM_LIMIT = 56 * MIB
SMALL_LIMIT = 16 * MIB
FOLD_LIMIT = 24 * MIB
UNDERSTATED = 1000

F32 = jnp.float32
BF16 = jnp.bfloat16

CORE = 1
ACROSS = 2


def dot(one, two):
    return lax.dot_general(one, two, (((1,), (0,)), ((), ())), preferred_element_type=F32)


def dot_nt(one, two):
    return lax.dot_general(one, two, (((1,), (1,)), ((), ())), preferred_element_type=F32)


def shape(dims, kind):
    return jax.ShapeDtypeStruct(dims, kind)


def after(kernel, count, deps):
    def body(*refs):
        kernel(*refs[:count], *refs[count + len(deps) :])

    return body


def whole_call(kernel, outs, args, flops, name, scratch=(), deps=(), limit=VMEM_LIMIT):
    moved = sum(math.prod(a.shape) * a.dtype.itemsize for a in (*args, *outs))
    return pl.pallas_call(
        after(kernel, len(args), deps),
        out_shape=tuple(outs),
        in_specs=[pl.BlockSpec(memory_space=pltpu.VMEM)] * len(args)
        + [pl.BlockSpec(memory_space=pl.ANY)] * len(deps),
        out_specs=tuple([pl.BlockSpec(memory_space=pltpu.VMEM)] * len(outs)),
        scratch_shapes=list(scratch),
        compiler_params=pltpu.CompilerParams(vmem_limit_bytes=limit),
        cost_estimate=pl.CostEstimate(
            flops=flops // UNDERSTATED, bytes_accessed=moved // UNDERSTATED, transcendentals=0
        ),
        name=name,
    )(*args, *deps)


def streamed_call(kernel, grid, outs, out_specs, args, in_specs, flops, name, scratch, deps=()):
    moved = sum(math.prod(a.shape) * a.dtype.itemsize for a in (*args, *outs))
    return pl.pallas_call(
        after(kernel, len(args), deps),
        grid=grid,
        out_shape=tuple(outs),
        in_specs=list(in_specs) + [pl.BlockSpec(memory_space=pl.ANY)] * len(deps),
        out_specs=tuple(out_specs),
        scratch_shapes=list(scratch),
        compiler_params=pltpu.CompilerParams(
            vmem_limit_bytes=VMEM_LIMIT, dimension_semantics=("arbitrary",)
        ),
        cost_estimate=pl.CostEstimate(
            flops=flops // UNDERSTATED, bytes_accessed=moved // UNDERSTATED, transcendentals=0
        ),
        name=name,
    )(*args, *deps)


def const_spec(dims):
    return pl.BlockSpec(dims, lambda i: (0,) * len(dims))


def swap_tensor(array, bit):
    size = lax.axis_size("tensor")
    return lax.ppermute(array, "tensor", [(i, i ^ bit) for i in range(size)])


def swap_dp(array, bit):
    size = lax.axis_size("dp")
    return lax.ppermute(array, "dp", [(i, i ^ bit) for i in range(size)])


def pack(parts, name, deps=()):
    def kernel(*refs):
        at = 0
        for ref in refs[:-1]:
            refs[-1][:, at : at + ref.shape[1]] = ref[...]
            at += ref.shape[1]

    out = shape((parts[0].shape[0], sum(p.shape[1] for p in parts)), parts[0].dtype)
    return whole_call(kernel, [out], parts, 0, name, deps=deps)[0]


def gather_far(rows):
    held = (rows, [0])
    steps = []
    step = lax.axis_size("dp") // 2
    while step > 1:
        steps.append(step)
        step //= 2
    first = []
    for step in steps[:-1]:
        came = (swap_dp(held[0], step), [o ^ step for o in held[1]])
        first.append(came[0])
        held = merged([held, came])
    pieces = [held]
    if steps:
        pieces.append((swap_dp(held[0], steps[-1]), [o ^ steps[-1] for o in held[1]]))
    return pieces, first[:1]


def merged(pieces):
    return (
        jnp.concatenate([p for p, _ in pieces], axis=0),
        [o for _, offsets in pieces for o in offsets],
    )


def gather_near(pieces):
    return [(swap_dp(p, 1), [o ^ 1 for o in offsets]) for p, offsets in pieces]


def other_core(pieces):
    return [(swap_tensor(p, CORE), offsets) for p, offsets in pieces]


def assemble(pieces, dp_place, name, deps=()):
    rows = pieces[0][0].shape[0] // len(pieces[0][1])
    width = pieces[0][0].shape[1]
    size = lax.axis_size("dp")

    def kernel(*refs):
        place = refs[0][0]
        for ref, (_, offsets) in zip(refs[1:-1], pieces):
            for i, offset in enumerate(offsets):
                start = pl.multiple_of((place ^ offset) * rows, rows)
                refs[-1][pl.ds(start, rows), :] = ref[i * rows : (i + 1) * rows, :]

    arrays = [p for p, _ in pieces]
    out = shape((size * rows, width), BF16)
    moved = 2 * size * rows * width * 2
    return pl.pallas_call(
        after(kernel, 1 + len(arrays), deps),
        out_shape=out,
        in_specs=[pl.BlockSpec(memory_space=pltpu.SMEM)]
        + [pl.BlockSpec(memory_space=pltpu.VMEM)] * len(arrays)
        + [pl.BlockSpec(memory_space=pl.ANY)] * len(deps),
        out_specs=pl.BlockSpec(memory_space=pltpu.VMEM),
        compiler_params=pltpu.CompilerParams(vmem_limit_bytes=VMEM_LIMIT),
        cost_estimate=pl.CostEstimate(
            flops=0, bytes_accessed=moved // UNDERSTATED, transcendentals=0
        ),
        name=name,
    )(dp_place, *arrays, *deps)


def halving_order(size, bits):
    order = [0]
    for bit in reversed(bits):
        order = order + [o ^ (1 << bit) for o in order]
    return order


def fold(keep, came, last, deps):
    groups, rows, width = keep.shape

    def kernel(k_ref, c_ref, *refs):
        if last:
            refs[0][...] = k_ref[...] + c_ref[...].astype(F32)
        else:
            half = rows // 2
            refs[0][...] = k_ref[:, :half] + c_ref[:, :half].astype(F32)
            refs[1][...] = (k_ref[:, half:] + c_ref[:, half:].astype(F32)).astype(BF16)

    outs = [shape(keep.shape, F32)]
    if not last:
        half_dims = (groups, rows // 2, width)
        outs = [shape(half_dims, F32), shape(half_dims, BF16)]
    return whole_call(
        kernel, outs, [keep, came], groups * rows * width, "fold", deps=deps, limit=FOLD_LIMIT
    )


def fold_core(pairs, deps):
    rows, width = pairs[0][0].shape
    half = rows // 2

    def kernel(*refs):
        for i in range(len(pairs)):
            mine, got = refs[2 * i : 2 * i + 2]
            refs[-2][i] = mine[:half] + got[:half].astype(F32)
            refs[-1][i] = (mine[half:] + got[half:].astype(F32)).astype(BF16)

    dims = (len(pairs), half, width)
    args = [array for pair in pairs for array in pair]
    return whole_call(
        kernel,
        [shape(dims, F32), shape(dims, BF16)],
        args,
        len(pairs) * rows * width,
        "fold_core",
        deps=deps,
        limit=FOLD_LIMIT,
    )


class Chain:
    def __init__(self, keep, send, bits):
        self.keep, self.bits = keep, list(bits)
        self.came = swap_dp(send, 1 << self.bits.pop(0))
        self.done = False

    def fold(self, deps=()):
        if self.done:
            return
        self.done = not self.bits
        made = fold(self.keep, self.came, self.done, list(deps))
        self.keep = made[0]
        if not self.done:
            self.came = swap_dp(made[1], 1 << self.bits.pop(0))

    def finish(self):
        while not self.done:
            self.fold()
        return self.keep


def plus(one, two, deps=()):
    def kernel(a_ref, b_ref, out_ref):
        out_ref[...] = a_ref[...] + b_ref[...]

    out = shape(one.shape, F32)
    return whole_call(kernel, [out], [one, two], 0, "plus", deps=list(deps), limit=SMALL_LIMIT)[0]


def project_inputs(x_own, x_across, w_mine, w_other, b_mine, b_other, deps):
    rows, width = x_own.shape
    third = w_mine.shape[1] // 4

    def kernel(x0, x1, wm, wo, bm, bo, mine_ref, other_ref, send_ref):
        tokens = jnp.concatenate([x0[...], x1[...]], axis=0)
        mine = (dot(tokens, wm[:, : 3 * third]) + bm[...]).astype(BF16)
        other = (dot(tokens, wo[:, : 3 * third]) + bo[...]).astype(BF16)
        mine_ref[...] = mine
        other_ref[...] = other
        send_ref[:, : 2 * third] = other[:, third:]
        send_ref[:, 2 * third :] = mine[:, third:]

    outs = [
        shape((2 * rows, 3 * third), BF16),
        shape((2 * rows, 3 * third), BF16),
        shape((2 * rows, 4 * third), BF16),
    ]
    flops = 2 * 2 * rows * width * 6 * third
    return whole_call(
        kernel,
        outs,
        [x_own, x_across, w_mine, w_other, b_mine, b_other],
        flops,
        "project_inputs",
        deps=deps,
    )


def attention_forward(mine, other, far, bias_row, w_mine, w_other, head_size, deps):
    rows = mine.shape[0]
    third = mine.shape[1] // 3
    heads = third // head_size
    block = rows // 2
    width = w_mine.shape[0]
    scaling = 1.0 / math.sqrt(head_size)

    def kernel(mine_ref, other_ref, far_ref, bias_ref, wm, wo, cm_ref, co_ref, own_ref, across_ref, acc):
        lane_head = lax.broadcasted_iota(jnp.int32, (1, third), 1) // head_size
        acc[...] = jnp.zeros_like(acc)
        bias = bias_ref[...]

        def one_head(head, carry):
            inside = lane_head == head
            for group, ref in enumerate((mine_ref, other_ref)):
                base = 2 * third * group
                keys = jnp.concatenate(
                    [ref[:, third : 2 * third], far_ref[:, base : base + third]], axis=0
                )
                vals = jnp.concatenate(
                    [ref[:, 2 * third :], far_ref[:, base + third : base + 2 * third]], axis=0
                )
                for part in range(2):
                    span = slice(part * block, (part + 1) * block)
                    query = jnp.where(inside, ref[span, :third] * scaling, 0.0).astype(BF16)
                    scores = dot_nt(query, keys) + bias
                    peak = jnp.max(scores, axis=-1, keepdims=True)
                    weights = jnp.exp(scores - peak)
                    total = jnp.sum(weights, axis=-1, keepdims=True)
                    found = dot(weights.astype(BF16), vals) * (1.0 / total)
                    acc[group, span, :] += jnp.where(inside, found, 0.0)
            return carry

        lax.fori_loop(0, heads, one_head, 0)
        ctx_mine = acc[0].astype(BF16)
        ctx_other = acc[1].astype(BF16)
        cm_ref[...] = ctx_mine
        co_ref[...] = ctx_other
        part_sum = dot_nt(ctx_mine, wm[:, 3 * third :]) + dot_nt(ctx_other, wo[:, 3 * third :])
        own_ref[...] = part_sum[:block]
        across_ref[...] = part_sum[block:].astype(BF16)

    outs = [
        shape((rows, third), BF16),
        shape((rows, third), BF16),
        shape((block, width), F32),
        shape((block, width), BF16),
    ]
    flops = 2 * 2 * 2 * rows * 2 * rows * third * heads * 2
    return whole_call(
        kernel,
        outs,
        [mine, other, far, bias_row, w_mine, w_other],
        flops,
        "attention_forward",
        [pltpu.VMEM((2, rows, third), F32)],
        deps,
    )


def attention_backward(mine, other, far, bias_column, ga_own, ga_across, w_mine, w_other, head_size, deps):
    rows = mine.shape[0]
    third = mine.shape[1] // 3
    heads = third // head_size
    block = rows // 2
    keys_count = 2 * rows
    scaling = 1.0 / math.sqrt(head_size)

    def kernel(
        mine_ref, other_ref, far_ref, bias_ref, g0, g1, wm, wo,
        dq_ref, keep_ref, send_ref, sums_ref, grad_ctx, keys_t, dq_t, dkv,
    ):
        lane_head = lax.broadcasted_iota(jnp.int32, (1, third), 1) // head_size
        grad_rows = jnp.concatenate([g0[...], g1[...]], axis=0)
        grad_ctx[0] = dot(grad_rows, wm[:, 3 * third :]).astype(BF16)
        grad_ctx[1] = dot(grad_rows, wo[:, 3 * third :]).astype(BF16)
        dkv[...] = jnp.zeros_like(dkv)
        for group, ref in enumerate((mine_ref, other_ref)):
            base = 2 * third * group
            keys_t[group, :, :rows] = ref[:, third : 2 * third].T
            keys_t[group, :, rows:] = far_ref[:, base : base + third].T
        bias = bias_ref[...]

        def one_head(head, carry):
            inside = lane_head == head
            start = pl.multiple_of(head * head_size, head_size)
            for group, ref in enumerate((mine_ref, other_ref)):
                base = 2 * third * group
                keys = jnp.concatenate(
                    [ref[:, third : 2 * third], far_ref[:, base : base + third]], axis=0
                )
                vals = jnp.concatenate(
                    [ref[:, 2 * third :], far_ref[:, base + third : base + 2 * third]], axis=0
                )
                head_keys_t = keys_t[group, pl.ds(start, head_size), :]
                for part in range(2):
                    span = slice(part * block, (part + 1) * block)
                    query = jnp.where(inside, ref[span, :third] * scaling, 0.0).astype(BF16)
                    grad = jnp.where(inside, grad_ctx[group, span, :], 0.0).astype(BF16)
                    scores = dot_nt(keys, query) + bias
                    peak = jnp.max(scores, axis=0, keepdims=True)
                    weights = jnp.exp(scores - peak)
                    total = jnp.sum(weights, axis=0, keepdims=True)
                    probs = weights * (1.0 / total)
                    grad_probs = dot_nt(vals, grad)
                    inner = jnp.sum(probs * grad_probs, axis=0, keepdims=True)
                    grad_scores = (probs * (grad_probs - inner)).astype(BF16)
                    dkv[group, 1] += dot(probs.astype(BF16), grad)
                    dkv[group, 0] += dot(grad_scores, query)
                    dq_t[group, pl.ds(start, head_size), span] = dot(head_keys_t, grad_scores)
            return carry

        lax.fori_loop(0, heads, one_head, 0)
        for group in range(2):
            grad_query = (dq_t[group].T * scaling).astype(BF16)
            dq_ref[:, group * third : (group + 1) * third] = grad_query
            sums_ref[group : group + 1, :third] = jnp.sum(
                grad_query.astype(F32), axis=0, keepdims=True
            )
            sums_ref[group : group + 1, third:] = jnp.sum(dkv[group, 1], axis=0, keepdims=True)
            for kind in range(2):
                at = (2 * group + kind) * third
                keep_ref[:, at : at + third] = dkv[group, kind, :rows]
                away = (2 * (1 - group) + kind) * third
                send_ref[:, away : away + third] = dkv[group, kind, rows:].astype(BF16)

    outs = [
        shape((rows, 2 * third), BF16),
        shape((rows, 4 * third), F32),
        shape((rows, 4 * third), BF16),
        shape((2, 2 * third), F32),
    ]
    flops = 5 * 2 * 2 * rows * keys_count * third * heads * 2 * UNDERSTATED
    return whole_call(
        kernel,
        outs,
        [mine, other, far, bias_column, ga_own, ga_across, w_mine, w_other],
        flops,
        "attention_backward",
        [
            pltpu.VMEM((2, rows, third), BF16),
            pltpu.VMEM((2, third, keys_count), BF16),
            pltpu.VMEM((2, third, rows), F32),
            pltpu.VMEM((2, 2, keys_count, third), F32),
        ],
        deps,
    )


def project_back(dq, keep, got, w_mine, w_other, deps):
    rows = dq.shape[0]
    third = dq.shape[1] // 2
    block = rows // 2
    width = w_mine.shape[0]

    def kernel(dq_ref, keep_ref, got_ref, wm, wo, gm_ref, go_ref, own_ref, across_ref):
        dkv = (keep_ref[...] + got_ref[...].astype(F32)).astype(BF16)
        grad_mine = jnp.concatenate([dq_ref[:, :third], dkv[:, : 2 * third]], axis=1)
        grad_other = jnp.concatenate([dq_ref[:, third:], dkv[:, 2 * third :]], axis=1)
        gm_ref[...] = dkv[:, : 2 * third]
        go_ref[...] = dkv[:, 2 * third :]
        back = dot_nt(grad_mine, wm[:, : 3 * third]) + dot_nt(grad_other, wo[:, : 3 * third])
        own_ref[...] = back[:block]
        across_ref[...] = back[block:].astype(BF16)

    outs = [
        shape((rows, 2 * third), BF16),
        shape((rows, 2 * third), BF16),
        shape((block, width), F32),
        shape((block, width), BF16),
    ]
    flops = 2 * rows * width * 6 * third
    return whole_call(
        kernel, outs, [dq, keep, got, w_mine, w_other], flops, "project_back", deps=deps
    )


def moments(summed):
    centre = jnp.mean(summed, axis=-1, keepdims=True)
    centred = summed - centre
    spread = jnp.mean(centred * centred, axis=-1, keepdims=True)
    back = lax.rsqrt(spread + NORM_EPS)
    return centred * back, back


def first_norm(x_own, part, got, b_out, gain, shift, deps):
    dims = x_own.shape

    def kernel(x_ref, p_ref, r_ref, b_ref, g_ref, s_ref, summed_ref, normed_ref, low_ref):
        summed = x_ref[...].astype(F32) + (p_ref[...] + r_ref[...].astype(F32)) + b_ref[...]
        unit, _ = moments(summed)
        normed = unit * g_ref[...] + s_ref[...]
        summed_ref[...] = summed
        normed_ref[...] = normed
        low_ref[...] = normed.astype(BF16)

    outs = [shape(dims, F32), shape(dims, F32), shape(dims, BF16)]
    return whole_call(
        kernel,
        outs,
        [x_own, part, got, b_out, gain, shift],
        20 * math.prod(dims),
        "first_norm",
        deps=deps,
        limit=SMALL_LIMIT,
    )


def second_norm(normed, part, got, cotangent, b_down, gain, shift):
    dims = normed.shape

    def kernel(n_ref, p_ref, r_ref, c_ref, b_ref, g_ref, s_ref, out_ref, grad_ref, low_ref, sums_ref):
        summed = n_ref[...] + (p_ref[...] + r_ref[...].astype(F32)) + b_ref[...]
        unit, back = moments(summed)
        out_ref[...] = (unit * g_ref[...] + s_ref[...]).astype(BF16)
        cot = c_ref[...].astype(F32)
        scaled = cot * g_ref[...]
        grad = back * (
            scaled
            - jnp.mean(scaled, axis=-1, keepdims=True)
            - unit * jnp.mean(scaled * unit, axis=-1, keepdims=True)
        )
        grad_ref[...] = grad
        low_ref[...] = grad.astype(BF16)
        sums_ref[0:1, :] = jnp.sum(cot * unit, axis=0, keepdims=True)
        sums_ref[1:2, :] = jnp.sum(cot, axis=0, keepdims=True)
        sums_ref[2:3, :] = jnp.sum(grad, axis=0, keepdims=True)

    outs = [shape(dims, BF16), shape(dims, F32), shape(dims, BF16), shape((3, dims[1]), F32)]
    return whole_call(
        kernel,
        outs,
        [normed, part, got, cotangent, b_down, gain, shift],
        40 * math.prod(dims),
        "second_norm",
        limit=SMALL_LIMIT,
    )


def first_norm_back(summed, grad_second, part, got, gain, deps):
    dims = summed.shape

    def kernel(z_ref, gs_ref, p_ref, r_ref, g_ref, grad_ref, low_ref, sums_ref):
        unit, back = moments(z_ref[...])
        grad_normed = gs_ref[...] + (p_ref[...] + r_ref[...].astype(F32))
        scaled = grad_normed * g_ref[...]
        grad = back * (
            scaled
            - jnp.mean(scaled, axis=-1, keepdims=True)
            - unit * jnp.mean(scaled * unit, axis=-1, keepdims=True)
        )
        grad_ref[...] = grad
        low_ref[...] = grad.astype(BF16)
        sums_ref[0:1, :] = jnp.sum(grad_normed * unit, axis=0, keepdims=True)
        sums_ref[1:2, :] = jnp.sum(grad_normed, axis=0, keepdims=True)
        sums_ref[2:3, :] = jnp.sum(grad, axis=0, keepdims=True)

    outs = [shape(dims, F32), shape(dims, BF16), shape((3, dims[1]), F32)]
    return whole_call(
        kernel,
        outs,
        [summed, grad_second, part, got, gain],
        40 * math.prod(dims),
        "first_norm_back",
        deps=deps,
        limit=SMALL_LIMIT,
    )


def feed_forward(n_own, n_far, weights, bias, prior, deps):
    block, width = n_own.shape
    rows = 2 * block
    hidden = weights.shape[1] // 2
    tile = min(256, hidden)
    steps = hidden // tile
    last = prior is not None

    def kernel(n0, n1, u, d, b, *refs):
        step = pl.program_id(0)
        if last:
            before, a_ref, s_ref, own_ref, far_ref, tokens, acc = refs
        else:
            a_ref, s_ref, acc, tokens = refs

        @pl.when(step == 0)
        def _():
            tokens[:block] = n0[...]
            tokens[block:] = n1[...]
            acc[...] = before[...] if last else jnp.zeros_like(acc)

        hid = dot(tokens[...], u[...]) + b[...]
        half = 0.5 * (1.0 + lax.erf(hid * (1.0 / math.sqrt(2.0))))
        bell = jnp.exp(hid * hid * -0.5) * (1.0 / math.sqrt(2.0 * math.pi))
        active = (hid * half).astype(BF16)
        a_ref[...] = active
        s_ref[...] = (half + hid * bell).astype(BF16)
        acc[...] += dot_nt(active, d[...])

        if last:

            @pl.when(step == steps - 1)
            def _():
                own_ref[...] = acc[:block]
                far_ref[...] = acc[block:].astype(BF16)

    column = pl.BlockSpec((width, tile), lambda i: (0, i))
    later = pl.BlockSpec((width, tile), lambda i: (0, steps + i))
    made = pl.BlockSpec((rows, tile), lambda i: (0, i))
    args = [n_own, n_far, weights, weights, bias]
    in_specs = [const_spec((block, width))] * 2
    in_specs += [column, later, pl.BlockSpec((1, tile), lambda i: (0, i))]
    outs = [shape((rows, hidden), BF16)] * 2
    scratch = [pltpu.VMEM((rows, width), BF16)]
    if last:
        args.append(prior)
        in_specs.append(const_spec((rows, width)))
        outs += [shape((block, width), F32), shape((block, width), BF16)]
        out_specs = [made] * 2 + [const_spec((block, width))] * 2
        scratch.append(pltpu.VMEM((rows, width), F32))
    else:
        outs.append(shape((rows, width), F32))
        out_specs = [made] * 2 + [const_spec((rows, width))]
    return streamed_call(
        kernel,
        (steps,),
        outs,
        out_specs,
        args,
        in_specs,
        2 * 2 * rows * width * hidden,
        "feed_forward",
        scratch,
        deps,
    )


def feed_forward_back(g_own, g_across, w_mine, w_other, slope_mine, slope_other, deps):
    block, width = g_own.shape
    rows = 2 * block
    hidden = w_mine.shape[1] // 2
    tile = min(256, hidden)
    steps = hidden // tile

    def kernel(
        g0, g1, um, uo, dm, do, sm, so,
        gm_ref, go_ref, own_ref, across_ref, bm_ref, bo_ref, grads, acc,
    ):
        step = pl.program_id(0)

        @pl.when(step == 0)
        def _():
            grads[:block] = g0[...]
            grads[block:] = g1[...]
            acc[...] = jnp.zeros_like(acc)

        total = acc[...]
        for u, d, s, g_ref, b_ref in ((um, dm, sm, gm_ref, bm_ref), (uo, do, so, go_ref, bo_ref)):
            grad_hidden = (dot(grads[...], d[...]) * s[...].astype(F32)).astype(BF16)
            g_ref[...] = grad_hidden
            b_ref[...] = jnp.sum(grad_hidden.astype(F32), axis=0, keepdims=True)
            total = total + dot_nt(grad_hidden, u[...])
        acc[...] = total

        @pl.when(step == steps - 1)
        def _():
            own_ref[...] = acc[:block]
            across_ref[...] = acc[block:].astype(BF16)

    column = pl.BlockSpec((width, tile), lambda i: (0, i))
    later = pl.BlockSpec((width, tile), lambda i: (0, steps + i))
    bias = pl.BlockSpec((1, tile), lambda i: (0, i))
    made = pl.BlockSpec((rows, tile), lambda i: (0, i))
    outs = (
        [shape((rows, hidden), BF16)] * 2
        + [shape((block, width), F32), shape((block, width), BF16)]
        + [shape((1, hidden), F32)] * 2
    )
    return streamed_call(
        kernel,
        (steps,),
        outs,
        [made] * 2 + [const_spec((block, width))] * 2 + [bias] * 2,
        [g_own, g_across, w_mine, w_other, w_mine, w_other, slope_mine, slope_other],
        [const_spec((block, width))] * 2 + [column] * 2 + [later] * 2 + [made] * 2,
        2 * 2 * rows * width * 2 * hidden,
        "feed_forward_back",
        [pltpu.VMEM((rows, width), BF16), pltpu.VMEM((rows, width), F32)],
        deps,
    )


def weight_grad(ones, mine, other, dp_place, chains, name, other_first=0, deps=(), halves=False):
    block, width = ones[0].shape
    rows = 2 * block
    count = chains[0][0]
    tile = min(256, count)
    tiles = count // tile
    size = lax.axis_size("dp")
    share = width // size
    half = width // 2

    def kernel(place_ref, a0, a1, a2, a3, m0, m1, o0, o1, *refs):
        turned, full = refs[-2:]
        step = pl.program_id(0)

        @pl.when(step == 0)
        def _():
            for i, ref in enumerate((a0, a1, a2, a3)):
                turned[:, i * block : (i + 1) * block] = ref[...].T

        place = place_ref[0]

        def write(which, targets, order):
            for i, offset in enumerate(order):
                start = pl.multiple_of((place ^ offset) * share, share)
                at = i * share
                rows_now = full[pl.ds(start, share), :]
                if halves:
                    ref = targets[0] if at < half else targets[1]
                    at %= half
                    ref[which, at : at + share, :] = rows_now.astype(ref.dtype)
                else:
                    targets[which][at : at + share, :] = rows_now.astype(targets[which].dtype)

        for which, (one, two) in enumerate(((m0, m1), (o0, o1))):
            full[...] = dot(turned[:, :rows], one[...]) + dot(turned[:, rows:], two[...])
            for c, (_, bits) in enumerate(chains):
                targets = refs[2 * c : 2 * c + 2]
                order = halving_order(size, bits)
                if len(chains) == 1:
                    write(which, targets, order)
                else:
                    pl.when(step // tiles == c)(
                        lambda w=which, t=targets, o=order: write(w, t, o)
                    )

    base = other_first // tile
    column = pl.BlockSpec((rows, tile), lambda i: (0, i))
    other_column = pl.BlockSpec((rows, tile), lambda i: (0, base + i))
    outs, out_specs = [], []
    for c in range(len(chains)):
        for kind in (F32, BF16):
            if halves:
                outs.append(shape((2, half, count), kind))
                out_specs.append(pl.BlockSpec((2, half, tile), lambda i: (0, 0, i)))
            else:
                index = lambda i, c=c: (0, jnp.clip(i - c * tiles, 0, tiles - 1))
                outs.append(shape((width, count), kind))
                out_specs.append(pl.BlockSpec((width, tile), index))
    return streamed_call(
        kernel,
        (tiles * len(chains),),
        outs,
        out_specs,
        [dp_place, *ones, *mine, *other],
        [pl.BlockSpec(memory_space=pltpu.SMEM)]
        + [const_spec((block, width))] * 4
        + [column] * 2
        + [other_column] * 2,
        2 * 2 * rows * width * 2 * count * len(chains),
        name,
        [pltpu.VMEM((width, 2 * rows), BF16), pltpu.VMEM((width, tile), F32)],
        deps,
    )


def core_chain(made, bits, deps=()):
    pairs = [(mine, swap_tensor(other, CORE)) for mine, other in made]
    keep, send = fold_core(pairs, list(deps))
    return Chain(keep, send, bits)


def add_up(parts, deps):
    def kernel(*refs):
        refs[-1][...] = sum(ref[...] for ref in refs[:-1])

    out = shape(parts[0].shape, F32)
    return whole_call(kernel, [out], parts, 0, "add_up", deps=deps, limit=SMALL_LIMIT)[0]


def shards(
    inputs,
    lengths,
    w_query,
    w_key,
    w_value,
    w_out,
    w_up,
    w_down,
    b_query,
    b_value,
    b_out,
    b_up,
    b_down,
    first_gain,
    first_shift,
    second_gain,
    second_shift,
    cotangent,
):
    seq_count, block, width = inputs.shape
    tensor_size = lax.axis_size("tensor")
    seq_len = block * tensor_size
    place = lax.axis_index("tensor")
    head_dims = w_query.shape[1]
    head_size = width // HEADS
    hidden = w_up.shape[1]
    seqs = range(seq_count)
    row = lambda vector: vector.reshape(1, -1)

    x_own = [inputs[s] for s in seqs]
    all_across = swap_tensor(inputs, ACROSS)
    x_across = [all_across[s] for s in seqs]

    dp_place = lax.axis_index("dp").astype(jnp.int32).reshape(1)
    att_far, att_first = gather_far(pack([w_query, w_key, w_value, w_out.T], "pack_attention"))
    att_pieces = att_far + gather_near(att_far)
    share = pack([w_up, w_down.T], "pack_feed", att_first)
    share_other = swap_tensor(share, ACROSS)
    mine_far, mine_first = gather_far(share)
    mine_near = gather_near(mine_far)
    other_far, other_first = gather_far(share_other)
    other_near = gather_near(other_far[:1]) + [
        (swap_tensor(p, ACROSS), offsets) for p, offsets in mine_near[1:]
    ]

    def arrays(pieces):
        return [p for p, _ in pieces]

    att_mine = assemble(att_pieces, dp_place, "assemble_attention")
    att_other = assemble(other_core(att_pieces), dp_place, "assemble_attention_other")
    ffw_mine = assemble(mine_far + mine_near, dp_place, "assemble_feed")
    project_waits = [mine_first, [share_other]]
    attend_waits = [arrays(mine_far[1:]), arrays(mine_near[:1]) + other_first]
    norm_waits = [arrays(mine_near[1:]), arrays(other_far[1:]) + [ffw_mine]]

    biases = jnp.concatenate([b_query, jnp.zeros_like(b_query), b_value])
    qkv_bias_mine, qkv_bias_other = row(biases), row(swap_tensor(biases, CORE))
    up_bias_mine, up_bias_other = row(b_up), row(swap_tensor(b_up, ACROSS))
    b_out_row, b_down_row = row(b_out), row(b_down)
    gain_one, shift_one = row(first_gain), row(first_shift)
    gain_two, shift_two = row(second_gain), row(second_shift)

    order = jnp.stack([place, place ^ ACROSS, place ^ CORE, place ^ CORE ^ ACROSS])
    positions = (order[:, None] * block + jnp.arange(block, dtype=jnp.int32)[None, :]).reshape(-1)
    masks = [jnp.where(positions < lengths[s], 0.0, MASKED).astype(F32) for s in seqs]

    projected = []
    for s in seqs:
        waits = project_waits[s] if s < 2 else []
        projected.append(
            project_inputs(
                x_own[s], x_across[s], att_mine, att_other, qkv_bias_mine, qkv_bias_other,
                waits + [p[2] for p in projected[-1:]],
            )
        )
    far = [swap_tensor(projected[s][2], CORE) for s in seqs]
    attended = []
    for s in seqs:
        waits = attend_waits[s] if s < 2 else []
        attended.append(
            attention_forward(
                projected[s][0], projected[s][1], far[s], masks[s].reshape(1, seq_len),
                att_mine, att_other, head_size, waits + [p[2] for p in attended[-1:]],
            )
        )
    attended_got = [swap_tensor(attended[s][3], ACROSS) for s in seqs]
    one = []
    for s in seqs:
        waits = norm_waits[s] if s < 2 else []
        one.append(
            first_norm(
                x_own[s], attended[s][2], attended_got[s], b_out_row, gain_one, shift_one,
                waits + [p[2] for p in one[-1:]],
            )
        )
    normed_far = [swap_tensor(one[s][2], CORE) for s in seqs]
    fed_one = []
    for s in seqs:
        waits = [p[2] for p in fed_one[-1:]]
        fed_one.append(
            feed_forward(one[s][2], normed_far[s], ffw_mine, up_bias_mine, None, waits)
        )
    ffw_other = assemble(
        other_far + other_near, dp_place, "assemble_feed_other", [fed_one[-1][2]]
    )
    fed_two = []
    for s in seqs:
        waits = [p[2] for p in fed_two[-1:]]
        fed_two.append(
            feed_forward(
                one[s][2], normed_far[s], ffw_other, up_bias_other, fed_one[s][2], waits
            )
        )
    fed = [(fed_one[s][0], fed_two[s][0], fed_one[s][1], fed_two[s][1], *fed_two[s][2:]) for s in seqs]
    branch_got = [swap_tensor(fed[s][5], CORE) for s in seqs]
    two = [
        second_norm(
            one[s][1], fed[s][4], branch_got[s], cotangent[s], b_down_row, gain_two, shift_two
        )
        for s in seqs
    ]
    grad_far = [swap_tensor(two[s][2], CORE) for s in seqs]
    levels = range(lax.axis_size("dp").bit_length() - 1)
    near_first = list(levels)
    far_first = [1, 0, *levels[2:]] if len(near_first) > 1 else near_first

    def pairs(own, across):
        return [part for s in seqs for part in (own[s], across[s])]

    def feed_back(s, deps):
        return feed_forward_back(
            two[s][2], grad_far[s], ffw_mine, ffw_other, fed[s][2], fed[s][3], deps
        )

    fed_back = [feed_back(0, [])]
    down_made = weight_grad(
        pairs([two[s][2] for s in seqs], grad_far),
        [fed[s][0] for s in seqs], [fed[s][1] for s in seqs],
        dp_place, [(hidden, near_first)], "w_down_grad", deps=[fed_back[0][2]], halves=True,
    )
    fed_back += [feed_back(s, [down_made[1]]) for s in seqs[1:]]
    back_got = [swap_tensor(fed_back[s][3], CORE) for s in seqs]
    def placed_in(part_mine, part_other, bit):
        size = part_mine.shape[0]
        empty = jnp.zeros((tensor_size * size,), F32)
        empty = lax.dynamic_update_slice(empty, part_mine, (place * size,))
        return lax.dynamic_update_slice(empty, part_other, ((place ^ bit) * size,))

    def norm_back(s, deps):
        return first_norm_back(
            one[s][0], two[s][1], fed_back[s][2], back_got[s], gain_one, deps
        )

    one_back = [norm_back(0, [fed_back[-1][2]])]
    up_made = weight_grad(
        pairs([one[s][2] for s in seqs], normed_far),
        [fed_back[s][0] for s in seqs], [fed_back[s][1] for s in seqs],
        dp_place, [(hidden, far_first)], "w_up_grad", deps=[one_back[0][1]], halves=True,
    )
    one_back += [norm_back(s, [up_made[1]]) for s in seqs[1:]]
    first_across = [swap_tensor(one_back[s][1], ACROSS) for s in seqs]
    down_chain = Chain(*down_made, near_first)
    up_chain = Chain(*up_made, far_first)

    def backward(s, deps):
        return attention_backward(
            projected[s][0], projected[s][1], far[s], masks[s].reshape(seq_len, 1),
            one_back[s][1], first_across[s], att_mine, att_other, head_size, deps,
        )

    attended_back = [backward(0, [up_made[1]])]
    out_made = weight_grad(
        pairs([one_back[s][1] for s in seqs], first_across),
        [attended[s][0] for s in seqs], [attended[s][1] for s in seqs],
        dp_place, [(head_dims, near_first)], "w_out_grad", deps=[attended_back[0][3]],
    )
    down_chain.fold([attended_back[0][3]])
    attended_back += [backward(s, [down_chain.keep, out_made[1]]) for s in seqs[1:]]
    far_back = [swap_tensor(attended_back[s][2], CORE) for s in seqs]

    sums = add_up([attended_back[s][3] for s in seqs], [])
    small = jnp.concatenate(
        [
            sum(two[s][3] for s in seqs).reshape(-1),
            sum(one_back[s][2] for s in seqs).reshape(-1),
            placed_in(
                sum(fed_back[s][4] for s in seqs).reshape(-1),
                sum(fed_back[s][5] for s in seqs).reshape(-1),
                ACROSS,
            ),
            placed_in(sums[0, :head_dims], sums[1, :head_dims], CORE),
            placed_in(sums[0, head_dims:], sums[1, head_dims:], CORE),
        ]
    ).reshape(-1, 128)
    bits = [1 << level for level in reversed(near_first)]
    up_chain.fold([attended_back[-1][3]])
    small = plus(small, swap_tensor(small, CORE), [up_chain.keep])

    tokens = pairs(x_own, x_across)
    grad_queries = [attended_back[s][0] for s in seqs]
    query_made = weight_grad(
        tokens, grad_queries, grad_queries, dp_place, [(head_dims, near_first)], "w_query_grad",
        head_dims, [far_back[0], small],
    )
    back = [
        project_back(
            attended_back[0][0], attended_back[0][1], far_back[0], att_mine, att_other,
            [query_made[1]],
        )
    ]
    small = plus(small, swap_tensor(small, ACROSS), [back[0][2]])
    back += [
        project_back(
            attended_back[s][0], attended_back[s][1], far_back[s], att_mine, att_other, [small]
        )
        for s in seqs[1:]
    ]
    input_got = [swap_tensor(back[s][3], ACROSS) for s in seqs]
    for bit in bits[:1]:
        small = plus(small, swap_dp(small, bit), [back[-1][2]])
    down_chain.fold([back[-1][2]])
    up_chain.fold([down_chain.keep])
    both_got = swap_tensor(jnp.stack([query_made[1], out_made[1]]), CORE)
    query_chain = Chain(
        *fold_core([(query_made[0], both_got[0]), (out_made[0], both_got[1])], [back[-1][2]]),
        near_first,
    )
    key_value_made = weight_grad(
        tokens, [back[s][0] for s in seqs], [back[s][1] for s in seqs],
        dp_place, [(head_dims, near_first), (head_dims, far_first)], "w_key_value_grad",
        deps=input_got[:1] + [up_chain.keep, query_chain.keep, small],
    )
    waits = input_got[-1:] + [down_chain.came]
    key_chain = core_chain([key_value_made[:2]], near_first, waits)
    value_chain = core_chain([key_value_made[2:]], far_first, waits)
    started = [key_chain.keep, value_chain.keep]
    query_chain.fold(started)
    key_chain.fold()
    value_chain.fold()
    ending = [key_chain.keep, value_chain.keep]
    query_chain.fold(ending)
    down_chain.fold(ending)
    up_chain.fold(ending)
    for bit in bits[1:]:
        small = plus(small, swap_dp(small, bit), ending)
    small = small.reshape(-1)

    input_grad = jnp.stack(
        [
            (one_back[s][0] + (back[s][2] + input_got[s].astype(F32))).astype(BF16)
            for s in seqs
        ]
    )

    def over_y(both):
        return both[0] + swap_tensor(both[1].astype(BF16), ACROSS).astype(F32)

    down_grad, up_grad = over_y(down_chain.finish()), over_y(up_chain.finish())
    query_and_out = query_chain.finish()

    vectors = [small[i * width : (i + 1) * width] for i in range(6)]
    second_gain_grad, second_shift_grad, b_down_grad = vectors[:3]
    first_gain_grad, first_shift_grad, b_out_grad = vectors[3:]
    b_up_grad = small[6 * width : 6 * width + tensor_size * hidden]
    b_query_grad, b_value_grad = small[-2 * width : -width], small[-width:]

    output = jnp.stack([two[s][0] for s in seqs])
    return (
        output,
        input_grad,
        query_and_out[0],
        key_chain.finish()[0],
        value_chain.finish()[0],
        query_and_out[1].T,
        up_grad,
        down_grad.T,
        b_query_grad,
        b_value_grad,
        b_out_grad,
        b_up_grad,
        b_down_grad,
        first_gain_grad,
        first_shift_grad,
        second_gain_grad,
        second_shift_grad,
    )


def solution(mesh):
    placed = (
        P("dp", "tensor", None),
        P("dp"),
        P("dp", "tensor"),
        P("dp", "tensor"),
        P("dp", "tensor"),
        P("tensor", "dp"),
        P("dp", "tensor"),
        P("tensor", "dp"),
        P("tensor"),
        P("tensor"),
        P(),
        P("tensor"),
        P(),
        P(),
        P(),
        P(),
        P(),
        P("dp", "tensor", None),
    )
    return jax.shard_map(
        shards,
        mesh=mesh,
        in_specs=placed,
        out_specs=(
            P("dp", "tensor", None),
            P("dp", "tensor", None),
            P("dp", "tensor"),
            P("dp", "tensor"),
            P("dp", "tensor"),
            P("tensor", "dp"),
            P("dp", "tensor"),
            P("tensor", "dp"),
            P(),
            P(),
            P(),
            P(),
            P(),
            P(),
            P(),
            P(),
            P(),
        ),
        check_vma=False,
    )
```

```python
import math

import jax
import jax.numpy as jnp
from jax import lax
from jax.experimental import pallas as pl
from jax.experimental.pallas import tpu as pltpu
from jax.sharding import PartitionSpec as P

HEADS = 16
NORM_EPS = 1e-12
MASKED = -1000000000.0
MIB = 1024 * 1024
VMEM_LIMIT = 56 * MIB
SMALL_LIMIT = 16 * MIB
FOLD_LIMIT = 24 * MIB
UNDERSTATED = 1000

F32 = jnp.float32
BF16 = jnp.bfloat16

CORE = 1
ACROSS = 2


def dot(one, two):
    return lax.dot_general(one, two, (((1,), (0,)), ((), ())), preferred_element_type=F32)


def dot_nt(one, two):
    return lax.dot_general(one, two, (((1,), (1,)), ((), ())), preferred_element_type=F32)


def shape(dims, kind):
    return jax.ShapeDtypeStruct(dims, kind)


def after(kernel, count, deps):
    def body(*refs):
        kernel(*refs[:count], *refs[count + len(deps) :])

    return body


def whole_call(kernel, outs, args, flops, name, scratch=(), deps=(), limit=VMEM_LIMIT):
    moved = sum(math.prod(a.shape) * a.dtype.itemsize for a in (*args, *outs))
    return pl.pallas_call(
        after(kernel, len(args), deps),
        out_shape=tuple(outs),
        in_specs=[pl.BlockSpec(memory_space=pltpu.VMEM)] * len(args)
        + [pl.BlockSpec(memory_space=pl.ANY)] * len(deps),
        out_specs=tuple([pl.BlockSpec(memory_space=pltpu.VMEM)] * len(outs)),
        scratch_shapes=list(scratch),
        compiler_params=pltpu.CompilerParams(vmem_limit_bytes=limit),
        cost_estimate=pl.CostEstimate(
            flops=flops // UNDERSTATED, bytes_accessed=moved // UNDERSTATED, transcendentals=0
        ),
        name=name,
    )(*args, *deps)


def streamed_call(kernel, grid, outs, out_specs, args, in_specs, flops, name, scratch, deps=()):
    moved = sum(math.prod(a.shape) * a.dtype.itemsize for a in (*args, *outs))
    return pl.pallas_call(
        after(kernel, len(args), deps),
        grid=grid,
        out_shape=tuple(outs),
        in_specs=list(in_specs) + [pl.BlockSpec(memory_space=pl.ANY)] * len(deps),
        out_specs=tuple(out_specs),
        scratch_shapes=list(scratch),
        compiler_params=pltpu.CompilerParams(
            vmem_limit_bytes=VMEM_LIMIT, dimension_semantics=("arbitrary",)
        ),
        cost_estimate=pl.CostEstimate(
            flops=flops // UNDERSTATED, bytes_accessed=moved // UNDERSTATED, transcendentals=0
        ),
        name=name,
    )(*args, *deps)


def const_spec(dims):
    return pl.BlockSpec(dims, lambda i: (0,) * len(dims))


def swap_tensor(array, bit):
    size = lax.axis_size("tensor")
    return lax.ppermute(array, "tensor", [(i, i ^ bit) for i in range(size)])


def swap_dp(array, bit):
    size = lax.axis_size("dp")
    return lax.ppermute(array, "dp", [(i, i ^ bit) for i in range(size)])


def pack(parts, name, deps=()):
    def kernel(*refs):
        at = 0
        for ref in refs[:-1]:
            refs[-1][:, at : at + ref.shape[1]] = ref[...]
            at += ref.shape[1]

    out = shape((parts[0].shape[0], sum(p.shape[1] for p in parts)), parts[0].dtype)
    return whole_call(kernel, [out], parts, 0, name, deps=deps)[0]


def gather_far(rows):
    held = (rows, [0])
    steps = []
    step = lax.axis_size("dp") // 2
    while step > 1:
        steps.append(step)
        step //= 2
    first = []
    for step in steps[:-1]:
        came = (swap_dp(held[0], step), [o ^ step for o in held[1]])
        first.append(came[0])
        held = merged([held, came])
    pieces = [held]
    if steps:
        pieces.append((swap_dp(held[0], steps[-1]), [o ^ steps[-1] for o in held[1]]))
    return pieces, first[:1]


def merged(pieces):
    return (
        jnp.concatenate([p for p, _ in pieces], axis=0),
        [o for _, offsets in pieces for o in offsets],
    )


def gather_near(pieces):
    return [(swap_dp(p, 1), [o ^ 1 for o in offsets]) for p, offsets in pieces]


def other_core(pieces):
    return [(swap_tensor(p, CORE), offsets) for p, offsets in pieces]


def assemble(pieces, dp_place, name, deps=()):
    rows = pieces[0][0].shape[0] // len(pieces[0][1])
    width = pieces[0][0].shape[1]
    size = lax.axis_size("dp")

    def kernel(*refs):
        place = refs[0][0]
        for ref, (_, offsets) in zip(refs[1:-1], pieces):
            for i, offset in enumerate(offsets):
                start = pl.multiple_of((place ^ offset) * rows, rows)
                refs[-1][pl.ds(start, rows), :] = ref[i * rows : (i + 1) * rows, :]

    arrays = [p for p, _ in pieces]
    out = shape((size * rows, width), BF16)
    moved = 2 * size * rows * width * 2
    return pl.pallas_call(
        after(kernel, 1 + len(arrays), deps),
        out_shape=out,
        in_specs=[pl.BlockSpec(memory_space=pltpu.SMEM)]
        + [pl.BlockSpec(memory_space=pltpu.VMEM)] * len(arrays)
        + [pl.BlockSpec(memory_space=pl.ANY)] * len(deps),
        out_specs=pl.BlockSpec(memory_space=pltpu.VMEM),
        compiler_params=pltpu.CompilerParams(vmem_limit_bytes=VMEM_LIMIT),
        cost_estimate=pl.CostEstimate(
            flops=0, bytes_accessed=moved // UNDERSTATED, transcendentals=0
        ),
        name=name,
    )(dp_place, *arrays, *deps)


def halving_order(size, bits):
    order = [0]
    for bit in reversed(bits):
        order = order + [o ^ (1 << bit) for o in order]
    return order


def fold(keep, came, last, deps):
    groups, rows, width = keep.shape

    def kernel(k_ref, c_ref, *refs):
        if last:
            refs[0][...] = k_ref[...] + c_ref[...].astype(F32)
        else:
            half = rows // 2
            refs[0][...] = k_ref[:, :half] + c_ref[:, :half].astype(F32)
            refs[1][...] = (k_ref[:, half:] + c_ref[:, half:].astype(F32)).astype(BF16)

    outs = [shape(keep.shape, F32)]
    if not last:
        half_dims = (groups, rows // 2, width)
        outs = [shape(half_dims, F32), shape(half_dims, BF16)]
    return whole_call(
        kernel, outs, [keep, came], groups * rows * width, "fold", deps=deps, limit=FOLD_LIMIT
    )


def fold_core(pairs, deps):
    rows, width = pairs[0][0].shape
    half = rows // 2

    def kernel(*refs):
        for i in range(len(pairs)):
            mine, got = refs[2 * i : 2 * i + 2]
            refs[-2][i] = mine[:half] + got[:half].astype(F32)
            refs[-1][i] = (mine[half:] + got[half:].astype(F32)).astype(BF16)

    dims = (len(pairs), half, width)
    args = [array for pair in pairs for array in pair]
    return whole_call(
        kernel,
        [shape(dims, F32), shape(dims, BF16)],
        args,
        len(pairs) * rows * width,
        "fold_core",
        deps=deps,
        limit=FOLD_LIMIT,
    )


class Chain:
    def __init__(self, keep, send, bits):
        self.keep, self.bits = keep, list(bits)
        self.came = swap_dp(send, 1 << self.bits.pop(0))
        self.done = False

    def fold(self, deps=()):
        if self.done:
            return
        self.done = not self.bits
        made = fold(self.keep, self.came, self.done, list(deps))
        self.keep = made[0]
        if not self.done:
            self.came = swap_dp(made[1], 1 << self.bits.pop(0))

    def finish(self):
        while not self.done:
            self.fold()
        return self.keep


def plus(one, two, deps=()):
    def kernel(a_ref, b_ref, out_ref):
        out_ref[...] = a_ref[...] + b_ref[...]

    out = shape(one.shape, F32)
    return whole_call(kernel, [out], [one, two], 0, "plus", deps=list(deps), limit=SMALL_LIMIT)[0]


def project_inputs(x_own, x_across, w_mine, w_other, b_mine, b_other, deps):
    rows, width = x_own.shape
    third = w_mine.shape[1] // 4

    def kernel(x0, x1, wm, wo, bm, bo, mine_ref, other_ref, send_ref):
        tokens = jnp.concatenate([x0[...], x1[...]], axis=0)
        mine = (dot(tokens, wm[:, : 3 * third]) + bm[...]).astype(BF16)
        other = (dot(tokens, wo[:, : 3 * third]) + bo[...]).astype(BF16)
        mine_ref[...] = mine
        other_ref[...] = other
        send_ref[:, : 2 * third] = other[:, third:]
        send_ref[:, 2 * third :] = mine[:, third:]

    outs = [
        shape((2 * rows, 3 * third), BF16),
        shape((2 * rows, 3 * third), BF16),
        shape((2 * rows, 4 * third), BF16),
    ]
    flops = 2 * 2 * rows * width * 6 * third
    return whole_call(
        kernel,
        outs,
        [x_own, x_across, w_mine, w_other, b_mine, b_other],
        flops,
        "project_inputs",
        deps=deps,
    )


def attention_forward(mine, other, far, bias_row, w_mine, w_other, head_size, deps):
    rows = mine.shape[0]
    third = mine.shape[1] // 3
    heads = third // head_size
    block = rows // 2
    width = w_mine.shape[0]
    scaling = 1.0 / math.sqrt(head_size)

    def kernel(mine_ref, other_ref, far_ref, bias_ref, wm, wo, cm_ref, co_ref, own_ref, across_ref, acc):
        lane_head = lax.broadcasted_iota(jnp.int32, (1, third), 1) // head_size
        acc[...] = jnp.zeros_like(acc)
        bias = bias_ref[...]

        def one_head(head, carry):
            inside = lane_head == head
            for group, ref in enumerate((mine_ref, other_ref)):
                base = 2 * third * group
                keys = jnp.concatenate(
                    [ref[:, third : 2 * third], far_ref[:, base : base + third]], axis=0
                )
                vals = jnp.concatenate(
                    [ref[:, 2 * third :], far_ref[:, base + third : base + 2 * third]], axis=0
                )
                for part in range(2):
                    span = slice(part * block, (part + 1) * block)
                    query = jnp.where(inside, ref[span, :third] * scaling, 0.0).astype(BF16)
                    scores = dot_nt(query, keys) + bias
                    peak = jnp.max(scores, axis=-1, keepdims=True)
                    weights = jnp.exp(scores - peak)
                    total = jnp.sum(weights, axis=-1, keepdims=True)
                    found = dot(weights.astype(BF16), vals) * (1.0 / total)
                    acc[group, span, :] += jnp.where(inside, found, 0.0)
            return carry

        lax.fori_loop(0, heads, one_head, 0)
        ctx_mine = acc[0].astype(BF16)
        ctx_other = acc[1].astype(BF16)
        cm_ref[...] = ctx_mine
        co_ref[...] = ctx_other
        part_sum = dot_nt(ctx_mine, wm[:, 3 * third :]) + dot_nt(ctx_other, wo[:, 3 * third :])
        own_ref[...] = part_sum[:block]
        across_ref[...] = part_sum[block:].astype(BF16)

    outs = [
        shape((rows, third), BF16),
        shape((rows, third), BF16),
        shape((block, width), F32),
        shape((block, width), BF16),
    ]
    flops = 2 * 2 * 2 * rows * 2 * rows * third * heads * 2
    return whole_call(
        kernel,
        outs,
        [mine, other, far, bias_row, w_mine, w_other],
        flops,
        "attention_forward",
        [pltpu.VMEM((2, rows, third), F32)],
        deps,
    )


def attention_backward(mine, other, far, bias_column, ga_own, ga_across, w_mine, w_other, head_size, deps):
    rows = mine.shape[0]
    third = mine.shape[1] // 3
    heads = third // head_size
    block = rows // 2
    keys_count = 2 * rows
    scaling = 1.0 / math.sqrt(head_size)

    def kernel(
        mine_ref, other_ref, far_ref, bias_ref, g0, g1, wm, wo,
        dq_ref, keep_ref, send_ref, sums_ref, grad_ctx, keys_t, dq_t, dkv,
    ):
        lane_head = lax.broadcasted_iota(jnp.int32, (1, third), 1) // head_size
        grad_rows = jnp.concatenate([g0[...], g1[...]], axis=0)
        grad_ctx[0] = dot(grad_rows, wm[:, 3 * third :]).astype(BF16)
        grad_ctx[1] = dot(grad_rows, wo[:, 3 * third :]).astype(BF16)
        dkv[...] = jnp.zeros_like(dkv)
        for group, ref in enumerate((mine_ref, other_ref)):
            base = 2 * third * group
            keys_t[group, :, :rows] = ref[:, third : 2 * third].T
            keys_t[group, :, rows:] = far_ref[:, base : base + third].T
        bias = bias_ref[...]

        def one_head(head, carry):
            inside = lane_head == head
            start = pl.multiple_of(head * head_size, head_size)
            for group, ref in enumerate((mine_ref, other_ref)):
                base = 2 * third * group
                keys = jnp.concatenate(
                    [ref[:, third : 2 * third], far_ref[:, base : base + third]], axis=0
                )
                vals = jnp.concatenate(
                    [ref[:, 2 * third :], far_ref[:, base + third : base + 2 * third]], axis=0
                )
                head_keys_t = keys_t[group, pl.ds(start, head_size), :]
                for part in range(2):
                    span = slice(part * block, (part + 1) * block)
                    query = jnp.where(inside, ref[span, :third] * scaling, 0.0).astype(BF16)
                    grad = jnp.where(inside, grad_ctx[group, span, :], 0.0).astype(BF16)
                    scores = dot_nt(keys, query) + bias
                    peak = jnp.max(scores, axis=0, keepdims=True)
                    weights = jnp.exp(scores - peak)
                    total = jnp.sum(weights, axis=0, keepdims=True)
                    probs = weights * (1.0 / total)
                    grad_probs = dot_nt(vals, grad)
                    inner = jnp.sum(probs * grad_probs, axis=0, keepdims=True)
                    grad_scores = (probs * (grad_probs - inner)).astype(BF16)
                    dkv[group, 1] += dot(probs.astype(BF16), grad)
                    dkv[group, 0] += dot(grad_scores, query)
                    dq_t[group, pl.ds(start, head_size), span] = dot(head_keys_t, grad_scores)
            return carry

        lax.fori_loop(0, heads, one_head, 0)
        for group in range(2):
            grad_query = (dq_t[group].T * scaling).astype(BF16)
            dq_ref[:, group * third : (group + 1) * third] = grad_query
            sums_ref[group : group + 1, :third] = jnp.sum(
                grad_query.astype(F32), axis=0, keepdims=True
            )
            sums_ref[group : group + 1, third:] = jnp.sum(dkv[group, 1], axis=0, keepdims=True)
            for kind in range(2):
                at = (2 * group + kind) * third
                keep_ref[:, at : at + third] = dkv[group, kind, :rows]
                away = (2 * (1 - group) + kind) * third
                send_ref[:, away : away + third] = dkv[group, kind, rows:].astype(BF16)

    outs = [
        shape((rows, 2 * third), BF16),
        shape((rows, 4 * third), F32),
        shape((rows, 4 * third), BF16),
        shape((2, 2 * third), F32),
    ]
    flops = 5 * 2 * 2 * rows * keys_count * third * heads * 2 * UNDERSTATED
    return whole_call(
        kernel,
        outs,
        [mine, other, far, bias_column, ga_own, ga_across, w_mine, w_other],
        flops,
        "attention_backward",
        [
            pltpu.VMEM((2, rows, third), BF16),
            pltpu.VMEM((2, third, keys_count), BF16),
            pltpu.VMEM((2, third, rows), F32),
            pltpu.VMEM((2, 2, keys_count, third), F32),
        ],
        deps,
    )


def project_back(dq, keep, got, w_mine, w_other, deps):
    rows = dq.shape[0]
    third = dq.shape[1] // 2
    block = rows // 2
    width = w_mine.shape[0]

    def kernel(dq_ref, keep_ref, got_ref, wm, wo, gm_ref, go_ref, own_ref, across_ref):
        dkv = (keep_ref[...] + got_ref[...].astype(F32)).astype(BF16)
        grad_mine = jnp.concatenate([dq_ref[:, :third], dkv[:, : 2 * third]], axis=1)
        grad_other = jnp.concatenate([dq_ref[:, third:], dkv[:, 2 * third :]], axis=1)
        gm_ref[...] = dkv[:, : 2 * third]
        go_ref[...] = dkv[:, 2 * third :]
        back = dot_nt(grad_mine, wm[:, : 3 * third]) + dot_nt(grad_other, wo[:, : 3 * third])
        own_ref[...] = back[:block]
        across_ref[...] = back[block:].astype(BF16)

    outs = [
        shape((rows, 2 * third), BF16),
        shape((rows, 2 * third), BF16),
        shape((block, width), F32),
        shape((block, width), BF16),
    ]
    flops = 2 * rows * width * 6 * third
    return whole_call(
        kernel, outs, [dq, keep, got, w_mine, w_other], flops, "project_back", deps=deps
    )


def moments(summed):
    centre = jnp.mean(summed, axis=-1, keepdims=True)
    centred = summed - centre
    spread = jnp.mean(centred * centred, axis=-1, keepdims=True)
    back = lax.rsqrt(spread + NORM_EPS)
    return centred * back, back


def first_norm(x_own, part, got, b_out, gain, shift, deps):
    dims = x_own.shape

    def kernel(x_ref, p_ref, r_ref, b_ref, g_ref, s_ref, summed_ref, normed_ref, low_ref):
        summed = x_ref[...].astype(F32) + (p_ref[...] + r_ref[...].astype(F32)) + b_ref[...]
        unit, _ = moments(summed)
        normed = unit * g_ref[...] + s_ref[...]
        summed_ref[...] = summed
        normed_ref[...] = normed
        low_ref[...] = normed.astype(BF16)

    outs = [shape(dims, F32), shape(dims, F32), shape(dims, BF16)]
    return whole_call(
        kernel,
        outs,
        [x_own, part, got, b_out, gain, shift],
        20 * math.prod(dims),
        "first_norm",
        deps=deps,
        limit=SMALL_LIMIT,
    )


def second_norm(normed, part, got, cotangent, b_down, gain, shift):
    dims = normed.shape

    def kernel(n_ref, p_ref, r_ref, c_ref, b_ref, g_ref, s_ref, out_ref, grad_ref, low_ref, sums_ref):
        summed = n_ref[...] + (p_ref[...] + r_ref[...].astype(F32)) + b_ref[...]
        unit, back = moments(summed)
        out_ref[...] = (unit * g_ref[...] + s_ref[...]).astype(BF16)
        cot = c_ref[...].astype(F32)
        scaled = cot * g_ref[...]
        grad = back * (
            scaled
            - jnp.mean(scaled, axis=-1, keepdims=True)
            - unit * jnp.mean(scaled * unit, axis=-1, keepdims=True)
        )
        grad_ref[...] = grad
        low_ref[...] = grad.astype(BF16)
        sums_ref[0:1, :] = jnp.sum(cot * unit, axis=0, keepdims=True)
        sums_ref[1:2, :] = jnp.sum(cot, axis=0, keepdims=True)
        sums_ref[2:3, :] = jnp.sum(grad, axis=0, keepdims=True)

    outs = [shape(dims, BF16), shape(dims, F32), shape(dims, BF16), shape((3, dims[1]), F32)]
    return whole_call(
        kernel,
        outs,
        [normed, part, got, cotangent, b_down, gain, shift],
        40 * math.prod(dims),
        "second_norm",
        limit=SMALL_LIMIT,
    )


def first_norm_back(summed, grad_second, part, got, gain, deps):
    dims = summed.shape

    def kernel(z_ref, gs_ref, p_ref, r_ref, g_ref, grad_ref, low_ref, sums_ref):
        unit, back = moments(z_ref[...])
        grad_normed = gs_ref[...] + (p_ref[...] + r_ref[...].astype(F32))
        scaled = grad_normed * g_ref[...]
        grad = back * (
            scaled
            - jnp.mean(scaled, axis=-1, keepdims=True)
            - unit * jnp.mean(scaled * unit, axis=-1, keepdims=True)
        )
        grad_ref[...] = grad
        low_ref[...] = grad.astype(BF16)
        sums_ref[0:1, :] = jnp.sum(grad_normed * unit, axis=0, keepdims=True)
        sums_ref[1:2, :] = jnp.sum(grad_normed, axis=0, keepdims=True)
        sums_ref[2:3, :] = jnp.sum(grad, axis=0, keepdims=True)

    outs = [shape(dims, F32), shape(dims, BF16), shape((3, dims[1]), F32)]
    return whole_call(
        kernel,
        outs,
        [summed, grad_second, part, got, gain],
        40 * math.prod(dims),
        "first_norm_back",
        deps=deps,
        limit=SMALL_LIMIT,
    )


def feed_forward(n_own, n_far, weights, bias, prior, deps):
    block, width = n_own.shape
    rows = 2 * block
    hidden = weights.shape[1] // 2
    tile = min(256, hidden)
    steps = hidden // tile
    last = prior is not None

    def kernel(n0, n1, u, d, b, *refs):
        step = pl.program_id(0)
        if last:
            before, a_ref, s_ref, own_ref, far_ref, tokens, acc = refs
        else:
            a_ref, s_ref, acc, tokens = refs

        @pl.when(step == 0)
        def _():
            tokens[:block] = n0[...]
            tokens[block:] = n1[...]
            acc[...] = before[...] if last else jnp.zeros_like(acc)

        hid = dot(tokens[...], u[...]) + b[...]
        half = 0.5 * (1.0 + lax.erf(hid * (1.0 / math.sqrt(2.0))))
        bell = jnp.exp(hid * hid * -0.5) * (1.0 / math.sqrt(2.0 * math.pi))
        active = (hid * half).astype(BF16)
        a_ref[...] = active
        s_ref[...] = (half + hid * bell).astype(BF16)
        acc[...] += dot_nt(active, d[...])

        if last:

            @pl.when(step == steps - 1)
            def _():
                own_ref[...] = acc[:block]
                far_ref[...] = acc[block:].astype(BF16)

    column = pl.BlockSpec((width, tile), lambda i: (0, i))
    later = pl.BlockSpec((width, tile), lambda i: (0, steps + i))
    made = pl.BlockSpec((rows, tile), lambda i: (0, i))
    args = [n_own, n_far, weights, weights, bias]
    in_specs = [const_spec((block, width))] * 2
    in_specs += [column, later, pl.BlockSpec((1, tile), lambda i: (0, i))]
    outs = [shape((rows, hidden), BF16)] * 2
    scratch = [pltpu.VMEM((rows, width), BF16)]
    if last:
        args.append(prior)
        in_specs.append(const_spec((rows, width)))
        outs += [shape((block, width), F32), shape((block, width), BF16)]
        out_specs = [made] * 2 + [const_spec((block, width))] * 2
        scratch.append(pltpu.VMEM((rows, width), F32))
    else:
        outs.append(shape((rows, width), F32))
        out_specs = [made] * 2 + [const_spec((rows, width))]
    return streamed_call(
        kernel,
        (steps,),
        outs,
        out_specs,
        args,
        in_specs,
        2 * 2 * rows * width * hidden,
        "feed_forward",
        scratch,
        deps,
    )


def feed_forward_back(g_own, g_across, w_mine, w_other, slope_mine, slope_other, deps):
    block, width = g_own.shape
    rows = 2 * block
    hidden = w_mine.shape[1] // 2
    tile = min(256, hidden)
    steps = hidden // tile

    def kernel(
        g0, g1, um, uo, dm, do, sm, so,
        gm_ref, go_ref, own_ref, across_ref, bm_ref, bo_ref, grads, acc,
    ):
        step = pl.program_id(0)

        @pl.when(step == 0)
        def _():
            grads[:block] = g0[...]
            grads[block:] = g1[...]
            acc[...] = jnp.zeros_like(acc)

        total = acc[...]
        for u, d, s, g_ref, b_ref in ((um, dm, sm, gm_ref, bm_ref), (uo, do, so, go_ref, bo_ref)):
            grad_hidden = (dot(grads[...], d[...]) * s[...].astype(F32)).astype(BF16)
            g_ref[...] = grad_hidden
            b_ref[...] = jnp.sum(grad_hidden.astype(F32), axis=0, keepdims=True)
            total = total + dot_nt(grad_hidden, u[...])
        acc[...] = total

        @pl.when(step == steps - 1)
        def _():
            own_ref[...] = acc[:block]
            across_ref[...] = acc[block:].astype(BF16)

    column = pl.BlockSpec((width, tile), lambda i: (0, i))
    later = pl.BlockSpec((width, tile), lambda i: (0, steps + i))
    bias = pl.BlockSpec((1, tile), lambda i: (0, i))
    made = pl.BlockSpec((rows, tile), lambda i: (0, i))
    outs = (
        [shape((rows, hidden), BF16)] * 2
        + [shape((block, width), F32), shape((block, width), BF16)]
        + [shape((1, hidden), F32)] * 2
    )
    return streamed_call(
        kernel,
        (steps,),
        outs,
        [made] * 2 + [const_spec((block, width))] * 2 + [bias] * 2,
        [g_own, g_across, w_mine, w_other, w_mine, w_other, slope_mine, slope_other],
        [const_spec((block, width))] * 2 + [column] * 2 + [later] * 2 + [made] * 2,
        2 * 2 * rows * width * 2 * hidden,
        "feed_forward_back",
        [pltpu.VMEM((rows, width), BF16), pltpu.VMEM((rows, width), F32)],
        deps,
    )


def weight_grad(ones, mine, other, dp_place, chains, name, other_first=0, deps=(), halves=False):
    block, width = ones[0].shape
    rows = 2 * block
    count = chains[0][0]
    tile = min(256, count)
    tiles = count // tile
    size = lax.axis_size("dp")
    share = width // size
    half = width // 2

    def kernel(place_ref, a0, a1, a2, a3, m0, m1, o0, o1, *refs):
        turned, full = refs[-2:]
        step = pl.program_id(0)

        @pl.when(step == 0)
        def _():
            for i, ref in enumerate((a0, a1, a2, a3)):
                turned[:, i * block : (i + 1) * block] = ref[...].T

        place = place_ref[0]

        def write(which, targets, order):
            for i, offset in enumerate(order):
                start = pl.multiple_of((place ^ offset) * share, share)
                at = i * share
                rows_now = full[pl.ds(start, share), :]
                if halves:
                    ref = targets[0] if at < half else targets[1]
                    at %= half
                    ref[which, at : at + share, :] = rows_now.astype(ref.dtype)
                else:
                    targets[which][at : at + share, :] = rows_now.astype(targets[which].dtype)

        for which, (one, two) in enumerate(((m0, m1), (o0, o1))):
            full[...] = dot(turned[:, :rows], one[...]) + dot(turned[:, rows:], two[...])
            for c, (_, bits) in enumerate(chains):
                targets = refs[2 * c : 2 * c + 2]
                order = halving_order(size, bits)
                if len(chains) == 1:
                    write(which, targets, order)
                else:
                    pl.when(step // tiles == c)(
                        lambda w=which, t=targets, o=order: write(w, t, o)
                    )

    base = other_first // tile
    column = pl.BlockSpec((rows, tile), lambda i: (0, i))
    other_column = pl.BlockSpec((rows, tile), lambda i: (0, base + i))
    outs, out_specs = [], []
    for c in range(len(chains)):
        for kind in (F32, BF16):
            if halves:
                outs.append(shape((2, half, count), kind))
                out_specs.append(pl.BlockSpec((2, half, tile), lambda i: (0, 0, i)))
            else:
                index = lambda i, c=c: (0, jnp.clip(i - c * tiles, 0, tiles - 1))
                outs.append(shape((width, count), kind))
                out_specs.append(pl.BlockSpec((width, tile), index))
    return streamed_call(
        kernel,
        (tiles * len(chains),),
        outs,
        out_specs,
        [dp_place, *ones, *mine, *other],
        [pl.BlockSpec(memory_space=pltpu.SMEM)]
        + [const_spec((block, width))] * 4
        + [column] * 2
        + [other_column] * 2,
        2 * 2 * rows * width * 2 * count * len(chains),
        name,
        [pltpu.VMEM((width, 2 * rows), BF16), pltpu.VMEM((width, tile), F32)],
        deps,
    )


def core_chain(made, bits, deps=()):
    pairs = [(mine, swap_tensor(other, CORE)) for mine, other in made]
    keep, send = fold_core(pairs, list(deps))
    return Chain(keep, send, bits)


def add_up(parts, deps):
    def kernel(*refs):
        refs[-1][...] = sum(ref[...] for ref in refs[:-1])

    out = shape(parts[0].shape, F32)
    return whole_call(kernel, [out], parts, 0, "add_up", deps=deps, limit=SMALL_LIMIT)[0]


def shards(
    inputs,
    lengths,
    w_query,
    w_key,
    w_value,
    w_out,
    w_up,
    w_down,
    b_query,
    b_value,
    b_out,
    b_up,
    b_down,
    first_gain,
    first_shift,
    second_gain,
    second_shift,
    cotangent,
):
    seq_count, block, width = inputs.shape
    tensor_size = lax.axis_size("tensor")
    seq_len = block * tensor_size
    place = lax.axis_index("tensor")
    head_dims = w_query.shape[1]
    head_size = width // HEADS
    hidden = w_up.shape[1]
    seqs = range(seq_count)
    row = lambda vector: vector.reshape(1, -1)

    x_own = [inputs[s] for s in seqs]
    all_across = swap_tensor(inputs, ACROSS)
    x_across = [all_across[s] for s in seqs]

    dp_place = lax.axis_index("dp").astype(jnp.int32).reshape(1)
    att_far, att_first = gather_far(pack([w_query, w_key, w_value, w_out.T], "pack_attention"))
    att_pieces = att_far + gather_near(att_far)
    share = pack([w_up, w_down.T], "pack_feed", att_first)
    share_other = swap_tensor(share, ACROSS)
    mine_far, mine_first = gather_far(share)
    mine_near = gather_near(mine_far)
    other_far, other_first = gather_far(share_other)
    other_near = gather_near(other_far[:1]) + [
        (swap_tensor(p, ACROSS), offsets) for p, offsets in mine_near[1:]
    ]

    def arrays(pieces):
        return [p for p, _ in pieces]

    att_mine = assemble(att_pieces, dp_place, "assemble_attention")
    att_other = assemble(other_core(att_pieces), dp_place, "assemble_attention_other")
    ffw_mine = assemble(mine_far + mine_near, dp_place, "assemble_feed")
    project_waits = [mine_first, [share_other]]
    attend_waits = [arrays(mine_far[1:]), arrays(mine_near[:1]) + other_first]
    norm_waits = [arrays(mine_near[1:]), arrays(other_far[1:]) + [ffw_mine]]

    biases = jnp.concatenate([b_query, jnp.zeros_like(b_query), b_value])
    qkv_bias_mine, qkv_bias_other = row(biases), row(swap_tensor(biases, CORE))
    up_bias_mine, up_bias_other = row(b_up), row(swap_tensor(b_up, ACROSS))
    b_out_row, b_down_row = row(b_out), row(b_down)
    gain_one, shift_one = row(first_gain), row(first_shift)
    gain_two, shift_two = row(second_gain), row(second_shift)

    order = jnp.stack([place, place ^ ACROSS, place ^ CORE, place ^ CORE ^ ACROSS])
    positions = (order[:, None] * block + jnp.arange(block, dtype=jnp.int32)[None, :]).reshape(-1)
    masks = [jnp.where(positions < lengths[s], 0.0, MASKED).astype(F32) for s in seqs]

    projected = []
    for s in seqs:
        waits = project_waits[s] if s < 2 else []
        projected.append(
            project_inputs(
                x_own[s], x_across[s], att_mine, att_other, qkv_bias_mine, qkv_bias_other,
                waits + [p[2] for p in projected[-1:]],
            )
        )
    far = [swap_tensor(projected[s][2], CORE) for s in seqs]
    attended = []
    for s in seqs:
        waits = attend_waits[s] if s < 2 else []
        attended.append(
            attention_forward(
                projected[s][0], projected[s][1], far[s], masks[s].reshape(1, seq_len),
                att_mine, att_other, head_size, waits + [p[2] for p in attended[-1:]],
            )
        )
    attended_got = [swap_tensor(attended[s][3], ACROSS) for s in seqs]
    one = []
    for s in seqs:
        waits = norm_waits[s] if s < 2 else []
        one.append(
            first_norm(
                x_own[s], attended[s][2], attended_got[s], b_out_row, gain_one, shift_one,
                waits + [p[2] for p in one[-1:]],
            )
        )
    normed_far = [swap_tensor(one[s][2], CORE) for s in seqs]
    fed_one = []
    for s in seqs:
        waits = [p[2] for p in fed_one[-1:]]
        fed_one.append(
            feed_forward(one[s][2], normed_far[s], ffw_mine, up_bias_mine, None, waits)
        )
    ffw_other = assemble(
        other_far + other_near, dp_place, "assemble_feed_other", [fed_one[-1][2]]
    )
    fed_two = []
    for s in seqs:
        waits = [p[2] for p in fed_two[-1:]]
        fed_two.append(
            feed_forward(
                one[s][2], normed_far[s], ffw_other, up_bias_other, fed_one[s][2], waits
            )
        )
    fed = [(fed_one[s][0], fed_two[s][0], fed_one[s][1], fed_two[s][1], *fed_two[s][2:]) for s in seqs]
    branch_got = [swap_tensor(fed[s][5], CORE) for s in seqs]
    two = [
        second_norm(
            one[s][1], fed[s][4], branch_got[s], cotangent[s], b_down_row, gain_two, shift_two
        )
        for s in seqs
    ]
    grad_far = [swap_tensor(two[s][2], CORE) for s in seqs]
    levels = range(lax.axis_size("dp").bit_length() - 1)
    near_first = list(levels)
    far_first = [1, 0, *levels[2:]] if len(near_first) > 1 else near_first

    def pairs(own, across):
        return [part for s in seqs for part in (own[s], across[s])]

    def feed_back(s, deps):
        return feed_forward_back(
            two[s][2], grad_far[s], ffw_mine, ffw_other, fed[s][2], fed[s][3], deps
        )

    fed_back = [feed_back(0, [])]
    down_made = weight_grad(
        pairs([two[s][2] for s in seqs], grad_far),
        [fed[s][0] for s in seqs], [fed[s][1] for s in seqs],
        dp_place, [(hidden, near_first)], "w_down_grad", deps=[fed_back[0][2]], halves=True,
    )
    fed_back += [feed_back(s, [down_made[1]]) for s in seqs[1:]]
    back_got = [swap_tensor(fed_back[s][3], CORE) for s in seqs]
    def placed_in(part_mine, part_other, bit):
        size = part_mine.shape[0]
        empty = jnp.zeros((tensor_size * size,), F32)
        empty = lax.dynamic_update_slice(empty, part_mine, (place * size,))
        return lax.dynamic_update_slice(empty, part_other, ((place ^ bit) * size,))

    def norm_back(s, deps):
        return first_norm_back(
            one[s][0], two[s][1], fed_back[s][2], back_got[s], gain_one, deps
        )

    one_back = [norm_back(0, [fed_back[-1][2]])]
    up_made = weight_grad(
        pairs([one[s][2] for s in seqs], normed_far),
        [fed_back[s][0] for s in seqs], [fed_back[s][1] for s in seqs],
        dp_place, [(hidden, far_first)], "w_up_grad", deps=[one_back[0][1]], halves=True,
    )
    one_back += [norm_back(s, [up_made[1]]) for s in seqs[1:]]
    first_across = [swap_tensor(one_back[s][1], ACROSS) for s in seqs]
    down_chain = Chain(*down_made, near_first)
    up_chain = Chain(*up_made, far_first)

    def backward(s, deps):
        return attention_backward(
            projected[s][0], projected[s][1], far[s], masks[s].reshape(seq_len, 1),
            one_back[s][1], first_across[s], att_mine, att_other, head_size, deps,
        )

    attended_back = [backward(0, [up_made[1]])]
    out_made = weight_grad(
        pairs([one_back[s][1] for s in seqs], first_across),
        [attended[s][0] for s in seqs], [attended[s][1] for s in seqs],
        dp_place, [(head_dims, near_first)], "w_out_grad", deps=[attended_back[0][3]],
    )
    down_chain.fold([attended_back[0][3]])
    attended_back += [backward(s, [down_chain.keep, out_made[1]]) for s in seqs[1:]]
    far_back = [swap_tensor(attended_back[s][2], CORE) for s in seqs]

    sums = add_up([attended_back[s][3] for s in seqs], [])
    small = jnp.concatenate(
        [
            sum(two[s][3] for s in seqs).reshape(-1),
            sum(one_back[s][2] for s in seqs).reshape(-1),
            placed_in(
                sum(fed_back[s][4] for s in seqs).reshape(-1),
                sum(fed_back[s][5] for s in seqs).reshape(-1),
                ACROSS,
            ),
            placed_in(sums[0, :head_dims], sums[1, :head_dims], CORE),
            placed_in(sums[0, head_dims:], sums[1, head_dims:], CORE),
        ]
    ).reshape(-1, 128)
    bits = [1 << level for level in reversed(near_first)]
    up_chain.fold([attended_back[-1][3]])
    small = plus(small, swap_tensor(small, CORE), [up_chain.keep])

    tokens = pairs(x_own, x_across)
    grad_queries = [attended_back[s][0] for s in seqs]
    query_made = weight_grad(
        tokens, grad_queries, grad_queries, dp_place, [(head_dims, near_first)], "w_query_grad",
        head_dims, [far_back[0], small],
    )
    back = [
        project_back(
            attended_back[0][0], attended_back[0][1], far_back[0], att_mine, att_other,
            [query_made[1]],
        )
    ]
    small = plus(small, swap_tensor(small, ACROSS), [back[0][2]])
    back += [
        project_back(
            attended_back[s][0], attended_back[s][1], far_back[s], att_mine, att_other, [small]
        )
        for s in seqs[1:]
    ]
    input_got = [swap_tensor(back[s][3], ACROSS) for s in seqs]
    for bit in bits[:1]:
        small = plus(small, swap_dp(small, bit), [back[-1][2]])
    down_chain.fold([back[-1][2]])
    up_chain.fold([down_chain.keep])
    both_got = swap_tensor(jnp.stack([query_made[1], out_made[1]]), CORE)
    query_chain = Chain(
        *fold_core([(query_made[0], both_got[0]), (out_made[0], both_got[1])], [back[-1][2]]),
        near_first,
    )
    key_value_made = weight_grad(
        tokens, [back[s][0] for s in seqs], [back[s][1] for s in seqs],
        dp_place, [(head_dims, near_first), (head_dims, near_first)], "w_key_value_grad",
        deps=input_got[:1] + [up_chain.keep, query_chain.keep, small],
    )
    waits = input_got[-1:] + [down_chain.came]
    key_chain = core_chain([key_value_made[:2]], near_first, waits)
    value_chain = core_chain([key_value_made[2:]], near_first, waits)
    started = [key_chain.keep, value_chain.keep]
    down_chain.fold(started)
    query_chain.fold(started)
    key_chain.fold()
    value_chain.fold()
    ending = [key_chain.keep, value_chain.keep]
    query_chain.fold(ending)
    up_chain.fold(ending)
    for bit in bits[1:]:
        small = plus(small, swap_dp(small, bit), ending)
    small = small.reshape(-1)

    input_grad = jnp.stack(
        [
            (one_back[s][0] + (back[s][2] + input_got[s].astype(F32))).astype(BF16)
            for s in seqs
        ]
    )

    def over_y(both):
        return both[0] + swap_tensor(both[1].astype(BF16), ACROSS).astype(F32)

    down_grad, up_grad = over_y(down_chain.finish()), over_y(up_chain.finish())
    query_and_out = query_chain.finish()

    vectors = [small[i * width : (i + 1) * width] for i in range(6)]
    second_gain_grad, second_shift_grad, b_down_grad = vectors[:3]
    first_gain_grad, first_shift_grad, b_out_grad = vectors[3:]
    b_up_grad = small[6 * width : 6 * width + tensor_size * hidden]
    b_query_grad, b_value_grad = small[-2 * width : -width], small[-width:]

    output = jnp.stack([two[s][0] for s in seqs])
    return (
        output,
        input_grad,
        query_and_out[0],
        key_chain.finish()[0],
        value_chain.finish()[0],
        query_and_out[1].T,
        up_grad,
        down_grad.T,
        b_query_grad,
        b_value_grad,
        b_out_grad,
        b_up_grad,
        b_down_grad,
        first_gain_grad,
        first_shift_grad,
        second_gain_grad,
        second_shift_grad,
    )


def solution(mesh):
    placed = (
        P("dp", "tensor", None),
        P("dp"),
        P("dp", "tensor"),
        P("dp", "tensor"),
        P("dp", "tensor"),
        P("tensor", "dp"),
        P("dp", "tensor"),
        P("tensor", "dp"),
        P("tensor"),
        P("tensor"),
        P(),
        P("tensor"),
        P(),
        P(),
        P(),
        P(),
        P(),
        P("dp", "tensor", None),
    )
    return jax.shard_map(
        shards,
        mesh=mesh,
        in_specs=placed,
        out_specs=(
            P("dp", "tensor", None),
            P("dp", "tensor", None),
            P("dp", "tensor"),
            P("dp", "tensor"),
            P("dp", "tensor"),
            P("tensor", "dp"),
            P("dp", "tensor"),
            P("tensor", "dp"),
            P(),
            P(),
            P(),
            P(),
            P(),
            P(),
            P(),
            P(),
            P(),
        ),
        check_vma=False,
    )
```
